256 devices in a mesh: gx: 16 (over y, x), gy: 16 (over z, core).
Axes of the slice: x: 4, y: 4, z: 8, core: 2. Of those that a mesh axis runs over, the one named last changes fastest.
Arguments:
- field_in: bfloat16 [256, 128, 20, 128], P('gx', 'gy'), may hold values from -6 to 6
- point_weight: bfloat16 [20, 20], replicated, may hold values from -1.25 to 1.25
- point_bias: float32 [20], replicated, may hold values from -3 to 3
- spec_weight: bfloat16 [24, 20, 20, 2, 2304], P(None, None, None, None, ('gx', 'gy')), may hold values from -1 to 1
- out_cotangent: bfloat16 [256, 128, 20, 128], P('gx', 'gy'), may hold values from -6 to 6
Outputs:
- output_field: bfloat16 [256, 128, 20, 128], P('gx', 'gy')
- grad_in: bfloat16 [256, 128, 20, 128], P('gx', 'gy')
- grad_spec: float32 [24, 20, 20, 2, 2304], P(None, None, None, None, ('gx', 'gy'))
- grad_point: float32 [20, 20], replicated
- grad_bias: float32 [20], replicated
The draws below stay inside these ranges and needn't reach their ends.
All inputs are finite; a program needn't handle non-finite values.
Results may differ from the reference program's by a relative error of at most 0.029.
Values may be sent and summed in bfloat16 or wider, within the bound.
No kernel may reach another device: no remote copies, remote signals or barrier semaphores. Data moves between devices by JAX's collectives and lax.ppermute only.
A program may use at most 64 MiB of HBM per device.

```python
import math
import jax
import jax.numpy as jnp
from jax import lax

C = 20
CX = 16
Z = 32
T_SIZE = 4
KX = 24
KY = 24
KZ = 24
KT = 4
NX = 256
NY = 128
ZT = 128
M = 96
MG = 6
MODES = 2304
N_GX = 16


def level_of(rng, extent, split, smallest, largest):
    loudness = 1.0
    for axis_at, parts in split:
        heights = jax.random.uniform(jax.random.fold_in(jax.random.fold_in(rng, 6), axis_at), (parts,), jnp.float32, smallest / len(split), largest / len(split))
        loudness = loudness * jnp.repeat(jnp.exp(heights), extent[axis_at] // parts).reshape((-1,) + (1,) * (len(extent) - 1 - axis_at))
    return loudness


def bell_draw(own_key, extent, width, most, split=(), kind=jnp.bfloat16):
    array = jax.random.normal(own_key, extent, jnp.float32) * width
    if len(split) > 0:
        array = level_of(own_key, extent, split, -0.22, 0.18) * array
    return jnp.clip(array, min=-most, max=most).astype(kind)


def setup_inputs(seed: int = 0) -> dict:
    arg_keys = jax.random.split(jax.random.key(seed), 6)
    return {
        "field_in": bell_draw(arg_keys[0], (NX, NY, C, ZT), 1.0, 6.0, ((0, 16), (1, 16))),
        "point_weight": bell_draw(arg_keys[1], (C, C), C ** -0.5, 1.25),
        "point_bias": bell_draw(arg_keys[2], (C,), 0.5, 3.0, (), jnp.float32),
        "spec_weight": bell_draw(arg_keys[3], (KY, C, C, 2, MODES), (2 * C) ** -0.5, 1.0, ((4, 256),)),
        "out_cotangent": bell_draw(arg_keys[4], (NX, NY, C, ZT), 1.0, 6.0, ((0, 16), (1, 16))),
    }


def centered(count):
    return (jnp.arange(count, dtype=jnp.int32) + count // 2) % count - count // 2


def line_table(modes, length, positions, scale, synthesis):
    turns = (centered(modes)[:, None] * positions[None, :]) % length
    angle = turns.astype(jnp.float32) * (2.0 * math.pi / length)
    cosine = jnp.cos(angle) * scale
    sine = jnp.sin(angle) * scale
    sign = 1.0
    if synthesis:
        cosine, sine, sign = cosine.T, sine.T, -1.0
    first = jnp.stack([cosine, sign * sine])
    second = jnp.stack([-sign * sine, cosine])
    return jnp.stack([first, second]).astype(jnp.bfloat16)


def depth_table(scale):
    cells = jnp.arange(ZT, dtype=jnp.int32)
    turn_z = (centered(KZ)[:, None] * (cells // T_SIZE)[None, :]) % Z
    turn_t = (centered(KT)[:, None] * (cells % T_SIZE)[None, :]) % T_SIZE
    angle = turn_z.astype(jnp.float32)[:, None, :] * (2.0 * math.pi / Z) + turn_t.astype(jnp.float32)[None, :, :] * (2.0 * math.pi / T_SIZE)
    angle = angle.reshape(M, ZT)
    return (jnp.stack([jnp.cos(angle), -jnp.sin(angle)]) * scale).astype(jnp.bfloat16)


def gelu_value(value):
    return 0.5 * value * (1.0 + lax.erf(value * 0.7071067811865476))


def gelu_slope(value):
    return 0.5 * (1.0 + lax.erf(value * 0.7071067811865476)) + value * jnp.exp(-0.5 * value * value) * 0.3989422804014327


def mix(form, left, right):
    return jnp.einsum(form, left.astype(jnp.float32), right.astype(jnp.float32), precision=lax.Precision.HIGHEST)


def reference(field_in, point_weight, point_bias, spec_weight, out_cotangent):
    blocks = NX // CX
    positions_x = jnp.arange(NX, dtype=jnp.int32)
    positions_y = jnp.arange(NY, dtype=jnp.int32)
    depth_in = depth_table(ZT ** -0.5)
    depth_mid = depth_table(M ** -0.5)
    x_fwd = line_table(KX, NX, positions_x, NX ** -0.5, False)
    x_fwd_back = line_table(KX, NX, positions_x, KX ** -0.5, False)
    x_syn = line_table(KX, NX, positions_x, KX ** -0.5, True)
    x_syn_back = line_table(KX, NX, positions_x, NX ** -0.5, True)
    y_fwd = line_table(KY, NY, positions_y, NY ** -0.5, False)
    y_fwd_back = line_table(KY, NY, positions_y, KY ** -0.5, False)
    y_syn = line_table(KY, NY, positions_y, KY ** -0.5, True)
    y_syn_back = line_table(KY, NY, positions_y, NY ** -0.5, True)

    def split_fwd(table):
        return jnp.moveaxis(table.reshape(2, 2, KX, blocks, CX), 3, 0)

    def split_syn(table):
        return jnp.moveaxis(table.reshape(2, 2, blocks, CX, KX), 2, 0)

    field_blocks = field_in.reshape(blocks, CX, NY, C, ZT)
    cot_blocks = out_cotangent.reshape(blocks, CX, NY, C, ZT)

    def analyse(total, inputs):
        block, table = inputs
        spectrum = mix('abcz,smz->abcsm', block, depth_in).astype(jnp.bfloat16)
        return total + mix('abcsm,tska->kbctm', spectrum, table), None

    zero = jnp.zeros((KX, NY, C, 2, M), jnp.float32)
    x_total, _ = lax.scan(analyse, zero, (field_blocks, split_fwd(x_fwd)))
    coef = mix('kbctm,utjb->kjcum', x_total.astype(jnp.bfloat16), y_fwd).astype(jnp.bfloat16)
    weights = spec_weight.reshape(KY, C, C, 2, N_GX, KX, MG).transpose(0, 1, 2, 3, 5, 4, 6).reshape(KY, C, C, 2, KX, M)
    coef_re, coef_im = coef[:, :, :, 0], coef[:, :, :, 1]
    weight_re, weight_im = weights[:, :, :, 0], weights[:, :, :, 1]
    prod_re = mix('kjim,jiokm->kjom', coef_re, weight_re) - mix('kjim,jiokm->kjom', coef_im, weight_im)
    prod_im = mix('kjim,jiokm->kjom', coef_im, weight_re) + mix('kjim,jiokm->kjom', coef_re, weight_im)
    product = jnp.stack([prod_re, prod_im], axis=3).astype(jnp.bfloat16)
    y_lines = mix('kjcsm,tsnj->knctm', product, y_syn).astype(jnp.bfloat16)

    def forward_block(carry, inputs):
        total, point_sum, bias_sum = carry
        block, cotangent, table_syn, table_back = inputs
        x_lines = mix('kncsm,tsak->anctm', y_lines, table_syn).astype(jnp.bfloat16)
        spectral = mix('abcsm,smz->abcz', x_lines, depth_mid)
        pre_act = spectral + mix('abcz,cd->abdz', block, point_weight) + point_bias[None, None, :, None]
        output_block = gelu_value(pre_act).astype(jnp.bfloat16)
        slope_grad = (cotangent.astype(jnp.float32) * gelu_slope(pre_act)).astype(jnp.bfloat16)
        spectrum = mix('abcz,smz->abcsm', slope_grad, depth_mid).astype(jnp.bfloat16)
        total = total + mix('abcsm,tska->kbctm', spectrum, table_back)
        point_sum = point_sum + mix('abcz,abdz->cd', block, slope_grad)
        bias_sum = bias_sum + jnp.sum(slope_grad.astype(jnp.float32), axis=(0, 1, 3))
        return (total, point_sum, bias_sum), (output_block, slope_grad)

    start = (zero, jnp.zeros((C, C), jnp.float32), jnp.zeros((C,), jnp.float32))
    (dual_total, point_sum, bias_sum), (out_blocks, grad_blocks) = lax.scan(
        forward_block, start, (field_blocks, cot_blocks, split_syn(x_syn), split_fwd(x_fwd_back)))
    dual = mix('kbctm,utjb->kjcum', dual_total.astype(jnp.bfloat16), y_fwd_back).astype(jnp.bfloat16)
    dual_re, dual_im = dual[:, :, :, 0], dual[:, :, :, 1]
    grad_re = mix('kjim,kjom->jiokm', coef_re, dual_re) + mix('kjim,kjom->jiokm', coef_im, dual_im)
    grad_im = mix('kjim,kjom->jiokm', coef_re, dual_im) - mix('kjim,kjom->jiokm', coef_im, dual_re)
    grad_natural = jnp.stack([grad_re, grad_im], axis=3)
    grad_spec = grad_natural.reshape(KY, C, C, 2, KX, N_GX, MG).transpose(0, 1, 2, 3, 5, 4, 6).reshape(KY, C, C, 2, MODES)
    back_re = mix('jiokm,kjom->kjim', weight_re, dual_re) + mix('jiokm,kjom->kjim', weight_im, dual_im)
    back_im = mix('jiokm,kjom->kjim', weight_re, dual_im) - mix('jiokm,kjom->kjim', weight_im, dual_re)
    back_modes = jnp.stack([back_re, back_im], axis=3).astype(jnp.bfloat16)
    back_y = mix('kjcsm,tsnj->knctm', back_modes, y_syn_back).astype(jnp.bfloat16)

    def backward_block(inputs):
        slope_grad, table = inputs
        back_x = mix('kncsm,tsak->anctm', back_y, table).astype(jnp.bfloat16)
        spectral = mix('abcsm,smz->abcz', back_x, depth_in)
        return (spectral + mix('abdz,cd->abcz', slope_grad, point_weight)).astype(jnp.bfloat16)

    in_blocks = lax.map(backward_block, (grad_blocks, split_syn(x_syn_back)))
    norm = (NX * NY * ZT) ** -0.5
    return (out_blocks.reshape(NX, NY, C, ZT), in_blocks.reshape(NX, NY, C, ZT), grad_spec,
            point_sum * norm, bias_sum * norm)
```

```python
import math

import jax
import jax.numpy as jnp
import ml_dtypes
import numpy as np
from jax import lax
from jax.experimental import pallas as pl
from jax.experimental.pallas import tpu as pltpu
from jax.sharding import PartitionSpec as P

C = 20
Z = 32
T_SIZE = 4
KX = 24
KY = 24
KZ = 24
KT = 4
NX = 256
NY = 128
ZT = 128
M = 96
N = 16
CX = NX // N
CY = NY // N
ROWS = 12 * C
GROUPS = C // 4
PAIRS = 9
LINE = PAIRS * KY

BF = jnp.bfloat16
F32 = jnp.float32


def centered(count):
    return (np.arange(count) + count // 2) % count - count // 2


def rounded(table):
    return np.asarray(table, np.float32).astype(ml_dtypes.bfloat16)


def line_table(modes, length, scale):
    turns = centered(modes)[:, None] * np.arange(length)[None, :] % length
    angle = turns.astype(np.float32) * np.float32(2.0 * math.pi / length)
    scale = np.float32(scale)
    return rounded(np.cos(angle) * scale), rounded(np.sin(angle) * scale)


def depth_table(scale):
    cells = np.arange(ZT)
    turn_z = centered(KZ)[:, None] * (cells // T_SIZE)[None, :] % Z
    turn_t = centered(KT)[:, None] * (cells % T_SIZE)[None, :] % T_SIZE
    angle = turn_z.astype(np.float32)[:, None, :] * np.float32(2.0 * math.pi / Z)
    angle = angle + turn_t.astype(np.float32)[None, :, :] * np.float32(2.0 * math.pi / T_SIZE)
    angle = angle.reshape(M, ZT)
    return rounded(np.stack([np.cos(angle), -np.sin(angle)]) * np.float32(scale))


def depth_matrix(scale):
    table = depth_table(scale).astype(np.float32).reshape(2, N, 2, 3, ZT)
    eye = np.eye(4, dtype=np.float32)
    full = np.einsum("sghmn,ce->ghcsmen", table, eye)
    return rounded(full.reshape(N * 2 * 4 * 2 * 3, 4 * ZT))


def x_matrix(scale):
    cosine, sine = line_table(KX, NX, scale)
    eye = np.eye(CY, dtype=np.float32)
    return rounded(
        np.concatenate([np.kron(t.astype(np.float32), eye) for t in (cosine, sine)], axis=0)
    )


def y_matrix(scale):
    return np.concatenate(line_table(KY, NY, scale), axis=0)


def lane_maps():
    plain = np.zeros((ROWS, 256), np.float32)
    turned = np.zeros((ROWS, 256), np.float32)
    for row in range(ROWS):
        group, rest = divmod(row, 48)
        half, rest = divmod(rest, 24)
        channel, rest = divmod(rest, 6)
        part, mode = divmod(rest, 3)
        base = half * 128 + (group * 4 + channel) * 6 + mode
        plain[row, base + 3 * part] = 1.0
        turned[row, base + 3 * (1 - part)] = 1.0 if part == 1 else -1.0
    return rounded(plain), rounded(turned)


def lane_picks():
    lanes = np.arange(128)
    inside = lanes < 6 * C
    channel = np.stack([(lanes // 6 == c) & inside for c in range(24)])
    kind = np.stack([(lanes % 6 == k) & inside for k in range(6)] + [inside * 0] * 2)
    return rounded(channel), kind.astype(np.float32)


def channel_spread():
    return rounded(np.kron(np.eye(C, dtype=np.float32), np.ones((1, CY), np.float32)))


DEPTH_IN = depth_matrix(ZT**-0.5)
DEPTH_MID = depth_matrix(M**-0.5)
X_IN = x_matrix(NX**-0.5)
X_MID = x_matrix(KX**-0.5)
Y_IN = y_matrix(NY**-0.5)
Y_MID = y_matrix(KY**-0.5)
PLAIN, TURNED = lane_maps()
CHANNEL, KIND = lane_picks()
SPREAD = channel_spread()


def dot(left, right, left_dim=1, right_dim=0, precision=None):
    return lax.dot_general(
        left,
        right,
        (((left_dim,), (right_dim,)), ((), ())),
        precision=precision,
        preferred_element_type=F32,
    )


def call(kernel, out_shape, flops=10**8, megabytes=4, name=None):
    return pl.pallas_call(
        kernel,
        out_shape=out_shape,
        compiler_params=pltpu.CompilerParams(vmem_limit_bytes=24 * 2**20),
        cost_estimate=pl.CostEstimate(
            flops=flops, bytes_accessed=megabytes * 10**6, transcendentals=0
        ),
        name=name,
    )


def shaped(shape, dtype):
    return jax.ShapeDtypeStruct(shape, dtype)


def to_columns(values):
    wide = values.astype(F32).reshape(CX, 4, CY, ZT)
    return jnp.concatenate([wide[:, k].reshape(CX * CY, ZT) for k in range(4)], axis=1)


def to_cells(columns):
    parts = [columns[:, k * ZT : (k + 1) * ZT].reshape(CX, CY, ZT) for k in range(4)]
    return jnp.stack(parts, axis=1).reshape(CX, 4 * CY, ZT)


def spectrum_kernel(field, depth, out):
    for group in range(GROUPS):
        columns = to_columns(field[:, group * 32 : group * 32 + 32, :]).astype(BF)
        spectrum = dot(depth[...], columns, 1, 1)
        out[:, group * 48 : group * 48 + 48, :] = spectrum.astype(BF).reshape(N, 48, 128)


def split_dot(left, right):
    high = left.astype(BF)
    low = (left - high.astype(F32)).astype(BF)
    return dot(high, right) + dot(low, right)


def x_analysis_kernel(lines, table, plain, turned, out):
    rows = jnp.concatenate([lines[a] for a in range(N)], axis=1)
    both = dot(table[...], rows, 1, 1)
    half = KX * CY
    coef = split_dot(both[:half], plain[...]) + split_dot(both[half:], turned[...])
    units = [coef[:, k * 128 : k * 128 + 128].reshape(KX, CY, 128) for k in range(2)]
    out[...] = jnp.stack(units, axis=1).reshape(N, 24, 128).astype(BF)


def x_synthesis(modes, table, plain, turned):
    units = modes.reshape(KX, 2, CY, 128)
    flat = jnp.concatenate([units[:, k].reshape(KX * CY, 128) for k in range(2)], axis=1)
    flat = flat.astype(BF)
    half = KX * CY
    first = dot(plain, flat, 1, 1).astype(BF)
    second = dot(turned, flat, 1, 1).astype(BF)
    return dot(first, table[:half]) + dot(second, table[half:])


def x_synthesis_kernel(modes, table, plain, turned, out):
    lines = x_synthesis(modes[...].astype(F32), table[...], plain[...], turned[...])
    lines = lines.astype(BF)
    for a in range(N):
        out[a] = lines[:, a * 128 : a * 128 + 128]


def x_synthesis_sums_kernel(modes, table, plain, turned, out):
    wide = modes[...].astype(F32)
    lines = x_synthesis(wide[:, :24], table[...], plain[...], turned[...]).astype(BF)
    sums = jnp.sum(wide[:, 24:], axis=0)
    block = pack_sums(sums[:4] + sums[4:])
    tail = jnp.concatenate([block, jnp.zeros_like(block)], axis=0).astype(BF)
    for a in range(N):
        out[a, :ROWS] = lines[:, a * 128 : a * 128 + 128]
        out[a, ROWS:] = tail


def pack_sums(values):
    high = values.astype(BF).astype(F32)
    return jnp.concatenate([high, values - high], axis=0)


def turn_lanes(values, sign):
    part = lax.broadcasted_iota(jnp.int32, values.shape, 1) % 6
    ahead = pltpu.roll(values, 125, 1)
    behind = pltpu.roll(values, 3, 1)
    return jnp.where(part < 3, sign * ahead, -sign * behind)


def y_analysis(lines, table, channel, kind):
    wide = lines.astype(F32).reshape(N, 3, CY, 128)
    wide = jnp.concatenate([wide[:, u].reshape(NY, 128) for u in range(3)], axis=1)
    both = dot(table, wide.astype(BF))
    coefs = []
    for u in range(3):
        piece = both[:, u * 128 : u * 128 + 128]
        coef = piece[:KY] + turn_lanes(piece[KY:], 1.0)
        coefs.append(coef.astype(BF).astype(F32))
    result = []
    for part in range(2):
        rows = [
            coefs[u] * kind[part * 3 + mode : part * 3 + mode + 1]
            for u in range(3)
            for mode in range(3)
        ]
        rows = jnp.concatenate(rows, axis=0).astype(BF)
        result.append(dot(channel, rows, 1, 1))
    return result


def y_synthesis(parts, table, channel, kind):
    picked = [dot(part.astype(BF), channel[:C], 0, 0) for part in parts]
    columns = []
    for u in range(3):
        total = jnp.zeros((KY, 128), F32)
        for part in range(2):
            for mode in range(3):
                start = (u * 3 + mode) * KY
                mask = kind[part * 3 + mode : part * 3 + mode + 1]
                total = total + picked[part][start : start + KY] * mask
        columns.append(jnp.concatenate([total, turn_lanes(total, -1.0)], axis=0))
    columns = jnp.concatenate(columns, axis=1).astype(BF)
    lines = dot(table, columns, 0, 0)
    units = [lines[:, u * 128 : u * 128 + 128].reshape(N, CY, 128) for u in range(3)]
    return jnp.stack(units, axis=1).reshape(N, 24, 128)


def product_kernel(lines, weights, analysis, synthesis, channel, kind, out, coef):
    kinds = kind[...]
    real, imag = y_analysis(lines[...], analysis[...], channel[...], kinds)
    coef[0] = real
    coef[1] = imag
    product_re = jnp.zeros((C, LINE), F32)
    product_im = jnp.zeros((C, LINE), F32)
    for i in range(C):
        weight_re, weight_im = weights[0, i], weights[1, i]
        re, im = real[i : i + 1], imag[i : i + 1]
        product_re = product_re + (weight_re * re - weight_im * im)
        product_im = product_im + (weight_re * im + weight_im * re)
    out[...] = y_synthesis([product_re, product_im], synthesis[...], channel[...], kinds).astype(BF)


def back_kernel(lines, weights, sums, analysis, synthesis, channel, kind, out, dual):
    kinds = kind[...]
    real, imag = y_analysis(lines[...], analysis[...], channel[...], kinds)
    dual[0] = real
    dual[1] = imag
    re, im = real[:C], imag[:C]
    back_re, back_im = [], []
    for i in range(C):
        weight_re, weight_im = weights[0, i], weights[1, i]
        back_re.append(jnp.sum(weight_re * re + weight_im * im, axis=0, keepdims=True))
        back_im.append(jnp.sum(weight_re * im - weight_im * re, axis=0, keepdims=True))
    parts = [jnp.concatenate(back_re, axis=0), jnp.concatenate(back_im, axis=0)]
    modes = y_synthesis(parts, synthesis[...], channel[...], kinds)
    tail = jnp.broadcast_to(sums[...].reshape(1, 8, 128), (N, 8, 128))
    out[...] = jnp.concatenate([modes, tail], axis=1).astype(BF)


def weight_grad_kernel(coef, dual, out):
    dual_re, dual_im = dual[0, :C], dual[1, :C]
    for i in range(C):
        re, im = coef[0, i : i + 1], coef[1, i : i + 1]
        out[0, i] = re * dual_re + im * dual_im
        out[1, i] = re * dual_im - im * dual_re


def same_cell(size):
    row = lax.broadcasted_iota(jnp.int32, (size, size), 0) % CY
    column = lax.broadcasted_iota(jnp.int32, (size, size), 1) % CY
    return jnp.where(row == column, 1.0, 0.0)


def spread_map(weight, spread, weight_dim):
    tall = dot(spread, weight, 0, weight_dim).astype(BF)
    return (dot(tall, spread) * same_cell(C * CY)).astype(BF)


def pointwise_kernel(field, weight, bias, spread, out):
    mixing = spread_map(weight[...], spread[...], 1)
    for x in range(CX):
        out[x] = dot(mixing, field[x]) + bias[...]


def point_back_kernel(field, slope, weight, spread, out, sums):
    mixing = spread_map(weight[...], spread[...], 0)
    for x in range(CX):
        out[x] = dot(mixing, slope[x])
    fields = jnp.concatenate([field[x] for x in range(CX)], axis=1)
    slopes = jnp.concatenate([slope[x] for x in range(CX)], axis=1)
    cross = dot(fields, slopes, 1, 1) * same_cell(C * CY)
    ones = jnp.ones((8, CX * ZT), BF)
    bias = dot(ones, slopes, 1, 1)
    picks = spread[...].astype(F32)
    exact = lax.Precision.HIGHEST
    point = dot(dot(picks, cross, 1, 0, exact), picks, 1, 1, exact)
    total = dot(bias, picks, 1, 1, exact)[:1]
    rows = jnp.concatenate([point, total], axis=0)
    rows = jnp.concatenate([rows, jnp.zeros((C + 1, 128 - C), F32)], axis=1)
    packed = []
    for r in range(4):
        line = jnp.zeros((1, 128), F32)
        for q in range(6):
            if r * 6 + q <= C:
                row = rows[r * 6 + q : r * 6 + q + 1]
                line = line + (pltpu.roll(row, q * C, 1) if q > 0 else row)
        packed.append(line)
    sums[...] = pack_sums(jnp.concatenate(packed, axis=0))


def cells_kernel(lines, depth, pointwise, cotangent, field_out, slope_out, out):
    for group in range(GROUPS):
        rows = lines[:, group * 48 : group * 48 + 48, :].reshape(N * 48, 128)
        span = slice(group * 32, group * 32 + 32)
        pre = dot(rows, depth[...], 0, 0) + to_columns(pointwise[:, span, :])
        phi = 0.5 * (1.0 + lax.erf(pre * 0.7071067811865476))
        field_out[:, span, :] = to_cells(pre * phi).astype(BF)
        slope = phi + pre * jnp.exp(-0.5 * pre * pre) * 0.3989422804014327
        slope = slope * to_columns(cotangent[:, span, :])
        slope_out[:, span, :] = to_cells(slope).astype(BF)
        spectrum = dot(depth[...], slope.astype(BF), 1, 1)
        out[:, group * 48 : group * 48 + 48, :] = spectrum.astype(BF).reshape(N, 48, 128)


def last_kernel(lines, depth, pointwise, field_out, point_out, bias_out):
    for group in range(GROUPS):
        rows = lines[:, group * 48 : group * 48 + 48, :].reshape(N * 48, 128)
        span = slice(group * 32, group * 32 + 32)
        total = to_cells(dot(rows, depth[...], 0, 0)) + pointwise[:, span, :]
        field_out[:, span, :] = total.astype(BF)
    tails = jnp.sum(lines[:, ROWS:, :].astype(F32), axis=0)
    sums = (tails[:4] + tails[4:8]) * (NX * NY * ZT) ** -0.5
    for r in range(4):
        for q in range(6):
            index = r * 6 + q
            if index <= C:
                row = sums[r : r + 1]
                row = pltpu.roll(row, 128 - q * C, 1) if q > 0 else row
                if index < C:
                    point_out[index : index + 1, :] = row[:, :C]
                else:
                    bias_out[...] = row[:, :C]


def exchange(values, axis):
    return lax.all_to_all(values, axis, split_axis=0, concat_axis=0, tiled=True)


def body(field_in, point_weight, point_bias, spec_weight, out_cotangent):
    cells = (CX, C * CY, ZT)
    line_message = shaped((N, ROWS, 128), BF)
    mode_message = shaped((N, 24, 128), BF)
    field = field_in.transpose(0, 2, 1, 3).reshape(cells)
    cotangent = out_cotangent.transpose(0, 2, 1, 3).reshape(cells)
    weights = spec_weight.transpose(3, 1, 2, 4, 0).reshape(2, C, C, LINE).astype(F32)
    bias = jnp.broadcast_to(point_bias[:, None, None], (C, CY, 1)).reshape(C * CY, 1)

    message = call(spectrum_kernel, line_message, name="spectrum")(field, DEPTH_IN)
    message = exchange(message, "gx")
    pointwise = call(pointwise_kernel, shaped(cells, F32), name="pointwise")(
        field, point_weight, bias, SPREAD
    )
    message = call(x_analysis_kernel, mode_message, name="x_analysis")(message, X_IN, PLAIN, TURNED)
    message = exchange(message, "gy")
    message, coef = call(
        product_kernel, (mode_message, shaped((2, 24, LINE), F32)), name="product"
    )(message, weights, Y_IN, Y_MID, CHANNEL, KIND)
    message = exchange(message, "gy")
    message = call(x_synthesis_kernel, line_message, name="x_synthesis")(
        message, X_MID, PLAIN, TURNED
    )
    message = exchange(message, "gx")
    output_field, slope, message = call(
        cells_kernel, (shaped(cells, BF), shaped(cells, BF), line_message), name="cells"
    )(message, DEPTH_MID, pointwise, cotangent)
    message = exchange(message, "gx")
    point_back, sums = call(
        point_back_kernel, (shaped(cells, F32), shaped((8, 128), F32)), name="point_back"
    )(field, slope, point_weight, SPREAD)
    message = call(x_analysis_kernel, mode_message, name="x_analysis_back")(
        message, X_MID, PLAIN, TURNED
    )
    message = exchange(message, "gy")
    message, dual = call(
        back_kernel,
        (shaped((N, 32, 128), BF), shaped((2, 24, LINE), F32)),
        name="back",
    )(message, weights, sums, Y_MID, Y_IN, CHANNEL, KIND)
    message = exchange(message, "gy")
    weight_grad = call(weight_grad_kernel, shaped((2, C, C, LINE), F32), name="weight_grad")(
        coef, dual
    )
    message = call(x_synthesis_sums_kernel, shaped((N, 256, 128), BF), name="x_synthesis_back")(
        message, X_IN, PLAIN, TURNED
    )
    message = exchange(message, "gx")
    grad_in, grad_point, grad_bias = call(
        last_kernel,
        (shaped(cells, BF), shaped((C, C), F32), shaped((1, C), F32)),
        name="last",
    )(message, DEPTH_IN, point_back)
    grad_spec = weight_grad.reshape(2, C, C, PAIRS, KY).transpose(4, 1, 2, 0, 3)

    def natural(values):
        return values.reshape(CX, C, CY, ZT).transpose(0, 2, 1, 3)

    return natural(output_field), natural(grad_in), grad_spec, grad_point, grad_bias.reshape(C)


def solution(mesh):
    return jax.shard_map(
        body,
        mesh=mesh,
        in_specs=(
            P("gx", "gy", None, None),
            P(),
            P(),
            P(None, None, None, None, ("gx", "gy")),
            P("gx", "gy", None, None),
        ),
        out_specs=(
            P("gx", "gy", None, None),
            P("gx", "gy", None, None),
            P(None, None, None, None, ("gx", "gy")),
            P(),
            P(),
        ),
        check_vma=False,
    )
```

```python
import math

import jax
import jax.numpy as jnp
import ml_dtypes
import numpy as np
from jax import lax
from jax.experimental import pallas as pl
from jax.experimental.pallas import tpu as pltpu
from jax.sharding import PartitionSpec as P

C = 20
Z = 32
T_SIZE = 4
KX = 24
KY = 24
KZ = 24
KT = 4
NX = 256
NY = 128
ZT = 128
M = 96
N = 16
CX = NX // N
CY = NY // N
ROWS = 12 * C
GROUPS = C // 4
PAIRS = 9
WEIGHTS = C * C * PAIRS * 2

BF = jnp.bfloat16
F32 = jnp.float32


def centered(count):
    return (np.arange(count) + count // 2) % count - count // 2


def rounded(table):
    return np.asarray(table, np.float32).astype(ml_dtypes.bfloat16)


def line_table(modes, length, scale):
    turns = centered(modes)[:, None] * np.arange(length)[None, :] % length
    angle = turns.astype(np.float32) * np.float32(2.0 * math.pi / length)
    scale = np.float32(scale)
    return rounded(np.cos(angle) * scale), rounded(np.sin(angle) * scale)


def depth_table(scale):
    cells = np.arange(ZT)
    turn_z = centered(KZ)[:, None] * (cells // T_SIZE)[None, :] % Z
    turn_t = centered(KT)[:, None] * (cells % T_SIZE)[None, :] % T_SIZE
    angle = turn_z.astype(np.float32)[:, None, :] * np.float32(2.0 * math.pi / Z)
    angle = angle + turn_t.astype(np.float32)[None, :, :] * np.float32(2.0 * math.pi / T_SIZE)
    angle = angle.reshape(M, ZT)
    return rounded(np.stack([np.cos(angle), -np.sin(angle)]) * np.float32(scale))


def depth_rows(scale):
    table = depth_table(scale).reshape(2, N, 2, 3, ZT).transpose(1, 2, 0, 3, 4)
    table = np.broadcast_to(table[:, :, None], (N, 2, 4, 2, 3, ZT))
    return np.ascontiguousarray(table).reshape(2 * N, 24, ZT)


def x_rows(scale):
    table = np.concatenate(line_table(KX, NX, scale), axis=0)
    return np.ascontiguousarray(np.repeat(table, CY, axis=1))


def y_rows(scale):
    return np.concatenate(line_table(KY, NY, scale), axis=0)


def lane_picks():
    rows, lanes = np.arange(6 * 24)[:, None], np.arange(128)[None, :]
    return rounded((lanes == rows % 24 * 6 + rows // 24) & (rows % 24 < C))


DEPTH_IN = depth_rows(ZT**-0.5)
DEPTH_MID = depth_rows(M**-0.5)
X_IN = x_rows(NX**-0.5)
X_MID = x_rows(KX**-0.5)
Y_ALL = np.concatenate([y_rows(NY**-0.5), y_rows(KY**-0.5), lane_picks()], axis=0)
Y_IN = slice(0, 48)
Y_MID = slice(48, 96)
PICKS = slice(96, 96 + 144)


def dot(left, right, left_dim=1, right_dim=0, precision=None):
    return lax.dot_general(
        left,
        right,
        (((left_dim,), (right_dim,)), ((), ())),
        precision=precision,
        preferred_element_type=F32,
    )


def call(kernel, out_shape, spaces=None, out_spaces=None, scratch=(), name=None, limit=24 * 2**20):
    def spec(space):
        return pl.BlockSpec(memory_space=space)

    options = {}
    if spaces is not None:
        options["in_specs"] = [spec(space) for space in spaces]
    if out_spaces is not None:
        specs = [spec(space) for space in out_spaces]
        options["out_specs"] = specs if isinstance(out_shape, (tuple, list)) else specs[0]
    return pl.pallas_call(
        kernel,
        out_shape=out_shape,
        scratch_shapes=scratch,
        compiler_params=pltpu.CompilerParams(vmem_limit_bytes=limit),
        cost_estimate=pl.CostEstimate(flops=10**8, bytes_accessed=4 * 10**6, transcendentals=0),
        name=name,
        **options,
    )


VMEM = pltpu.VMEM
HBM = pltpu.HBM
DMA = pltpu.SemaphoreType.DMA


def shaped(shape, dtype):
    return jax.ShapeDtypeStruct(shape, dtype)


def start_copies(pairs, semaphores, base=0):
    copies = [
        pltpu.make_async_copy(source, target, semaphores.at[base + k])
        for k, (source, target) in enumerate(pairs)
    ]
    for copy in copies:
        copy.start()
    return copies


def rows_of(group, count):
    return slice(group * count, group * count + count)


def iota(shape, dim):
    return lax.broadcasted_iota(jnp.int32, shape, dim)


def ones_where(condition):
    return jnp.where(condition, 1.0, 0.0)


def depth_matrix(rows):
    wide = rows.astype(F32)
    channel = iota((1, 24, 1), 1) // 6
    parts = [(wide * ones_where(channel == k)).reshape(N * 48, ZT) for k in range(4)]
    return jnp.concatenate(parts, axis=1).astype(BF)


def x_matrix(rows):
    size = rows.shape[1]
    same = ones_where(iota((1, CY, size), 1) == iota((1, CY, size), 2) % CY)
    wide = rows.astype(F32).reshape(KX, 1, size) * same
    return wide.reshape(KX * CY, size).astype(BF)


def lane_maps():
    row, lane = iota((ROWS, 1), 0), iota((1, 256), 1)
    inner = row % 24
    start = (row // 24) % 2 * 128 + row // 48 * 24
    real = inner % 6 < 3
    plain = ones_where(lane == start + inner)
    other = jnp.where(real, inner + 3, inner - 3)
    turned = ones_where(lane == start + other) * jnp.where(real, -1.0, 1.0)
    return plain.astype(BF), turned.astype(BF)


def spread_matrix():
    return ones_where(iota((C, C * CY), 0) == iota((C, C * CY), 1) // CY)


def to_columns(values):
    wide = values.astype(F32).reshape(CX, 4, CY, ZT)
    return jnp.concatenate([wide[:, k].reshape(CX * CY, ZT) for k in range(4)], axis=1)


def to_cells(columns):
    parts = [columns[:, k * ZT : (k + 1) * ZT].reshape(CX, CY, ZT) for k in range(4)]
    return jnp.stack(parts, axis=1).reshape(CX, 4 * CY, ZT)


def wide_to_columns(wide):
    def channel(k):
        rows = wide[k * CY : k * CY + CY]
        return jnp.concatenate([rows[:, x * ZT : x * ZT + ZT] for x in range(CX)], axis=0)

    return jnp.concatenate([channel(k) for k in range(4)], axis=1)


def wide_to_cells(wide):
    return jnp.stack([wide[:, x * ZT : x * ZT + ZT] for x in range(CX)], axis=0)


def spectrum_kernel(field, depth, out):
    matrix = depth_matrix(depth[...])
    for group in range(GROUPS):
        columns = to_columns(field[:, rows_of(group, 32), :]).astype(BF)
        spectrum = dot(matrix, columns, 1, 1)
        out[:, rows_of(group, 48), :] = spectrum.astype(BF).reshape(N, 48, 128)


def split_dot(left, right):
    high = left.astype(BF)
    low = (left - high.astype(F32)).astype(BF)
    return dot(high, right) + dot(low, right)


def x_analysis_kernel(lines, table, out):
    plain, turned = lane_maps()
    rows = jnp.concatenate([lines[a] for a in range(N)], axis=1)
    coef = split_dot(dot(x_matrix(table[:KX]), rows, 1, 1), plain)
    coef = coef + split_dot(dot(x_matrix(table[KX:]), rows, 1, 1), turned)
    units = [coef[:, k * 128 : k * 128 + 128].reshape(KX, CY, 128) for k in range(2)]
    out[...] = jnp.stack(units, axis=1).reshape(N, 24, 128).astype(BF)


def x_modes(modes):
    plain, turned = lane_maps()
    units = modes.reshape(KX, 2, CY, 128)
    flat = jnp.concatenate([units[:, k].reshape(KX * CY, 128) for k in range(2)], axis=1)
    flat = flat.astype(BF)
    return dot(plain, flat, 1, 1).astype(BF), dot(turned, flat, 1, 1).astype(BF)


def x_lines(first, second, table):
    lines = dot(first, x_matrix(table[:KX])) + dot(second, x_matrix(table[KX:]))
    return lines.astype(BF)


def x_synthesis_kernel(modes, table, out):
    first, second = x_modes(modes[...].astype(F32))
    lines = x_lines(first, second, table[...])
    for a in range(N):
        out[a] = lines[:, a * 128 : a * 128 + 128]


def x_synthesis_sums_kernel(modes, table, out):
    wide = modes[...].astype(F32)
    first, second = x_modes(wide[:, :24])
    lines = x_lines(first, second, table[...])
    sums = jnp.sum(wide[:, 24:], axis=0)
    block = pack_sums(sums[:4] + sums[4:])
    tail = jnp.concatenate([block, jnp.zeros_like(block)], axis=0).astype(BF)
    for a in range(N):
        out[a, :ROWS] = lines[:, a * 128 : a * 128 + 128]
        out[a, ROWS:] = tail


def pack_sums(values):
    high = values.astype(BF).astype(F32)
    return jnp.concatenate([high, values - high], axis=0)


def turn_lanes(values, sign):
    part = iota(values.shape, 1) % 6
    ahead = pltpu.roll(values, 125, 1)
    behind = pltpu.roll(values, 3, 1)
    return jnp.where(part < 3, sign * ahead, -sign * behind)


def y_analysis(lines, table, picks):
    wide = lines.astype(F32).reshape(N, 3, CY, 128)
    wide = jnp.concatenate([wide[:, u].reshape(NY, 128) for u in range(3)], axis=1)
    both = dot(table, wide.astype(BF))
    result = []
    for u in range(3):
        piece = both[:, u * 128 : u * 128 + 128]
        coef = piece[:KY] + turn_lanes(piece[KY:], 1.0)
        result.append(dot(picks, coef.astype(BF), 1, 1))
    return result


def y_synthesis(units, table, picks):
    columns = []
    for unit in units:
        modes = dot(unit.astype(BF), picks, 0, 0)
        columns.append(jnp.concatenate([modes, turn_lanes(modes, -1.0)], axis=0))
    columns = jnp.concatenate(columns, axis=1).astype(BF)
    lines = dot(table, columns, 0, 0)
    lines = [lines[:, u * 128 : u * 128 + 128].reshape(N, CY, 128) for u in range(3)]
    return jnp.stack(lines, axis=1).reshape(N, 24, 128)


def line_of(modes, unit, kind, channel):
    return modes[unit, pl.ds(kind * 24 + channel, 1), :]


def load_weights(weights, wide):
    step = WEIGHTS // 10
    for k in range(10):
        wide[k * step : k * step + step, :] = weights[k * step : k * step + step, :].astype(F32)


def mix_channels(weights, modes, out_step, in_step, sign):
    units = []
    for unit in range(3):
        reals, imags = [], []
        for mode in range(3):
            pair = unit * 3 + mode
            real = jnp.zeros((C, KY), F32)
            imag = jnp.zeros((C, KY), F32)
            for k in range(C):
                start = k * in_step + 2 * pair
                weight_re = weights[pl.ds(start, C, stride=out_step), :]
                weight_im = weights[pl.ds(start + 1, C, stride=out_step), :]
                re = line_of(modes, unit, mode, k)
                im = line_of(modes, unit, 3 + mode, k)
                real = real + (weight_re * re - sign * (weight_im * im))
                imag = imag + (weight_re * im + sign * (weight_im * re))
            reals.append(real)
            imags.append(imag)
        empty = jnp.zeros((4, KY), F32)
        parts = [jnp.concatenate([part, empty], axis=0) for part in reals + imags]
        units.append(jnp.concatenate(parts, axis=0))
    return units


def product_kernel(lines, weights, tables, out, coef, wide):
    load_weights(weights, wide)
    for u, unit in enumerate(y_analysis(lines[...], tables[Y_IN], tables[PICKS])):
        coef[u] = unit
    product = mix_channels(wide, coef, 2 * PAIRS, 2 * PAIRS * C, 1.0)
    out[...] = y_synthesis(product, tables[Y_MID], tables[PICKS]).astype(BF)


def back_kernel(lines, weights, sums, tables, out, dual, wide):
    load_weights(weights, wide)
    for u, unit in enumerate(y_analysis(lines[...], tables[Y_MID], tables[PICKS])):
        dual[u] = unit
    modes = mix_channels(wide, dual, 2 * PAIRS * C, 2 * PAIRS, -1.0)
    modes = y_synthesis(modes, tables[Y_IN], tables[PICKS])
    tail = jnp.broadcast_to(sums[...].reshape(1, 8, 128), (N, 8, 128))
    out[...] = jnp.concatenate([modes, tail], axis=1).astype(BF)


def weight_gradient(coef, dual, channel, out):
    for pair in range(PAIRS):
        unit, mode = divmod(pair, 3)
        dual_re = dual[unit, mode * 24 : mode * 24 + C, :]
        dual_im = dual[unit, (3 + mode) * 24 : (3 + mode) * 24 + C, :]
        re = line_of(coef, unit, mode, channel)
        im = line_of(coef, unit, 3 + mode, channel)
        start = channel * 2 * PAIRS * C + 2 * pair
        out[pl.ds(start, C, stride=2 * PAIRS), :] = re * dual_re + im * dual_im
        out[pl.ds(start + 1, C, stride=2 * PAIRS), :] = re * dual_im - im * dual_re


def same_cell(size):
    return ones_where(iota((size, 1), 0) % CY == iota((1, size), 1) % CY)


def spread_map(weight, weight_dim):
    spread = spread_matrix().astype(BF)
    tall = dot(spread, weight, 0, weight_dim).astype(BF)
    return (dot(tall, spread) * same_cell(C * CY)).astype(BF)


def flat_cells(values):
    return jnp.concatenate([values[x] for x in range(CX)], axis=1)


def pack_lines(cross, bias):
    picks = spread_matrix()
    exact = lax.Precision.HIGHEST
    point = dot(dot(picks, cross * same_cell(C * CY), 1, 0, exact), picks, 1, 1, exact)
    total = dot(bias, picks, 1, 1, exact)[:1]
    rows = jnp.concatenate([point, total], axis=0)
    rows = jnp.concatenate([rows, jnp.zeros((C + 1, 128 - C), F32)], axis=1)
    packed = []
    for r in range(4):
        line = jnp.zeros((1, 128), F32)
        for q in range(6):
            if r * 6 + q <= C:
                row = rows[r * 6 + q : r * 6 + q + 1]
                line = line + (pltpu.roll(row, q * C, 1) if q > 0 else row)
        packed.append(line)
    return jnp.concatenate(packed, axis=0)


def cells_kernel(
    lines,
    depth,
    field,
    cotangent,
    weight,
    bias,
    out,
    sums,
    slope_out,
    field_to,
    field_out,
    semaphores,
):
    matrix = depth_matrix(depth[...])
    mixing = spread_map(weight[...], 1)
    shift = dot(spread_matrix(), bias[...], 0, 1, lax.Precision.HIGHEST)
    fields = flat_cells(field)
    ones = jnp.ones((8, CX * ZT), BF)
    stores, cross, total = [], [], []
    for group in range(GROUPS):
        rows = lines[:, group * 48 : group * 48 + 48, :].reshape(N * 48, 128)
        span = rows_of(group, 32)
        pointwise = dot(mixing[span], fields) + shift[span]
        pre = dot(rows, matrix, 0, 0) + wide_to_columns(pointwise)
        phi = 0.5 * (1.0 + lax.erf(pre * 0.7071067811865476))
        field_out[group] = to_cells(pre * phi).astype(BF)
        slope = phi + pre * jnp.exp(-0.5 * pre * pre) * 0.3989422804014327
        slope = slope * to_columns(cotangent[:, span, :])
        pair = (field_out.at[group], field_to.at[:, span, :])
        stores += start_copies([pair], semaphores, group)
        slopes = to_cells(slope).astype(BF)
        slope_out[:, span, :] = slopes
        spectrum = dot(matrix, slope.astype(BF), 1, 1)
        out[:, group * 48 : group * 48 + 48, :] = spectrum.astype(BF).reshape(N, 48, 128)
        slopes = flat_cells(slopes)
        cross.append(dot(fields, slopes, 1, 1))
        total.append(dot(ones, slopes, 1, 1))
    cross = jnp.concatenate(cross, axis=1)
    total = jnp.concatenate(total, axis=1)
    sums[...] = pack_sums(pack_lines(cross, total))
    for store in stores:
        store.wait()


def last_kernel(
    lines,
    depth,
    slope,
    weight,
    coef,
    dual,
    point_out,
    bias_out,
    field_to,
    weight_to,
    field_out,
    weight_out,
    semaphores,
):
    stores = []
    step = WEIGHTS // GROUPS
    for group in range(GROUPS):
        for k in range(4):
            weight_gradient(coef, dual, group * 4 + k, weight_out)
        pair = (weight_out.at[rows_of(group, step)], weight_to.at[rows_of(group, step)])
        stores += start_copies([pair], semaphores, group)
    tails = jnp.sum(lines[:, ROWS:, :].astype(F32), axis=0)
    sums = (tails[:4] + tails[4:8]) * (NX * NY * ZT) ** -0.5
    for r in range(4):
        for q in range(6):
            index = r * 6 + q
            if index <= C:
                row = sums[r : r + 1]
                row = pltpu.roll(row, 128 - q * C, 1) if q > 0 else row
                if index < C:
                    point_out[index : index + 1, :] = row[:, :C]
                else:
                    bias_out[...] = row[:, :C]
    mixing = spread_map(weight[...], 0)
    slopes = flat_cells(slope)
    matrix = depth_matrix(depth[...])
    for group in range(GROUPS):
        rows = lines[:, group * 48 : group * 48 + 48, :].reshape(N * 48, 128)
        span = rows_of(group, 32)
        pointwise = wide_to_cells(dot(mixing[span], slopes))
        field_out[group] = (to_cells(dot(rows, matrix, 0, 0)) + pointwise).astype(BF)
        pair = (field_out.at[group], field_to.at[:, span, :])
        stores += start_copies([pair], semaphores, GROUPS + group)
    for store in stores:
        store.wait()


def exchange(values, axis):
    return lax.all_to_all(values, axis, split_axis=0, concat_axis=0, tiled=True)


def body(field_in, point_weight, point_bias, spec_weight, out_cotangent):
    cells = (CX, C * CY, ZT)
    line_message = shaped((N, ROWS, 128), BF)
    mode_message = shaped((N, 24, 128), BF)
    mode_lines = shaped((3, 144, KY), F32)
    group_cells = VMEM((GROUPS, CX, 4 * CY, ZT), BF)
    wide_weights = VMEM((WEIGHTS, KY), F32)
    field = field_in.transpose(0, 2, 1, 3).reshape(cells)
    cotangent = out_cotangent.transpose(0, 2, 1, 3).reshape(cells)
    weights = spec_weight.transpose(1, 2, 4, 3, 0).reshape(WEIGHTS, KY)

    message = call(spectrum_kernel, line_message, name="spectrum")(field, DEPTH_IN)
    message = exchange(message, "gx")
    message = call(x_analysis_kernel, mode_message, name="x_analysis")(message, X_IN)
    message = exchange(message, "gy")
    message, coef = call(
        product_kernel, (mode_message, mode_lines), scratch=[wide_weights], name="product"
    )(message, weights, Y_ALL)
    message = exchange(message, "gy")
    message = call(x_synthesis_kernel, line_message, name="x_synthesis")(message, X_MID)
    message = exchange(message, "gx")
    message, sums, slope, output_field = call(
        cells_kernel,
        (line_message, shaped((8, 128), F32), shaped(cells, BF), shaped(cells, BF)),
        [VMEM] * 6,
        [VMEM, VMEM, VMEM, HBM],
        [group_cells, DMA((GROUPS,))],
        "cells",
    )(message, DEPTH_MID, field, cotangent, point_weight, point_bias.reshape(1, C))
    message = exchange(message, "gx")
    message = call(x_analysis_kernel, mode_message, name="x_analysis_back")(message, X_MID)
    message = exchange(message, "gy")
    message, dual = call(
        back_kernel,
        (shaped((N, 32, 128), BF), mode_lines),
        scratch=[wide_weights],
        name="back",
    )(message, weights, sums, Y_ALL)
    message = exchange(message, "gy")
    message = call(
        x_synthesis_sums_kernel, shaped((N, 256, 128), BF), name="x_synthesis_back"
    )(message, X_IN)
    message = exchange(message, "gx")
    grad_point, grad_bias, grad_in, weight_grad = call(
        last_kernel,
        (
            shaped((C, C), F32),
            shaped((1, C), F32),
            shaped(cells, BF),
            shaped((WEIGHTS, KY), F32),
        ),
        [VMEM] * 6,
        [VMEM, VMEM, HBM, HBM],
        [group_cells, wide_weights, DMA((2 * GROUPS,))],
        "last",
    )(message, DEPTH_IN, slope, point_weight, coef, dual)
    grad_spec = weight_grad.reshape(C, C, PAIRS, 2, KY).transpose(4, 0, 1, 3, 2)

    def natural(values):
        return values.reshape(CX, C, CY, ZT).transpose(0, 2, 1, 3)

    return natural(output_field), natural(grad_in), grad_spec, grad_point, grad_bias.reshape(C)


def solution(mesh):
    return jax.shard_map(
        body,
        mesh=mesh,
        in_specs=(
            P("gx", "gy", None, None),
            P(),
            P(),
            P(None, None, None, None, ("gx", "gy")),
            P("gx", "gy", None, None),
        ),
        out_specs=(
            P("gx", "gy", None, None),
            P("gx", "gy", None, None),
            P(None, None, None, None, ("gx", "gy")),
            P(),
            P(),
        ),
        check_vma=False,
    )
```

```python
import math

import jax
import jax.numpy as jnp
import ml_dtypes
import numpy as np
from jax import lax
from jax.experimental import pallas as pl
from jax.experimental.pallas import tpu as pltpu
from jax.sharding import PartitionSpec as P

C = 20
Z = 32
T_SIZE = 4
KX = 24
KY = 24
KZ = 24
KT = 4
NX = 256
NY = 128
ZT = 128
M = 96
N = 16
CX = NX // N
CY = NY // N
ROWS = 12 * C
GROUPS = C // 4
PAIRS = 9
WEIGHTS = C * C * PAIRS * 2

BF = jnp.bfloat16
F32 = jnp.float32


def centered(count):
    return (np.arange(count) + count // 2) % count - count // 2


def rounded(table):
    return np.asarray(table, np.float32).astype(ml_dtypes.bfloat16)


def line_table(modes, length, scale):
    turns = centered(modes)[:, None] * np.arange(length)[None, :] % length
    angle = turns.astype(np.float32) * np.float32(2.0 * math.pi / length)
    scale = np.float32(scale)
    return rounded(np.cos(angle) * scale), rounded(np.sin(angle) * scale)


def depth_table(scale):
    cells = np.arange(ZT)
    turn_z = centered(KZ)[:, None] * (cells // T_SIZE)[None, :] % Z
    turn_t = centered(KT)[:, None] * (cells % T_SIZE)[None, :] % T_SIZE
    angle = turn_z.astype(np.float32)[:, None, :] * np.float32(2.0 * math.pi / Z)
    angle = angle + turn_t.astype(np.float32)[None, :, :] * np.float32(2.0 * math.pi / T_SIZE)
    angle = angle.reshape(M, ZT)
    return rounded(np.stack([np.cos(angle), -np.sin(angle)]) * np.float32(scale))


def depth_rows(scale):
    table = depth_table(scale).reshape(2, N, 2, 3, ZT).transpose(1, 2, 0, 3, 4)
    table = np.broadcast_to(table[:, :, None], (N, 2, 4, 2, 3, ZT))
    return np.ascontiguousarray(table).reshape(2 * N, 24, ZT)


def x_rows(scale):
    table = np.concatenate(line_table(KX, NX, scale), axis=0)
    return np.ascontiguousarray(np.repeat(table, CY, axis=1))


def y_rows(scale):
    return np.concatenate(line_table(KY, NY, scale), axis=0)


def lane_picks():
    rows, lanes = np.arange(6 * 24)[:, None], np.arange(128)[None, :]
    return rounded((lanes == rows % 24 * 6 + rows // 24) & (rows % 24 < C))


DEPTH_IN = depth_rows(ZT**-0.5)
DEPTH_MID = depth_rows(M**-0.5)
X_IN = x_rows(NX**-0.5)
X_MID = x_rows(KX**-0.5)
Y_ALL = np.concatenate([y_rows(NY**-0.5), y_rows(KY**-0.5), lane_picks()], axis=0)
Y_IN = slice(0, 48)
Y_MID = slice(48, 96)
PICKS = slice(96, 96 + 144)


def dot(left, right, left_dim=1, right_dim=0, precision=None):
    return lax.dot_general(
        left,
        right,
        (((left_dim,), (right_dim,)), ((), ())),
        precision=precision,
        preferred_element_type=F32,
    )


def call(kernel, out_shape, scratch=(), name=None):
    return pl.pallas_call(
        kernel,
        out_shape=out_shape,
        scratch_shapes=scratch,
        compiler_params=pltpu.CompilerParams(vmem_limit_bytes=24 * 2**20),
        cost_estimate=pl.CostEstimate(flops=10**8, bytes_accessed=4 * 10**6, transcendentals=0),
        name=name,
    )


def shaped(shape, dtype):
    return jax.ShapeDtypeStruct(shape, dtype)


def rows_of(group, count):
    return slice(group * count, group * count + count)


def iota(shape, dim):
    return lax.broadcasted_iota(jnp.int32, shape, dim)


def ones_where(condition):
    return jnp.where(condition, 1.0, 0.0)


def depth_matrix(rows):
    wide = rows.astype(F32)
    channel = iota((1, 24, 1), 1) // 6
    parts = [(wide * ones_where(channel == k)).reshape(N * 48, ZT) for k in range(4)]
    return jnp.concatenate(parts, axis=1).astype(BF)


def x_matrix(rows):
    size = rows.shape[1]
    same = ones_where(iota((1, CY, size), 1) == iota((1, CY, size), 2) % CY)
    wide = rows.astype(F32).reshape(KX, 1, size) * same
    return wide.reshape(KX * CY, size).astype(BF)


def lane_maps():
    row, lane = iota((ROWS, 1), 0), iota((1, 256), 1)
    inner = row % 24
    start = (row // 24) % 2 * 128 + row // 48 * 24
    real = inner % 6 < 3
    plain = ones_where(lane == start + inner)
    other = jnp.where(real, inner + 3, inner - 3)
    turned = ones_where(lane == start + other) * jnp.where(real, -1.0, 1.0)
    return plain.astype(BF), turned.astype(BF)


def spread_matrix():
    return ones_where(iota((C, C * CY), 0) == iota((C, C * CY), 1) // CY)


def to_columns(values):
    wide = values.astype(F32).reshape(CX, 4, CY, ZT)
    return jnp.concatenate([wide[:, k].reshape(CX * CY, ZT) for k in range(4)], axis=1)


def to_cells(columns):
    parts = [columns[:, k * ZT : (k + 1) * ZT].reshape(CX, CY, ZT) for k in range(4)]
    return jnp.stack(parts, axis=1).reshape(CX, 4 * CY, ZT)


def wide_to_columns(wide):
    def channel(k):
        rows = wide[k * CY : k * CY + CY]
        return jnp.concatenate([rows[:, x * ZT : x * ZT + ZT] for x in range(CX)], axis=0)

    return jnp.concatenate([channel(k) for k in range(4)], axis=1)


def wide_to_cells(wide):
    return jnp.stack([wide[:, x * ZT : x * ZT + ZT] for x in range(CX)], axis=0)


def put_spectra(matrix, columns, first, out):
    spectra = dot(matrix, jnp.concatenate(columns, axis=0), 1, 1).astype(BF)
    for k in range(len(columns)):
        spectrum = spectra[:, k * 128 : k * 128 + 128].reshape(N, 48, 128)
        out[:, rows_of(first + k, 48), :] = spectrum


BATCHES = ((0, 1), (2, 3), (4,))


def spectrum_kernel(field, depth, out):
    matrix = depth_matrix(depth[...])
    for batch in BATCHES:
        columns = [to_columns(field[:, rows_of(g, 32), :]).astype(BF) for g in batch]
        put_spectra(matrix, columns, batch[0], out)


def from_spectra(lines, matrix):
    rows = [lines[:, rows_of(g, 48), :].reshape(N * 48, 128) for g in range(GROUPS)]
    return dot(jnp.concatenate(rows, axis=1), matrix, 0, 0)


def split_dot(left, right):
    high = left.astype(BF)
    low = (left - high.astype(F32)).astype(BF)
    return dot(high, right) + dot(low, right)


def x_analysis_kernel(lines, table, out):
    plain, turned = lane_maps()
    rows = jnp.concatenate([lines[a] for a in range(N)], axis=1)
    matrix = jnp.concatenate([x_matrix(table[:KX]), x_matrix(table[KX:])], axis=0)
    both = dot(matrix, rows, 1, 1)
    half = KX * CY
    coef = split_dot(both[:half], plain) + split_dot(both[half:], turned)
    units = [coef[:, k * 128 : k * 128 + 128].reshape(KX, CY, 128) for k in range(2)]
    out[...] = jnp.stack(units, axis=1).reshape(N, 24, 128).astype(BF)


def x_modes(modes):
    plain, turned = lane_maps()
    units = modes.reshape(KX, 2, CY, 128)
    flat = jnp.concatenate([units[:, k].reshape(KX * CY, 128) for k in range(2)], axis=1)
    flat = flat.astype(BF)
    return dot(plain, flat, 1, 1).astype(BF), dot(turned, flat, 1, 1).astype(BF)


def x_lines(first, second, table):
    lines = dot(first, x_matrix(table[:KX])) + dot(second, x_matrix(table[KX:]))
    return lines.astype(BF)


def x_synthesis_kernel(modes, table, out):
    first, second = x_modes(modes[...].astype(F32))
    lines = x_lines(first, second, table[...])
    for a in range(N):
        out[a] = lines[:, a * 128 : a * 128 + 128]


def x_synthesis_sums_kernel(modes, table, out):
    wide = modes[...].astype(F32)
    first, second = x_modes(wide[:, :24])
    lines = x_lines(first, second, table[...])
    sums = jnp.sum(wide[:, 24:], axis=0)
    block = pack_sums(sums[:4] + sums[4:])
    tail = jnp.concatenate([block, jnp.zeros_like(block)], axis=0).astype(BF)
    for a in range(N):
        out[a, :ROWS] = lines[:, a * 128 : a * 128 + 128]
        out[a, ROWS:] = tail


def pack_sums(values):
    high = values.astype(BF).astype(F32)
    return jnp.concatenate([high, values - high], axis=0)


def turn_lanes(values, sign):
    part = iota(values.shape, 1) % 6
    ahead = pltpu.roll(values, 125, 1)
    behind = pltpu.roll(values, 3, 1)
    return jnp.where(part < 3, sign * ahead, -sign * behind)


def y_analysis(lines, table, picks):
    wide = lines.astype(F32).reshape(N, 3, CY, 128)
    wide = jnp.concatenate([wide[:, u].reshape(NY, 128) for u in range(3)], axis=1)
    both = dot(table, wide.astype(BF))
    result = []
    for u in range(3):
        piece = both[:, u * 128 : u * 128 + 128]
        coef = piece[:KY] + turn_lanes(piece[KY:], 1.0)
        result.append(dot(picks, coef.astype(BF), 1, 1))
    return result


def y_synthesis(units, table, picks):
    columns = []
    for unit in units:
        modes = dot(unit.astype(BF), picks, 0, 0)
        columns.append(jnp.concatenate([modes, turn_lanes(modes, -1.0)], axis=0))
    columns = jnp.concatenate(columns, axis=1).astype(BF)
    lines = dot(table, columns, 0, 0)
    lines = [lines[:, u * 128 : u * 128 + 128].reshape(N, CY, 128) for u in range(3)]
    return jnp.stack(lines, axis=1).reshape(N, 24, 128)


def line_of(modes, unit, kind, channel):
    return modes[unit, pl.ds(kind * 24 + channel, 1), :]


def load_weights(weights, wide):
    step = WEIGHTS // 10
    for k in range(10):
        wide[k * step : k * step + step, :] = weights[k * step : k * step + step, :].astype(F32)


def mix_channels(weights, modes, out_step, in_step, sign):
    units = []
    for unit in range(3):
        reals, imags = [], []
        for mode in range(3):
            pair = unit * 3 + mode
            real = jnp.zeros((C, KY), F32)
            imag = jnp.zeros((C, KY), F32)
            for k in range(C):
                start = k * in_step + 2 * pair
                weight_re = weights[pl.ds(start, C, stride=out_step), :]
                weight_im = weights[pl.ds(start + 1, C, stride=out_step), :]
                re = line_of(modes, unit, mode, k)
                im = line_of(modes, unit, 3 + mode, k)
                real = real + (weight_re * re - sign * (weight_im * im))
                imag = imag + (weight_re * im + sign * (weight_im * re))
            reals.append(real)
            imags.append(imag)
        empty = jnp.zeros((4, KY), F32)
        parts = [jnp.concatenate([part, empty], axis=0) for part in reals + imags]
        units.append(jnp.concatenate(parts, axis=0))
    return units


def product_kernel(lines, weights, tables, out, coef, wide):
    load_weights(weights, wide)
    for u, unit in enumerate(y_analysis(lines[...], tables[Y_IN], tables[PICKS])):
        coef[u] = unit
    product = mix_channels(wide, coef, 2 * PAIRS, 2 * PAIRS * C, 1.0)
    out[...] = y_synthesis(product, tables[Y_MID], tables[PICKS]).astype(BF)


def back_kernel(lines, weights, sums, tables, out, dual, wide):
    load_weights(weights, wide)
    for u, unit in enumerate(y_analysis(lines[...], tables[Y_MID], tables[PICKS])):
        dual[u] = unit
    modes = mix_channels(wide, dual, 2 * PAIRS * C, 2 * PAIRS, -1.0)
    modes = y_synthesis(modes, tables[Y_IN], tables[PICKS])
    tail = jnp.broadcast_to(sums[...].reshape(1, 8, 128), (N, 8, 128))
    out[...] = jnp.concatenate([modes, tail], axis=1).astype(BF)


def weight_gradient(coef, dual, channel, out):
    for pair in range(PAIRS):
        unit, mode = divmod(pair, 3)
        dual_re = dual[unit, mode * 24 : mode * 24 + C, :]
        dual_im = dual[unit, (3 + mode) * 24 : (3 + mode) * 24 + C, :]
        re = line_of(coef, unit, mode, channel)
        im = line_of(coef, unit, 3 + mode, channel)
        start = channel * 2 * PAIRS * C + 2 * pair
        out[pl.ds(start, C, stride=2 * PAIRS), :] = re * dual_re + im * dual_im
        out[pl.ds(start + 1, C, stride=2 * PAIRS), :] = re * dual_im - im * dual_re


def same_cell(size):
    return ones_where(iota((size, 1), 0) % CY == iota((1, size), 1) % CY)


def spread_map(weight, weight_dim):
    spread = spread_matrix().astype(BF)
    tall = dot(spread, weight, 0, weight_dim).astype(BF)
    return (dot(tall, spread) * same_cell(C * CY)).astype(BF)


def flat_cells(values):
    return jnp.concatenate([values[x] for x in range(CX)], axis=1)


def pack_lines(cross, bias):
    picks = spread_matrix()
    exact = lax.Precision.HIGHEST
    point = dot(dot(picks, cross * same_cell(C * CY), 1, 0, exact), picks, 1, 1, exact)
    total = dot(bias, picks, 1, 1, exact)[:1]
    rows = jnp.concatenate([point, total], axis=0)
    rows = jnp.concatenate([rows, jnp.zeros((C + 1, 128 - C), F32)], axis=1)
    packed = []
    for r in range(4):
        line = jnp.zeros((1, 128), F32)
        for q in range(6):
            if r * 6 + q <= C:
                row = rows[r * 6 + q : r * 6 + q + 1]
                line = line + (pltpu.roll(row, q * C, 1) if q > 0 else row)
        packed.append(line)
    return jnp.concatenate(packed, axis=0)


def cells_kernel(
    lines, depth, field, cotangent, weight, bias, out, sums, slope_out, field_out
):
    matrix = depth_matrix(depth[...])
    mixing = spread_map(weight[...], 1)
    shift = dot(spread_matrix(), bias[...], 0, 1, lax.Precision.HIGHEST)
    fields = flat_cells(field)
    spectral = from_spectra(lines, matrix)
    pointwise = dot(mixing, fields) + shift
    slopes = []
    for batch in BATCHES:
        columns = []
        for group in batch:
            span = rows_of(group, 32)
            pre = spectral[rows_of(group, 128)] + wide_to_columns(pointwise[span])
            phi = 0.5 * (1.0 + lax.erf(pre * 0.7071067811865476))
            field_out[:, span, :] = to_cells(pre * phi).astype(BF)
            slope = phi + pre * jnp.exp(-0.5 * pre * pre) * 0.3989422804014327
            slope = slope * to_columns(cotangent[:, span, :])
            columns.append(slope.astype(BF))
            slope = to_cells(slope).astype(BF)
            slope_out[:, span, :] = slope
            slopes.append(flat_cells(slope))
        put_spectra(matrix, columns, batch[0], out)
    slopes = jnp.concatenate(slopes, axis=0)
    cross = dot(fields, slopes, 1, 1)
    total = dot(jnp.ones((8, CX * ZT), BF), slopes, 1, 1)
    sums[...] = pack_sums(pack_lines(cross, total))


def last_kernel(
    lines, depth, slope, weight, coef, dual, point_out, bias_out, field_out, weight_out
):
    for channel in range(C):
        weight_gradient(coef, dual, channel, weight_out)
    tails = jnp.sum(lines[:, ROWS:, :].astype(F32), axis=0)
    sums = (tails[:4] + tails[4:8]) * (NX * NY * ZT) ** -0.5
    for r in range(4):
        for q in range(6):
            index = r * 6 + q
            if index <= C:
                row = sums[r : r + 1]
                row = pltpu.roll(row, 128 - q * C, 1) if q > 0 else row
                if index < C:
                    point_out[index : index + 1, :] = row[:, :C]
                else:
                    bias_out[...] = row[:, :C]
    pointwise = dot(spread_map(weight[...], 0), flat_cells(slope))
    spectral = from_spectra(lines, depth_matrix(depth[...]))
    for group in range(GROUPS):
        span = rows_of(group, 32)
        total = to_cells(spectral[rows_of(group, 128)]) + wide_to_cells(pointwise[span])
        field_out[:, span, :] = total.astype(BF)


def exchange(values, axis):
    return lax.all_to_all(values, axis, split_axis=0, concat_axis=0, tiled=True)


def body(field_in, point_weight, point_bias, spec_weight, out_cotangent):
    cells = (CX, C * CY, ZT)
    line_message = shaped((N, ROWS, 128), BF)
    mode_message = shaped((N, 24, 128), BF)
    mode_lines = shaped((3, 144, KY), F32)
    wide_weights = pltpu.VMEM((WEIGHTS, KY), F32)
    field = field_in.transpose(0, 2, 1, 3).reshape(cells)
    cotangent = out_cotangent.transpose(0, 2, 1, 3).reshape(cells)
    weights = spec_weight.transpose(1, 2, 4, 3, 0).reshape(WEIGHTS, KY)

    message = call(spectrum_kernel, line_message, name="spectrum")(field, DEPTH_IN)
    message = exchange(message, "gx")
    message = call(x_analysis_kernel, mode_message, name="x_analysis")(message, X_IN)
    message = exchange(message, "gy")
    message, coef = call(
        product_kernel, (mode_message, mode_lines), scratch=[wide_weights], name="product"
    )(message, weights, Y_ALL)
    message = exchange(message, "gy")
    message = call(x_synthesis_kernel, line_message, name="x_synthesis")(message, X_MID)
    message = exchange(message, "gx")
    message, sums, slope, output_field = call(
        cells_kernel,
        (line_message, shaped((8, 128), F32), shaped(cells, BF), shaped(cells, BF)),
        name="cells",
    )(message, DEPTH_MID, field, cotangent, point_weight, point_bias.reshape(1, C))
    message = exchange(message, "gx")
    message = call(x_analysis_kernel, mode_message, name="x_analysis_back")(message, X_MID)
    message = exchange(message, "gy")
    message, dual = call(
        back_kernel,
        (shaped((N, 32, 128), BF), mode_lines),
        scratch=[wide_weights],
        name="back",
    )(message, weights, sums, Y_ALL)
    message = exchange(message, "gy")
    message = call(
        x_synthesis_sums_kernel, shaped((N, 256, 128), BF), name="x_synthesis_back"
    )(message, X_IN)
    message = exchange(message, "gx")
    grad_point, grad_bias, grad_in, weight_grad = call(
        last_kernel,
        (
            shaped((C, C), F32),
            shaped((1, C), F32),
            shaped(cells, BF),
            shaped((WEIGHTS, KY), F32),
        ),
        name="last",
    )(message, DEPTH_IN, slope, point_weight, coef, dual)
    grad_spec = weight_grad.reshape(C, C, PAIRS, 2, KY).transpose(4, 0, 1, 3, 2)

    def natural(values):
        return values.reshape(CX, C, CY, ZT).transpose(0, 2, 1, 3)

    return natural(output_field), natural(grad_in), grad_spec, grad_point, grad_bias.reshape(C)


def solution(mesh):
    return jax.shard_map(
        body,
        mesh=mesh,
        in_specs=(
            P("gx", "gy", None, None),
            P(),
            P(),
            P(None, None, None, None, ("gx", "gy")),
            P("gx", "gy", None, None),
        ),
        out_specs=(
            P("gx", "gy", None, None),
            P("gx", "gy", None, None),
            P(None, None, None, None, ("gx", "gy")),
            P(),
            P(),
        ),
        check_vma=False,
    )
```

```python
import math

import jax
import jax.numpy as jnp
import ml_dtypes
import numpy as np
from jax import lax
from jax.experimental import pallas as pl
from jax.experimental.pallas import tpu as pltpu
from jax.sharding import PartitionSpec as P

C = 20
Z = 32
T_SIZE = 4
KX = 24
KY = 24
KZ = 24
KT = 4
NX = 256
NY = 128
ZT = 128
M = 96
N = 16
CX = NX // N
CY = NY // N
ROWS = 12 * C
GROUPS = C // 4
PAIRS = 9
WEIGHTS = C * C * PAIRS * 2
FIRST = 0

BF = jnp.bfloat16
F32 = jnp.float32


def centered(count):
    return (np.arange(count) + count // 2) % count - count // 2


def rounded(table):
    return np.asarray(table, np.float32).astype(ml_dtypes.bfloat16)


def line_table(modes, length, scale):
    turns = centered(modes)[:, None] * np.arange(length)[None, :] % length
    angle = turns.astype(np.float32) * np.float32(2.0 * math.pi / length)
    scale = np.float32(scale)
    return rounded(np.cos(angle) * scale), rounded(np.sin(angle) * scale)


def depth_table(scale):
    cells = np.arange(ZT)
    turn_z = centered(KZ)[:, None] * (cells // T_SIZE)[None, :] % Z
    turn_t = centered(KT)[:, None] * (cells % T_SIZE)[None, :] % T_SIZE
    angle = turn_z.astype(np.float32)[:, None, :] * np.float32(2.0 * math.pi / Z)
    angle = angle + turn_t.astype(np.float32)[None, :, :] * np.float32(2.0 * math.pi / T_SIZE)
    angle = angle.reshape(M, ZT)
    return rounded(np.stack([np.cos(angle), -np.sin(angle)]) * np.float32(scale))


def depth_rows(scale):
    table = depth_table(scale).reshape(2, N, 2, 3, ZT).transpose(1, 2, 0, 3, 4)
    table = np.broadcast_to(table[:, :, None], (N, 2, 4, 2, 3, ZT))
    return np.ascontiguousarray(table).reshape(2 * N, 24, ZT)


def x_rows(scale):
    table = np.concatenate(line_table(KX, NX, scale), axis=0)
    return np.ascontiguousarray(np.repeat(table, CY, axis=1))


def y_rows(scale):
    return np.concatenate(line_table(KY, NY, scale), axis=0)


def lane_picks():
    rows, lanes = np.arange(6 * 24)[:, None], np.arange(128)[None, :]
    return rounded((lanes == rows % 24 * 6 + rows // 24) & (rows % 24 < C))


DEPTH_IN = depth_rows(ZT**-0.5)
DEPTH_MID = depth_rows(M**-0.5)
X_IN = x_rows(NX**-0.5)
X_MID = x_rows(KX**-0.5)
Y_ALL = np.concatenate([y_rows(NY**-0.5), y_rows(KY**-0.5), lane_picks()], axis=0)
Y_IN = slice(0, 48)
Y_MID = slice(48, 96)
PICKS = slice(96, 96 + 144)


def dot(left, right, left_dim=1, right_dim=0, precision=None):
    return lax.dot_general(
        left,
        right,
        (((left_dim,), (right_dim,)), ((), ())),
        precision=precision,
        preferred_element_type=F32,
    )


def call(kernel, out_shape, scratch=(), name=None, spaces=None, out_spaces=None, aliases=None):
    options = {}
    if spaces is not None:
        options["in_specs"] = [pl.BlockSpec(memory_space=space) for space in spaces]
        options["out_specs"] = [pl.BlockSpec(memory_space=space) for space in out_spaces]
    return pl.pallas_call(
        kernel,
        out_shape=out_shape,
        scratch_shapes=scratch,
        compiler_params=pltpu.CompilerParams(vmem_limit_bytes=24 * 2**20),
        cost_estimate=pl.CostEstimate(flops=10**8, bytes_accessed=4 * 10**6, transcendentals=0),
        input_output_aliases=aliases or {},
        name=name,
        **options,
    )


def shaped(shape, dtype):
    return jax.ShapeDtypeStruct(shape, dtype)


def rows_of(group, count):
    return slice(group * count, group * count + count)


def iota(shape, dim):
    return lax.broadcasted_iota(jnp.int32, shape, dim)


def ones_where(condition):
    return jnp.where(condition, 1.0, 0.0)


def depth_matrix(rows):
    wide = rows.astype(F32)
    channel = iota((1, 24, 1), 1) // 6
    parts = [(wide * ones_where(channel == k)).reshape(N * 48, ZT) for k in range(4)]
    return jnp.concatenate(parts, axis=1).astype(BF)


def x_matrix(rows):
    size = rows.shape[1]
    same = ones_where(iota((1, CY, size), 1) == iota((1, CY, size), 2) % CY)
    wide = rows.astype(F32).reshape(KX, 1, size) * same
    return wide.reshape(KX * CY, size).astype(BF)


def lane_maps():
    row, lane = iota((ROWS, 1), 0), iota((1, 256), 1)
    inner = row % 24
    start = (row // 24) % 2 * 128 + row // 48 * 24
    real = inner % 6 < 3
    plain = ones_where(lane == start + inner)
    other = jnp.where(real, inner + 3, inner - 3)
    turned = ones_where(lane == start + other) * jnp.where(real, -1.0, 1.0)
    return plain.astype(BF), turned.astype(BF)


def spread_matrix():
    return ones_where(iota((C, C * CY), 0) == iota((C, C * CY), 1) // CY)


def to_columns(values):
    wide = values.astype(F32).reshape(CX, 4, CY, ZT)
    return jnp.concatenate([wide[:, k].reshape(CX * CY, ZT) for k in range(4)], axis=1)


def to_cells(columns):
    parts = [columns[:, k * ZT : (k + 1) * ZT].reshape(CX, CY, ZT) for k in range(4)]
    return jnp.stack(parts, axis=1).reshape(CX, 4 * CY, ZT)


def wide_to_columns(wide):
    def channel(k):
        rows = wide[k * CY : k * CY + CY]
        return jnp.concatenate([rows[:, x * ZT : x * ZT + ZT] for x in range(CX)], axis=0)

    return jnp.concatenate([channel(k) for k in range(4)], axis=1)


def wide_to_cells(wide):
    return jnp.stack([wide[:, x * ZT : x * ZT + ZT] for x in range(CX)], axis=0)


def put_spectra(matrix, columns, first, out):
    spectra = dot(matrix, jnp.concatenate(columns, axis=0), 1, 1).astype(BF)
    for k in range(len(columns)):
        spectrum = spectra[:, k * 128 : k * 128 + 128].reshape(N, 48, 128)
        out[:, rows_of(first + k, 48), :] = spectrum


BATCHES = ((0, 1), (2, 3), (4,))


def spectrum_kernel(field, depth, out):
    matrix = depth_matrix(depth[...])
    for batch in BATCHES:
        columns = [to_columns(field[:, rows_of(g, 32), :]).astype(BF) for g in batch]
        put_spectra(matrix, columns, batch[0], out)


def from_spectra(lines, matrix):
    rows = [lines[:, rows_of(g, 48), :].reshape(N * 48, 128) for g in range(GROUPS)]
    return dot(jnp.concatenate(rows, axis=1), matrix, 0, 0)


def split_dot(left, right):
    high = left.astype(BF)
    low = (left - high.astype(F32)).astype(BF)
    return dot(high, right) + dot(low, right)


def x_analysis_kernel(lines, table, out):
    plain, turned = lane_maps()
    rows = jnp.concatenate([lines[a] for a in range(N)], axis=1)
    matrix = jnp.concatenate([x_matrix(table[:KX]), x_matrix(table[KX:])], axis=0)
    both = dot(matrix, rows, 1, 1)
    half = KX * CY
    coef = split_dot(both[:half], plain) + split_dot(both[half:], turned)
    units = [coef[:, k * 128 : k * 128 + 128].reshape(KX, CY, 128) for k in range(2)]
    out[...] = jnp.stack(units, axis=1).reshape(N, 24, 128).astype(BF)


def x_modes(modes):
    plain, turned = lane_maps()
    units = modes.reshape(KX, 2, CY, 128)
    flat = jnp.concatenate([units[:, k].reshape(KX * CY, 128) for k in range(2)], axis=1)
    flat = flat.astype(BF)
    return dot(plain, flat, 1, 1).astype(BF), dot(turned, flat, 1, 1).astype(BF)


def x_lines(first, second, table):
    lines = dot(first, x_matrix(table[:KX])) + dot(second, x_matrix(table[KX:]))
    return lines.astype(BF)


def x_synthesis_kernel(modes, table, out):
    first, second = x_modes(modes[...].astype(F32))
    lines = x_lines(first, second, table[...])
    for a in range(N):
        out[a] = lines[:, a * 128 : a * 128 + 128]


def when_core(core):
    return pl.when(lax.axis_index("gy") % 2 == core)


def start_weight_gradient(core, coef, dual, made, target, semaphore):
    @when_core(core)
    def _():
        for channel in range(C):
            weight_gradient(coef, dual, channel, made)
        pltpu.make_async_copy(made, target, semaphore).start()


def end_weight_gradient(core, made, target, semaphore):
    @when_core(core)
    def _():
        pltpu.make_async_copy(made, target, semaphore).wait()


def x_synthesis_sums_kernel(modes, table, coef, dual, out, weight_to, made, semaphore):
    start_weight_gradient(FIRST, coef, dual, made, weight_to, semaphore)
    wide = modes[...].astype(F32)
    first, second = x_modes(wide[:, :24])
    lines = x_lines(first, second, table[...])
    sums = jnp.sum(wide[:, 24:], axis=0)
    block = pack_sums(sums[:4] + sums[4:])
    tail = jnp.concatenate([block, jnp.zeros_like(block)], axis=0).astype(BF)
    for a in range(N):
        out[a, :ROWS] = lines[:, a * 128 : a * 128 + 128]
        out[a, ROWS:] = tail
    end_weight_gradient(FIRST, made, weight_to, semaphore)


def pack_sums(values):
    high = values.astype(BF).astype(F32)
    return jnp.concatenate([high, values - high], axis=0)


def turn_lanes(values, sign):
    part = iota(values.shape, 1) % 6
    ahead = pltpu.roll(values, 125, 1)
    behind = pltpu.roll(values, 3, 1)
    return jnp.where(part < 3, sign * ahead, -sign * behind)


def y_analysis(lines, table, picks):
    wide = lines.astype(F32).reshape(N, 3, CY, 128)
    wide = jnp.concatenate([wide[:, u].reshape(NY, 128) for u in range(3)], axis=1)
    both = dot(table, wide.astype(BF))
    result = []
    for u in range(3):
        piece = both[:, u * 128 : u * 128 + 128]
        coef = piece[:KY] + turn_lanes(piece[KY:], 1.0)
        result.append(dot(picks, coef.astype(BF), 1, 1))
    return result


def y_synthesis(units, table, picks):
    columns = []
    for unit in units:
        modes = dot(unit.astype(BF), picks, 0, 0)
        columns.append(jnp.concatenate([modes, turn_lanes(modes, -1.0)], axis=0))
    columns = jnp.concatenate(columns, axis=1).astype(BF)
    lines = dot(table, columns, 0, 0)
    lines = [lines[:, u * 128 : u * 128 + 128].reshape(N, CY, 128) for u in range(3)]
    return jnp.stack(lines, axis=1).reshape(N, 24, 128)


def line_of(modes, unit, kind, channel):
    return modes[unit, pl.ds(kind * 24 + channel, 1), :]


def load_weights(weights, wide):
    step = WEIGHTS // 10
    for k in range(10):
        wide[k * step : k * step + step, :] = weights[k * step : k * step + step, :].astype(F32)


def mix_channels(weights, modes, out_step, in_step, sign):
    units = []
    for unit in range(3):
        reals, imags = [], []
        for mode in range(3):
            pair = unit * 3 + mode
            real = jnp.zeros((C, KY), F32)
            imag = jnp.zeros((C, KY), F32)
            for k in range(C):
                start = k * in_step + 2 * pair
                weight_re = weights[pl.ds(start, C, stride=out_step), :]
                weight_im = weights[pl.ds(start + 1, C, stride=out_step), :]
                re = line_of(modes, unit, mode, k)
                im = line_of(modes, unit, 3 + mode, k)
                real = real + (weight_re * re - sign * (weight_im * im))
                imag = imag + (weight_re * im + sign * (weight_im * re))
            reals.append(real)
            imags.append(imag)
        empty = jnp.zeros((4, KY), F32)
        parts = [jnp.concatenate([part, empty], axis=0) for part in reals + imags]
        units.append(jnp.concatenate(parts, axis=0))
    return units


def product_kernel(lines, weights, tables, out, coef, wide):
    load_weights(weights, wide)
    for u, unit in enumerate(y_analysis(lines[...], tables[Y_IN], tables[PICKS])):
        coef[u] = unit
    product = mix_channels(wide, coef, 2 * PAIRS, 2 * PAIRS * C, 1.0)
    out[...] = y_synthesis(product, tables[Y_MID], tables[PICKS]).astype(BF)


def back_kernel(lines, weights, sums, tables, out, dual, wide):
    load_weights(weights, wide)
    for u, unit in enumerate(y_analysis(lines[...], tables[Y_MID], tables[PICKS])):
        dual[u] = unit
    modes = mix_channels(wide, dual, 2 * PAIRS * C, 2 * PAIRS, -1.0)
    modes = y_synthesis(modes, tables[Y_IN], tables[PICKS])
    tail = jnp.broadcast_to(sums[...].reshape(1, 8, 128), (N, 8, 128))
    out[...] = jnp.concatenate([modes, tail], axis=1).astype(BF)


def weight_gradient(coef, dual, channel, out):
    for pair in range(PAIRS):
        unit, mode = divmod(pair, 3)
        dual_re = dual[unit, mode * 24 : mode * 24 + C, :]
        dual_im = dual[unit, (3 + mode) * 24 : (3 + mode) * 24 + C, :]
        re = line_of(coef, unit, mode, channel)
        im = line_of(coef, unit, 3 + mode, channel)
        start = channel * 2 * PAIRS * C + 2 * pair
        out[pl.ds(start, C, stride=2 * PAIRS), :] = re * dual_re + im * dual_im
        out[pl.ds(start + 1, C, stride=2 * PAIRS), :] = re * dual_im - im * dual_re


def same_cell(size):
    return ones_where(iota((size, 1), 0) % CY == iota((1, size), 1) % CY)


def spread_map(weight, weight_dim):
    spread = spread_matrix().astype(BF)
    tall = dot(spread, weight, 0, weight_dim).astype(BF)
    return (dot(tall, spread) * same_cell(C * CY)).astype(BF)


def flat_cells(values):
    return jnp.concatenate([values[x] for x in range(CX)], axis=1)


def pack_lines(cross, bias):
    picks = spread_matrix()
    exact = lax.Precision.HIGHEST
    point = dot(dot(picks, cross * same_cell(C * CY), 1, 0, exact), picks, 1, 1, exact)
    total = dot(bias, picks, 1, 1, exact)[:1]
    rows = jnp.concatenate([point, total], axis=0)
    rows = jnp.concatenate([rows, jnp.zeros((C + 1, 128 - C), F32)], axis=1)
    packed = []
    for r in range(4):
        line = jnp.zeros((1, 128), F32)
        for q in range(6):
            if r * 6 + q <= C:
                row = rows[r * 6 + q : r * 6 + q + 1]
                line = line + (pltpu.roll(row, q * C, 1) if q > 0 else row)
        packed.append(line)
    return jnp.concatenate(packed, axis=0)


def cells_kernel(
    lines, depth, field, cotangent, weight, bias, out, sums, slope_out, field_out
):
    matrix = depth_matrix(depth[...])
    mixing = spread_map(weight[...], 1)
    shift = dot(spread_matrix(), bias[...], 0, 1, lax.Precision.HIGHEST)
    fields = flat_cells(field)
    spectral = from_spectra(lines, matrix)
    pointwise = dot(mixing, fields) + shift
    slopes = []
    for batch in BATCHES:
        columns = []
        for group in batch:
            span = rows_of(group, 32)
            pre = spectral[rows_of(group, 128)] + wide_to_columns(pointwise[span])
            phi = 0.5 * (1.0 + lax.erf(pre * 0.7071067811865476))
            field_out[:, span, :] = to_cells(pre * phi).astype(BF)
            slope = phi + pre * jnp.exp(-0.5 * pre * pre) * 0.3989422804014327
            slope = slope * to_columns(cotangent[:, span, :])
            columns.append(slope.astype(BF))
            slope = to_cells(slope).astype(BF)
            slope_out[:, span, :] = slope
            slopes.append(flat_cells(slope))
        put_spectra(matrix, columns, batch[0], out)
    slopes = jnp.concatenate(slopes, axis=0)
    cross = dot(fields, slopes, 1, 1)
    total = dot(jnp.ones((8, CX * ZT), BF), slopes, 1, 1)
    sums[...] = pack_sums(pack_lines(cross, total))


def last_kernel(
    lines,
    depth,
    slope,
    weight,
    coef,
    dual,
    _,
    point_out,
    bias_out,
    field_out,
    weight_to,
    made,
    semaphore,
):
    start_weight_gradient(1 - FIRST, coef, dual, made, weight_to, semaphore)
    tails = jnp.sum(lines[:, ROWS:, :].astype(F32), axis=0)
    sums = (tails[:4] + tails[4:8]) * (NX * NY * ZT) ** -0.5
    for r in range(4):
        for q in range(6):
            index = r * 6 + q
            if index <= C:
                row = sums[r : r + 1]
                row = pltpu.roll(row, 128 - q * C, 1) if q > 0 else row
                if index < C:
                    point_out[index : index + 1, :] = row[:, :C]
                else:
                    bias_out[...] = row[:, :C]
    pointwise = dot(spread_map(weight[...], 0), flat_cells(slope))
    spectral = from_spectra(lines, depth_matrix(depth[...]))
    for group in range(GROUPS):
        span = rows_of(group, 32)
        total = to_cells(spectral[rows_of(group, 128)]) + wide_to_cells(pointwise[span])
        field_out[:, span, :] = total.astype(BF)
    end_weight_gradient(1 - FIRST, made, weight_to, semaphore)


def exchange(values, axis):
    return lax.all_to_all(values, axis, split_axis=0, concat_axis=0, tiled=True)


def body(field_in, point_weight, point_bias, spec_weight, out_cotangent):
    cells = (CX, C * CY, ZT)
    line_message = shaped((N, ROWS, 128), BF)
    mode_message = shaped((N, 24, 128), BF)
    mode_lines = shaped((3, 144, KY), F32)
    wide_weights = pltpu.VMEM((WEIGHTS, KY), F32)
    field = field_in.transpose(0, 2, 1, 3).reshape(cells)
    cotangent = out_cotangent.transpose(0, 2, 1, 3).reshape(cells)
    weights = spec_weight.transpose(1, 2, 4, 3, 0).reshape(WEIGHTS, KY)

    message = call(spectrum_kernel, line_message, name="spectrum")(field, DEPTH_IN)
    message = exchange(message, "gx")
    message = call(x_analysis_kernel, mode_message, name="x_analysis")(message, X_IN)
    message = exchange(message, "gy")
    message, coef = call(
        product_kernel, (mode_message, mode_lines), scratch=[wide_weights], name="product"
    )(message, weights, Y_ALL)
    message = exchange(message, "gy")
    message = call(x_synthesis_kernel, line_message, name="x_synthesis")(message, X_MID)
    message = exchange(message, "gx")
    message, sums, slope, output_field = call(
        cells_kernel,
        (line_message, shaped((8, 128), F32), shaped(cells, BF), shaped(cells, BF)),
        name="cells",
    )(message, DEPTH_MID, field, cotangent, point_weight, point_bias.reshape(1, C))
    message = exchange(message, "gx")
    message = call(x_analysis_kernel, mode_message, name="x_analysis_back")(message, X_MID)
    message = exchange(message, "gy")
    message, dual = call(
        back_kernel,
        (shaped((N, 32, 128), BF), mode_lines),
        scratch=[wide_weights],
        name="back",
    )(message, weights, sums, Y_ALL)
    message = exchange(message, "gy")
    made = [wide_weights, pltpu.SemaphoreType.DMA(())]
    weight_shape = shaped((WEIGHTS, KY), F32)
    message, weight_grad = call(
        x_synthesis_sums_kernel,
        (shaped((N, 256, 128), BF), weight_shape),
        made,
        "x_synthesis_back",
        [pltpu.VMEM] * 4,
        [pltpu.VMEM, pl.ANY],
    )(message, X_IN, coef, dual)
    message = exchange(message, "gx")
    grad_point, grad_bias, grad_in, weight_grad = call(
        last_kernel,
        (shaped((C, C), F32), shaped((1, C), F32), shaped(cells, BF), weight_shape),
        made,
        "last",
        [pltpu.VMEM] * 6 + [pl.ANY],
        [pltpu.VMEM] * 3 + [pl.ANY],
        {6: 3},
    )(message, DEPTH_IN, slope, point_weight, coef, dual, weight_grad)
    grad_spec = weight_grad.reshape(C, C, PAIRS, 2, KY).transpose(4, 0, 1, 3, 2)

    def natural(values):
        return values.reshape(CX, C, CY, ZT).transpose(0, 2, 1, 3)

    return natural(output_field), natural(grad_in), grad_spec, grad_point, grad_bias.reshape(C)


def solution(mesh):
    return jax.shard_map(
        body,
        mesh=mesh,
        in_specs=(
            P("gx", "gy", None, None),
            P(),
            P(),
            P(None, None, None, None, ("gx", "gy")),
            P("gx", "gy", None, None),
        ),
        out_specs=(
            P("gx", "gy", None, None),
            P("gx", "gy", None, None),
            P(None, None, None, None, ("gx", "gy")),
            P(),
            P(),
        ),
        check_vma=False,
    )
```

```python
import math

import jax
import jax.numpy as jnp
import ml_dtypes
import numpy as np
from jax import lax
from jax.experimental import pallas as pl
from jax.experimental.pallas import tpu as pltpu
from jax.sharding import PartitionSpec as P

C = 20
Z = 32
T_SIZE = 4
KX = 24
KY = 24
KZ = 24
KT = 4
NX = 256
NY = 128
ZT = 128
M = 96
N = 16
CX = NX // N
CY = NY // N
ROWS = 12 * C
GROUPS = C // 4
PAIRS = 9
WEIGHTS = C * C * PAIRS * 2
FIRST = 0

BF = jnp.bfloat16
F32 = jnp.float32


def centered(count):
    return (np.arange(count) + count // 2) % count - count // 2


def rounded(table):
    return np.asarray(table, np.float32).astype(ml_dtypes.bfloat16)


def line_table(modes, length, scale):
    turns = centered(modes)[:, None] * np.arange(length)[None, :] % length
    angle = turns.astype(np.float32) * np.float32(2.0 * math.pi / length)
    scale = np.float32(scale)
    return rounded(np.cos(angle) * scale), rounded(np.sin(angle) * scale)


def depth_table(scale):
    cells = np.arange(ZT)
    turn_z = centered(KZ)[:, None] * (cells // T_SIZE)[None, :] % Z
    turn_t = centered(KT)[:, None] * (cells % T_SIZE)[None, :] % T_SIZE
    angle = turn_z.astype(np.float32)[:, None, :] * np.float32(2.0 * math.pi / Z)
    angle = angle + turn_t.astype(np.float32)[None, :, :] * np.float32(2.0 * math.pi / T_SIZE)
    angle = angle.reshape(M, ZT)
    return rounded(np.stack([np.cos(angle), -np.sin(angle)]) * np.float32(scale))


def depth_rows(scale):
    table = depth_table(scale).reshape(2, N, 2, 3, ZT).transpose(1, 2, 0, 3, 4)
    table = np.broadcast_to(table[:, :, None], (N, 2, 4, 2, 3, ZT))
    return np.ascontiguousarray(table).reshape(2 * N, 24, ZT)


def x_rows(scale):
    table = np.concatenate(line_table(KX, NX, scale), axis=0)
    return np.ascontiguousarray(np.repeat(table, CY, axis=1))


def y_rows(scale):
    return np.concatenate(line_table(KY, NY, scale), axis=0)


def lane_picks():
    rows, lanes = np.arange(6 * 24)[:, None], np.arange(128)[None, :]
    return rounded((lanes == rows % 24 * 6 + rows // 24) & (rows % 24 < C))


DEPTH_IN = depth_rows(ZT**-0.5)
DEPTH_MID = depth_rows(M**-0.5)
X_IN = x_rows(NX**-0.5)
X_MID = x_rows(KX**-0.5)
Y_ALL = np.concatenate([y_rows(NY**-0.5), y_rows(KY**-0.5), lane_picks()], axis=0)
Y_IN = slice(0, 48)
Y_MID = slice(48, 96)
PICKS = slice(96, 96 + 144)


def dot(left, right, left_dim=1, right_dim=0, precision=None):
    return lax.dot_general(
        left,
        right,
        (((left_dim,), (right_dim,)), ((), ())),
        precision=precision,
        preferred_element_type=F32,
    )


def call(kernel, out_shape, scratch=(), name=None, spaces=None, out_spaces=None, aliases=None):
    options = {}
    if spaces is not None:
        options["in_specs"] = [pl.BlockSpec(memory_space=space) for space in spaces]
        options["out_specs"] = [pl.BlockSpec(memory_space=space) for space in out_spaces]
    return pl.pallas_call(
        kernel,
        out_shape=out_shape,
        scratch_shapes=scratch,
        compiler_params=pltpu.CompilerParams(vmem_limit_bytes=24 * 2**20),
        cost_estimate=pl.CostEstimate(flops=10**8, bytes_accessed=4 * 10**6, transcendentals=0),
        input_output_aliases=aliases or {},
        name=name,
        **options,
    )


def shaped(shape, dtype):
    return jax.ShapeDtypeStruct(shape, dtype)


def rows_of(group, count):
    return slice(group * count, group * count + count)


def iota(shape, dim):
    return lax.broadcasted_iota(jnp.int32, shape, dim)


def ones_where(condition):
    return jnp.where(condition, 1.0, 0.0)


def depth_matrix(rows):
    wide = rows.astype(F32)
    channel = iota((1, 24, 1), 1) // 6
    parts = [(wide * ones_where(channel == k)).reshape(N * 48, ZT) for k in range(4)]
    return jnp.concatenate(parts, axis=1).astype(BF)


def x_matrix(rows):
    size = rows.shape[1]
    same = ones_where(iota((1, CY, size), 1) == iota((1, CY, size), 2) % CY)
    wide = rows.reshape(KX, 1, size) * same
    return wide.reshape(KX * CY, size).astype(BF)


def lane_maps():
    row, lane = iota((ROWS, 1), 0), iota((1, 256), 1)
    inner = row % 24
    start = (row // 24) % 2 * 128 + row // 48 * 24
    real = inner % 6 < 3
    plain = ones_where(lane == start + inner)
    other = jnp.where(real, inner + 3, inner - 3)
    turned = ones_where(lane == start + other) * jnp.where(real, -1.0, 1.0)
    return plain.astype(BF), turned.astype(BF)


def spread_matrix():
    return ones_where(iota((C, C * CY), 0) == iota((C, C * CY), 1) // CY)


def to_columns(values):
    wide = values.astype(F32).reshape(CX, 4, CY, ZT)
    return jnp.concatenate([wide[:, k].reshape(CX * CY, ZT) for k in range(4)], axis=1)


def to_cells(columns):
    parts = [columns[:, k * ZT : (k + 1) * ZT].reshape(CX, CY, ZT) for k in range(4)]
    return jnp.stack(parts, axis=1).reshape(CX, 4 * CY, ZT)


def wide_to_columns(wide):
    def channel(k):
        rows = wide[k * CY : k * CY + CY]
        return jnp.concatenate([rows[:, x * ZT : x * ZT + ZT] for x in range(CX)], axis=0)

    return jnp.concatenate([channel(k) for k in range(4)], axis=1)


def wide_to_cells(wide):
    return jnp.stack([wide[:, x * ZT : x * ZT + ZT] for x in range(CX)], axis=0)


def put_spectra(matrix, columns, first, out):
    spectra = dot(matrix, jnp.concatenate(columns, axis=0), 1, 1).astype(BF)
    for k in range(len(columns)):
        spectrum = spectra[:, k * 128 : k * 128 + 128].reshape(N, 48, 128)
        out[:, rows_of(first + k, 48), :] = spectrum


BATCHES = ((0, 1), (2, 3), (4,))


def spectrum_kernel(field, depth, out):
    matrix = depth_matrix(depth[...])
    for batch in BATCHES:
        columns = [to_columns(field[:, rows_of(g, 32), :]).astype(BF) for g in batch]
        put_spectra(matrix, columns, batch[0], out)


def from_spectra(lines, matrix):
    rows = [lines[:, rows_of(g, 48), :].reshape(N * 48, 128) for g in range(GROUPS)]
    return dot(jnp.concatenate(rows, axis=1), matrix, 0, 0)


def split_dot(left, right):
    high = left.astype(BF)
    low = (left - high.astype(F32)).astype(BF)
    return dot(high, right) + dot(low, right)


def x_analysis_kernel(lines, table, out):
    plain, turned = lane_maps()
    rows = jnp.concatenate([lines[a] for a in range(N)], axis=1)
    table = table[...].astype(F32)
    matrix = jnp.concatenate([x_matrix(table[:KX]), x_matrix(table[KX:])], axis=0)
    both = dot(matrix, rows, 1, 1)
    half = KX * CY
    coef = split_dot(both[:half], plain) + split_dot(both[half:], turned)
    units = [coef[:, k * 128 : k * 128 + 128].reshape(KX, CY, 128) for k in range(2)]
    out[...] = jnp.stack(units, axis=1).reshape(N, 24, 128).astype(BF)


def x_modes(modes):
    plain, turned = lane_maps()
    units = modes.reshape(KX, 2, CY, 128)
    flat = jnp.concatenate([units[:, k].reshape(KX * CY, 128) for k in range(2)], axis=1)
    flat = flat.astype(BF)
    return dot(plain, flat, 1, 1).astype(BF), dot(turned, flat, 1, 1).astype(BF)


def x_lines(first, second, table):
    table = table.astype(F32)
    lines = dot(first, x_matrix(table[:KX])) + dot(second, x_matrix(table[KX:]))
    return lines.astype(BF)


def x_synthesis_kernel(modes, table, out):
    first, second = x_modes(modes[...].astype(F32))
    lines = x_lines(first, second, table[...])
    for a in range(N):
        out[a] = lines[:, a * 128 : a * 128 + 128]


def when_core(core):
    return pl.when(lax.axis_index("gy") % 2 == core)


def start_weight_gradient(core, coef, dual, made, target, semaphore):
    @when_core(core)
    def _():
        for channel in range(C):
            weight_gradient(coef, dual, channel, made)
        pltpu.make_async_copy(made, target, semaphore).start()


def end_weight_gradient(core, made, target, semaphore):
    @when_core(core)
    def _():
        pltpu.make_async_copy(made, target, semaphore).wait()


def x_synthesis_sums_kernel(modes, table, coef, dual, out, weight_to, made, semaphore):
    start_weight_gradient(FIRST, coef, dual, made, weight_to, semaphore)
    wide = modes[...].astype(F32)
    first, second = x_modes(wide[:, :24])
    lines = x_lines(first, second, table[...])
    sums = jnp.sum(wide[:, 24:], axis=0)
    block = pack_sums(sums[:4] + sums[4:])
    tail = jnp.concatenate([block, jnp.zeros_like(block)], axis=0).astype(BF)
    for a in range(N):
        out[a, :ROWS] = lines[:, a * 128 : a * 128 + 128]
        out[a, ROWS:] = tail
    end_weight_gradient(FIRST, made, weight_to, semaphore)


def pack_sums(values):
    high = values.astype(BF).astype(F32)
    return jnp.concatenate([high, values - high], axis=0)


def turn_lanes(values, sign):
    part = iota(values.shape, 1) % 6
    ahead = pltpu.roll(values, 125, 1)
    behind = pltpu.roll(values, 3, 1)
    return jnp.where(part < 3, sign * ahead, -sign * behind)


def y_analysis(lines, table, picks):
    wide = lines.astype(F32).reshape(N, 3, CY, 128)
    wide = jnp.concatenate([wide[:, u].reshape(NY, 128) for u in range(3)], axis=1)
    both = dot(table, wide.astype(BF))
    result = []
    for u in range(3):
        piece = both[:, u * 128 : u * 128 + 128]
        coef = piece[:KY] + turn_lanes(piece[KY:], 1.0)
        result.append(dot(picks, coef.astype(BF), 1, 1))
    return result


def y_synthesis(units, table, picks):
    columns = []
    for unit in units:
        modes = dot(unit.astype(BF), picks, 0, 0)
        columns.append(jnp.concatenate([modes, turn_lanes(modes, -1.0)], axis=0))
    columns = jnp.concatenate(columns, axis=1).astype(BF)
    lines = dot(table, columns, 0, 0)
    lines = [lines[:, u * 128 : u * 128 + 128].reshape(N, CY, 128) for u in range(3)]
    return jnp.stack(lines, axis=1).reshape(N, 24, 128)


def line_of(modes, unit, kind, channel):
    return modes[unit, pl.ds(kind * 24 + channel, 1), :]


def load_weights(weights, wide):
    step = WEIGHTS // 10
    for k in range(10):
        wide[k * step : k * step + step, :] = weights[k * step : k * step + step, :].astype(F32)


def mix_channels(weights, modes, out_step, in_step, sign):
    units = []
    for unit in range(3):
        reals, imags = [], []
        for mode in range(3):
            pair = unit * 3 + mode
            real = jnp.zeros((C, KY), F32)
            imag = jnp.zeros((C, KY), F32)
            for k in range(C):
                start = k * in_step + 2 * pair
                weight_re = weights[pl.ds(start, C, stride=out_step), :]
                weight_im = weights[pl.ds(start + 1, C, stride=out_step), :]
                re = line_of(modes, unit, mode, k)
                im = line_of(modes, unit, 3 + mode, k)
                real = real + (weight_re * re - sign * (weight_im * im))
                imag = imag + (weight_re * im + sign * (weight_im * re))
            reals.append(real)
            imags.append(imag)
        empty = jnp.zeros((4, KY), F32)
        parts = [jnp.concatenate([part, empty], axis=0) for part in reals + imags]
        units.append(jnp.concatenate(parts, axis=0))
    return units


def product_kernel(lines, weights, tables, out, coef, wide):
    load_weights(weights, wide)
    for u, unit in enumerate(y_analysis(lines[...], tables[Y_IN], tables[PICKS])):
        coef[u] = unit
    product = mix_channels(wide, coef, 2 * PAIRS, 2 * PAIRS * C, 1.0)
    out[...] = y_synthesis(product, tables[Y_MID], tables[PICKS]).astype(BF)


def back_kernel(lines, weights, sums, tables, out, dual, wide):
    load_weights(weights, wide)
    for u, unit in enumerate(y_analysis(lines[...], tables[Y_MID], tables[PICKS])):
        dual[u] = unit
    modes = mix_channels(wide, dual, 2 * PAIRS * C, 2 * PAIRS, -1.0)
    modes = y_synthesis(modes, tables[Y_IN], tables[PICKS])
    tail = jnp.broadcast_to(sums[...].reshape(1, 8, 128), (N, 8, 128))
    out[...] = jnp.concatenate([modes, tail], axis=1).astype(BF)


def weight_gradient(coef, dual, channel, out):
    for pair in range(PAIRS):
        unit, mode = divmod(pair, 3)
        dual_re = dual[unit, mode * 24 : mode * 24 + C, :]
        dual_im = dual[unit, (3 + mode) * 24 : (3 + mode) * 24 + C, :]
        re = line_of(coef, unit, mode, channel)
        im = line_of(coef, unit, 3 + mode, channel)
        start = channel * 2 * PAIRS * C + 2 * pair
        out[pl.ds(start, C, stride=2 * PAIRS), :] = re * dual_re + im * dual_im
        out[pl.ds(start + 1, C, stride=2 * PAIRS), :] = re * dual_im - im * dual_re


def same_cell(size):
    return ones_where(iota((size, 1), 0) % CY == iota((1, size), 1) % CY)


def spread_map(weight, weight_dim):
    spread = spread_matrix().astype(BF)
    tall = dot(spread, weight, 0, weight_dim).astype(BF)
    return (dot(tall, spread) * same_cell(C * CY)).astype(BF)


def flat_cells(values):
    return jnp.concatenate([values[x] for x in range(CX)], axis=1)


def pack_lines(cross, bias):
    picks = spread_matrix()
    exact = lax.Precision.HIGHEST
    point = dot(dot(picks, cross * same_cell(C * CY), 1, 0, exact), picks, 1, 1, exact)
    total = dot(bias, picks, 1, 1, exact)[:1]
    rows = jnp.concatenate([point, total], axis=0)
    rows = jnp.concatenate([rows, jnp.zeros((C + 1, 128 - C), F32)], axis=1)
    packed = []
    for r in range(4):
        line = jnp.zeros((1, 128), F32)
        for q in range(6):
            if r * 6 + q <= C:
                row = rows[r * 6 + q : r * 6 + q + 1]
                line = line + (pltpu.roll(row, q * C, 1) if q > 0 else row)
        packed.append(line)
    return jnp.concatenate(packed, axis=0)


def cells_kernel(
    lines, depth, field, cotangent, weight, bias, out, sums, slope_out, field_out
):
    matrix = depth_matrix(depth[...])
    mixing = spread_map(weight[...], 1)
    shift = dot(spread_matrix(), bias[...], 0, 1, lax.Precision.HIGHEST)
    fields = flat_cells(field)
    spectral = from_spectra(lines, matrix)
    pointwise = dot(mixing, fields) + shift
    slopes = []
    for batch in BATCHES:
        columns = []
        for group in batch:
            span = rows_of(group, 32)
            pre = spectral[rows_of(group, 128)] + wide_to_columns(pointwise[span])
            phi = 0.5 * (1.0 + lax.erf(pre * 0.7071067811865476))
            field_out[:, span, :] = to_cells(pre * phi).astype(BF)
            slope = phi + pre * jnp.exp(-0.5 * pre * pre) * 0.3989422804014327
            slope = slope * to_columns(cotangent[:, span, :])
            columns.append(slope.astype(BF))
            slope = to_cells(slope).astype(BF)
            slope_out[:, span, :] = slope
            slopes.append(flat_cells(slope))
        put_spectra(matrix, columns, batch[0], out)
    slopes = jnp.concatenate(slopes, axis=0)
    cross = dot(fields, slopes, 1, 1)
    total = dot(jnp.ones((8, CX * ZT), BF), slopes, 1, 1)
    sums[...] = pack_sums(pack_lines(cross, total))


def last_kernel(
    lines,
    depth,
    slope,
    weight,
    coef,
    dual,
    _,
    point_out,
    bias_out,
    field_out,
    weight_to,
    made,
    semaphore,
):
    start_weight_gradient(1 - FIRST, coef, dual, made, weight_to, semaphore)
    tails = jnp.sum(lines[:, ROWS:, :].astype(F32), axis=0)
    sums = (tails[:4] + tails[4:8]) * (NX * NY * ZT) ** -0.5
    for r in range(4):
        for q in range(6):
            index = r * 6 + q
            if index <= C:
                row = sums[r : r + 1]
                row = pltpu.roll(row, 128 - q * C, 1) if q > 0 else row
                if index < C:
                    point_out[index : index + 1, :] = row[:, :C]
                else:
                    bias_out[...] = row[:, :C]
    pointwise = dot(spread_map(weight[...], 0), flat_cells(slope))
    spectral = from_spectra(lines, depth_matrix(depth[...]))
    for group in range(GROUPS):
        span = rows_of(group, 32)
        total = to_cells(spectral[rows_of(group, 128)]) + wide_to_cells(pointwise[span])
        field_out[:, span, :] = total.astype(BF)
    end_weight_gradient(1 - FIRST, made, weight_to, semaphore)


def exchange(values, axis):
    return lax.all_to_all(values, axis, split_axis=0, concat_axis=0, tiled=True)


def body(field_in, point_weight, point_bias, spec_weight, out_cotangent):
    cells = (CX, C * CY, ZT)
    line_message = shaped((N, ROWS, 128), BF)
    mode_message = shaped((N, 24, 128), BF)
    mode_lines = shaped((3, 144, KY), F32)
    wide_weights = pltpu.VMEM((WEIGHTS, KY), F32)
    field = field_in.transpose(0, 2, 1, 3).reshape(cells)
    cotangent = out_cotangent.transpose(0, 2, 1, 3).reshape(cells)
    weights = spec_weight.transpose(1, 2, 4, 3, 0).reshape(WEIGHTS, KY)

    message = call(spectrum_kernel, line_message, name="spectrum")(field, DEPTH_IN)
    message = exchange(message, "gx")
    message = call(x_analysis_kernel, mode_message, name="x_analysis")(message, X_IN)
    message = exchange(message, "gy")
    message, coef = call(
        product_kernel, (mode_message, mode_lines), scratch=[wide_weights], name="product"
    )(message, weights, Y_ALL)
    message = exchange(message, "gy")
    message = call(x_synthesis_kernel, line_message, name="x_synthesis")(message, X_MID)
    message = exchange(message, "gx")
    message, sums, slope, output_field = call(
        cells_kernel,
        (line_message, shaped((8, 128), F32), shaped(cells, BF), shaped(cells, BF)),
        name="cells",
    )(message, DEPTH_MID, field, cotangent, point_weight, point_bias.reshape(1, C))
    message = exchange(message, "gx")
    message = call(x_analysis_kernel, mode_message, name="x_analysis_back")(message, X_MID)
    message = exchange(message, "gy")
    message, dual = call(
        back_kernel,
        (shaped((N, 32, 128), BF), mode_lines),
        scratch=[wide_weights],
        name="back",
    )(message, weights, sums, Y_ALL)
    message = exchange(message, "gy")
    made = [wide_weights, pltpu.SemaphoreType.DMA(())]
    weight_shape = shaped((WEIGHTS, KY), F32)
    message, weight_grad = call(
        x_synthesis_sums_kernel,
        (shaped((N, 256, 128), BF), weight_shape),
        made,
        "x_synthesis_back",
        [pltpu.VMEM] * 4,
        [pltpu.VMEM, pl.ANY],
    )(message, X_IN, coef, dual)
    message = exchange(message, "gx")
    grad_point, grad_bias, grad_in, weight_grad = call(
        last_kernel,
        (shaped((C, C), F32), shaped((1, C), F32), shaped(cells, BF), weight_shape),
        made,
        "last",
        [pltpu.VMEM] * 6 + [pl.ANY],
        [pltpu.VMEM] * 3 + [pl.ANY],
        {6: 3},
    )(message, DEPTH_IN, slope, point_weight, coef, dual, weight_grad)
    grad_spec = weight_grad.reshape(C, C, PAIRS, 2, KY).transpose(4, 0, 1, 3, 2)

    def natural(values):
        return values.reshape(CX, C, CY, ZT).transpose(0, 2, 1, 3)

    return natural(output_field), natural(grad_in), grad_spec, grad_point, grad_bias.reshape(C)


def solution(mesh):
    return jax.shard_map(
        body,
        mesh=mesh,
        in_specs=(
            P("gx", "gy", None, None),
            P(),
            P(),
            P(None, None, None, None, ("gx", "gy")),
            P("gx", "gy", None, None),
        ),
        out_specs=(
            P("gx", "gy", None, None),
            P("gx", "gy", None, None),
            P(None, None, None, None, ("gx", "gy")),
            P(),
            P(),
        ),
        check_vma=False,
    )
```

```python
import math

import jax
import jax.numpy as jnp
import ml_dtypes
import numpy as np
from jax import lax
from jax.experimental import pallas as pl
from jax.experimental.pallas import tpu as pltpu
from jax.sharding import PartitionSpec as P

C = 20
Z = 32
T_SIZE = 4
KX = 24
KY = 24
KZ = 24
KT = 4
NX = 256
NY = 128
ZT = 128
M = 96
N = 16
CX = NX // N
CY = NY // N
ROWS = 12 * C
GROUPS = C // 4
PAIRS = 9
WEIGHTS = C * C * PAIRS * 2
FIRST = 0

BF = jnp.bfloat16
F32 = jnp.float32


def centered(count):
    return (np.arange(count) + count // 2) % count - count // 2


def rounded(table):
    return np.asarray(table, np.float32).astype(ml_dtypes.bfloat16)


def line_table(modes, length, scale):
    turns = centered(modes)[:, None] * np.arange(length)[None, :] % length
    angle = turns.astype(np.float32) * np.float32(2.0 * math.pi / length)
    scale = np.float32(scale)
    return rounded(np.cos(angle) * scale), rounded(np.sin(angle) * scale)


def depth_table(scale):
    cells = np.arange(ZT)
    turn_z = centered(KZ)[:, None] * (cells // T_SIZE)[None, :] % Z
    turn_t = centered(KT)[:, None] * (cells % T_SIZE)[None, :] % T_SIZE
    angle = turn_z.astype(np.float32)[:, None, :] * np.float32(2.0 * math.pi / Z)
    angle = angle + turn_t.astype(np.float32)[None, :, :] * np.float32(2.0 * math.pi / T_SIZE)
    angle = angle.reshape(M, ZT)
    return rounded(np.stack([np.cos(angle), -np.sin(angle)]) * np.float32(scale))


def depth_rows(scale):
    table = depth_table(scale).reshape(2, N, 2, 3, ZT).transpose(1, 2, 0, 3, 4)
    table = np.broadcast_to(table[:, :, None], (N, 2, 4, 2, 3, ZT))
    return np.ascontiguousarray(table).reshape(2 * N, 24, ZT)


def x_rows(scale):
    table = np.concatenate(line_table(KX, NX, scale), axis=0)
    return np.ascontiguousarray(np.repeat(table, CY, axis=1))


def y_rows(scale):
    return np.concatenate(line_table(KY, NY, scale), axis=0)


def lane_picks():
    rows, lanes = np.arange(6 * 24)[:, None], np.arange(128)[None, :]
    return rounded((lanes == rows % 24 * 6 + rows // 24) & (rows % 24 < C))


DEPTH_IN = depth_rows(ZT**-0.5)
DEPTH_MID = depth_rows(M**-0.5)
X_IN = x_rows(NX**-0.5)
X_MID = x_rows(KX**-0.5)
Y_ALL = np.concatenate([y_rows(NY**-0.5), y_rows(KY**-0.5), lane_picks()], axis=0)
Y_IN = slice(0, 48)
Y_MID = slice(48, 96)
PICKS = slice(96, 96 + 144)


def dot(left, right, left_dim=1, right_dim=0, precision=None):
    return lax.dot_general(
        left,
        right,
        (((left_dim,), (right_dim,)), ((), ())),
        precision=precision,
        preferred_element_type=F32,
    )


def call(kernel, out_shape, scratch=(), name=None, spaces=None, out_spaces=None, aliases=None):
    options = {}
    if spaces is not None:
        options["in_specs"] = [pl.BlockSpec(memory_space=space) for space in spaces]
        options["out_specs"] = [pl.BlockSpec(memory_space=space) for space in out_spaces]
    return pl.pallas_call(
        kernel,
        out_shape=out_shape,
        scratch_shapes=scratch,
        compiler_params=pltpu.CompilerParams(vmem_limit_bytes=24 * 2**20),
        cost_estimate=pl.CostEstimate(flops=10**8, bytes_accessed=4 * 10**6, transcendentals=0),
        input_output_aliases=aliases or {},
        name=name,
        **options,
    )


def shaped(shape, dtype):
    return jax.ShapeDtypeStruct(shape, dtype)


def rows_of(group, count):
    return slice(group * count, group * count + count)


def iota(shape, dim):
    return lax.broadcasted_iota(jnp.int32, shape, dim)


def ones_where(condition):
    return jnp.where(condition, 1.0, 0.0)


def depth_matrix(rows):
    wide = rows.astype(F32)
    channel = iota((1, 24, 1), 1) // 6
    parts = [(wide * ones_where(channel == k)).reshape(N * 48, ZT) for k in range(4)]
    return jnp.concatenate(parts, axis=1).astype(BF)


def x_matrix(rows):
    size = rows.shape[1]
    same = ones_where(iota((1, CY, size), 1) == iota((1, CY, size), 2) % CY)
    wide = rows.reshape(KX, 1, size) * same
    return wide.reshape(KX * CY, size).astype(BF)


def lane_maps():
    row, lane = iota((ROWS, 1), 0), iota((1, 256), 1)
    inner = row % 24
    start = (row // 24) % 2 * 128 + row // 48 * 24
    real = inner % 6 < 3
    plain = ones_where(lane == start + inner)
    other = jnp.where(real, inner + 3, inner - 3)
    turned = ones_where(lane == start + other) * jnp.where(real, -1.0, 1.0)
    return plain.astype(BF), turned.astype(BF)


def spread_matrix():
    return ones_where(iota((C, C * CY), 0) == iota((C, C * CY), 1) // CY)


def to_columns(values):
    wide = values.astype(F32).reshape(CX, 4, CY, ZT)
    return jnp.concatenate([wide[:, k].reshape(CX * CY, ZT) for k in range(4)], axis=1)


def to_cells(columns):
    parts = [columns[:, k * ZT : (k + 1) * ZT].reshape(CX, CY, ZT) for k in range(4)]
    return jnp.stack(parts, axis=1).reshape(CX, 4 * CY, ZT)


def wide_to_columns(wide):
    def channel(k):
        rows = wide[k * CY : k * CY + CY]
        return jnp.concatenate([rows[:, x * ZT : x * ZT + ZT] for x in range(CX)], axis=0)

    return jnp.concatenate([channel(k) for k in range(4)], axis=1)


def wide_to_cells(wide):
    return jnp.stack([wide[:, x * ZT : x * ZT + ZT] for x in range(CX)], axis=0)


def put_spectra(matrix, columns, first, out):
    spectra = dot(matrix, jnp.concatenate(columns, axis=0), 1, 1).astype(BF)
    for k in range(len(columns)):
        spectrum = spectra[:, k * 128 : k * 128 + 128].reshape(N, 48, 128)
        out[:, rows_of(first + k, 48), :] = spectrum


BATCHES = ((0, 1), (2, 3), (4,))


def spectrum_kernel(field, depth, out):
    matrix = depth_matrix(depth[...])
    for batch in BATCHES:
        columns = [to_columns(field[:, rows_of(g, 32), :]).astype(BF) for g in batch]
        put_spectra(matrix, columns, batch[0], out)


def from_spectra(lines, matrix):
    rows = [lines[:, rows_of(g, 48), :].reshape(N * 48, 128) for g in range(GROUPS)]
    return dot(jnp.concatenate(rows, axis=1), matrix, 0, 0)


def split_dot(left, right):
    high = left.astype(BF)
    low = (left - high.astype(F32)).astype(BF)
    return dot(high, right) + dot(low, right)


def x_analysis_kernel(lines, table, out):
    plain, turned = lane_maps()
    rows = jnp.concatenate([lines[a] for a in range(N)], axis=1)
    table = table[...].astype(F32)
    matrix = jnp.concatenate([x_matrix(table[:KX]), x_matrix(table[KX:])], axis=0)
    both = dot(matrix, rows, 1, 1)
    half = KX * CY
    coef = split_dot(both[:half], plain) + split_dot(both[half:], turned)
    units = [coef[:, k * 128 : k * 128 + 128].reshape(KX, CY, 128) for k in range(2)]
    out[...] = jnp.stack(units, axis=1).reshape(N, 24, 128).astype(BF)


def x_modes(modes):
    plain, turned = lane_maps()
    units = modes.reshape(KX, 2, CY, 128)
    flat = jnp.concatenate([units[:, k].reshape(KX * CY, 128) for k in range(2)], axis=1)
    flat = flat.astype(BF)
    return dot(plain, flat, 1, 1).astype(BF), dot(turned, flat, 1, 1).astype(BF)


def x_lines(first, second, table):
    table = table.astype(F32)
    lines = dot(first, x_matrix(table[:KX])) + dot(second, x_matrix(table[KX:]))
    return lines.astype(BF)


def x_synthesis_kernel(modes, table, out):
    first, second = x_modes(modes[...].astype(F32))
    lines = x_lines(first, second, table[...])
    for a in range(N):
        out[a] = lines[:, a * 128 : a * 128 + 128]


def when_core(core):
    return pl.when(lax.axis_index("gy") % 2 == core)


def start_weight_gradient(core, coef, dual, made, target, semaphore):
    @when_core(core)
    def _():
        for channel in range(C):
            weight_gradient(coef, dual, channel, made)
        pltpu.make_async_copy(made, target, semaphore).start()


def end_weight_gradient(core, made, target, semaphore):
    @when_core(core)
    def _():
        pltpu.make_async_copy(made, target, semaphore).wait()


def x_synthesis_sums_kernel(modes, table, coef, dual, out, weight_to, made, semaphore):
    start_weight_gradient(FIRST, coef, dual, made, weight_to, semaphore)
    wide = modes[...].astype(F32)
    first, second = x_modes(wide[:, :24])
    lines = x_lines(first, second, table[...])
    sums = jnp.sum(wide[:, 24:], axis=0)
    block = pack_sums(sums[:4] + sums[4:])
    tail = jnp.concatenate([block, jnp.zeros_like(block)], axis=0).astype(BF)
    for a in range(N):
        out[a, :ROWS] = lines[:, a * 128 : a * 128 + 128]
        out[a, ROWS:] = tail
    end_weight_gradient(FIRST, made, weight_to, semaphore)


def pack_sums(values):
    high = values.astype(BF).astype(F32)
    return jnp.concatenate([high, values - high], axis=0)


def turn_lanes(values, sign):
    part = iota(values.shape, 1) % 6
    ahead = pltpu.roll(values, 125, 1)
    behind = pltpu.roll(values, 3, 1)
    return jnp.where(part < 3, sign * ahead, -sign * behind)


def y_analysis(lines, table, picks):
    wide = lines.astype(F32).reshape(N, 3, CY, 128)
    wide = jnp.concatenate([wide[:, u].reshape(NY, 128) for u in range(3)], axis=1)
    both = dot(table, wide.astype(BF))
    result = []
    for u in range(3):
        piece = both[:, u * 128 : u * 128 + 128]
        coef = piece[:KY] + turn_lanes(piece[KY:], 1.0)
        result.append(dot(picks, coef.astype(BF), 1, 1))
    return result


def y_synthesis(units, table, picks):
    columns = []
    for unit in units:
        modes = dot(unit.astype(BF), picks, 0, 0)
        columns.append(jnp.concatenate([modes, turn_lanes(modes, -1.0)], axis=0))
    columns = jnp.concatenate(columns, axis=1).astype(BF)
    lines = dot(table, columns, 0, 0)
    lines = [lines[:, u * 128 : u * 128 + 128].reshape(N, CY, 128) for u in range(3)]
    return jnp.stack(lines, axis=1).reshape(N, 24, 128)


def line_of(modes, unit, kind, channel):
    return modes[unit, pl.ds(kind * 24 + channel, 1), :]


FIVE = 5
STEP = C // FIVE


def beside(pieces):
    empty = jnp.zeros((pieces[0].shape[0], 128 - FIVE * KY), F32)
    return jnp.concatenate(list(pieces) + [empty], axis=1)


def piece_of(values, q):
    return (pltpu.roll(values, 128 - q * KY, 1) if q > 0 else values)[:, :KY]


def pack_weights(weights, packed):
    size = WEIGHTS // C
    for half in range(2):
        wide = weights[half * (WEIGHTS // 2) : (half + 1) * (WEIGHTS // 2), :].astype(F32)
        for group in range(STEP // 2):
            base = group * FIVE * size
            rows = [wide[base + q * size : base + q * size + size] for q in range(FIVE)]
            start = (half * (STEP // 2) + group) * size
            packed[start : start + size, :] = beside(rows)


def mix_forward(packed, modes, lanes):
    size = WEIGHTS // C
    empty = jnp.zeros((4, KY), F32)
    units = []
    for unit in range(3):
        for kind in range(6):
            starts = [kind * 24 + q for q in range(FIVE)]
            rows = [modes[unit, pl.ds(start, STEP, stride=FIVE), :] for start in starts]
            lanes[unit, kind * 8 : kind * 8 + STEP, :] = beside(rows)
        parts = [[], []]
        for mode in range(3):
            real = jnp.zeros((C, 128), F32)
            imag = jnp.zeros((C, 128), F32)
            for group in range(STEP):
                start = group * size + 2 * (unit * 3 + mode)
                weight_re = packed[pl.ds(start, C, stride=2 * PAIRS), :]
                weight_im = packed[pl.ds(start + 1, C, stride=2 * PAIRS), :]
                re = lanes[unit, pl.ds(mode * 8 + group, 1), :]
                im = lanes[unit, pl.ds((3 + mode) * 8 + group, 1), :]
                real = real + (weight_re * re - weight_im * im)
                imag = imag + (weight_re * im + weight_im * re)
            for part, total in enumerate((real, imag)):
                pieces = [piece_of(total, q) for q in range(FIVE)]
                parts[part] += [sum(pieces[1:], pieces[0]), empty]
        units.append(jnp.concatenate(parts[0] + parts[1], axis=0))
    return units


def mix_back(packed, modes, lanes, result):
    size = WEIGHTS // C
    result[...] = jnp.zeros(result.shape, F32)
    units = []
    for unit in range(3):
        lanes[unit] = beside([modes[unit]] * FIVE)
        for mode in range(3):
            real = jnp.zeros((STEP, 128), F32)
            imag = jnp.zeros((STEP, 128), F32)
            for k in range(C):
                start = k * 2 * PAIRS + 2 * (unit * 3 + mode)
                weight_re = packed[pl.ds(start, STEP, stride=size), :]
                weight_im = packed[pl.ds(start + 1, STEP, stride=size), :]
                re = lanes[unit, pl.ds(mode * 24 + k, 1), :]
                im = lanes[unit, pl.ds((3 + mode) * 24 + k, 1), :]
                real = real + (weight_re * re + weight_im * im)
                imag = imag + (weight_re * im - weight_im * re)
            for part, total in enumerate((real, imag)):
                for q in range(FIVE):
                    rows = pl.ds((part * 3 + mode) * 24 + q, STEP, stride=FIVE)
                    result[unit, rows, :] = piece_of(total, q)
        units.append(result[unit])
    return units


def product_kernel(lines, weights, tables, out, coef, packed, lanes):
    pack_weights(weights, packed)
    for u, unit in enumerate(y_analysis(lines[...], tables[Y_IN], tables[PICKS])):
        coef[u] = unit
    product = mix_forward(packed, coef, lanes)
    out[...] = y_synthesis(product, tables[Y_MID], tables[PICKS]).astype(BF)


def back_kernel(lines, packed, sums, tables, out, dual, lanes, result):
    for u, unit in enumerate(y_analysis(lines[...], tables[Y_MID], tables[PICKS])):
        dual[u] = unit
    modes = mix_back(packed, dual, lanes, result)
    modes = y_synthesis(modes, tables[Y_IN], tables[PICKS])
    tail = jnp.broadcast_to(sums[...].reshape(1, 8, 128), (N, 8, 128))
    out[...] = jnp.concatenate([modes, tail], axis=1).astype(BF)


def weight_gradient(coef, dual, channel, out):
    for pair in range(PAIRS):
        unit, mode = divmod(pair, 3)
        dual_re = dual[unit, mode * 24 : mode * 24 + C, :]
        dual_im = dual[unit, (3 + mode) * 24 : (3 + mode) * 24 + C, :]
        re = line_of(coef, unit, mode, channel)
        im = line_of(coef, unit, 3 + mode, channel)
        start = channel * 2 * PAIRS * C + 2 * pair
        out[pl.ds(start, C, stride=2 * PAIRS), :] = re * dual_re + im * dual_im
        out[pl.ds(start + 1, C, stride=2 * PAIRS), :] = re * dual_im - im * dual_re


def same_cell(size):
    return ones_where(iota((size, 1), 0) % CY == iota((1, size), 1) % CY)


def spread_map(weight, weight_dim):
    spread = spread_matrix().astype(BF)
    tall = dot(spread, weight, 0, weight_dim).astype(BF)
    return (dot(tall, spread) * same_cell(C * CY)).astype(BF)


def flat_cells(values):
    return jnp.concatenate([values[x] for x in range(CX)], axis=1)


def pack_lines(cross, bias):
    picks = spread_matrix()
    exact = lax.Precision.HIGHEST
    point = dot(dot(picks, cross * same_cell(C * CY), 1, 0, exact), picks, 1, 1, exact)
    total = dot(bias, picks, 1, 1, exact)[:1]
    rows = jnp.concatenate([point, total], axis=0)
    rows = jnp.concatenate([rows, jnp.zeros((C + 1, 128 - C), F32)], axis=1)
    packed = []
    for r in range(4):
        line = jnp.zeros((1, 128), F32)
        for q in range(6):
            if r * 6 + q <= C:
                row = rows[r * 6 + q : r * 6 + q + 1]
                line = line + (pltpu.roll(row, q * C, 1) if q > 0 else row)
        packed.append(line)
    return jnp.concatenate(packed, axis=0)


def cells_kernel(
    lines, depth, field, cotangent, weight, bias, out, sums, slope_out, field_out
):
    matrix = depth_matrix(depth[...])
    mixing = spread_map(weight[...], 1)
    shift = dot(spread_matrix(), bias[...], 0, 1, lax.Precision.HIGHEST)
    fields = flat_cells(field)
    spectral = from_spectra(lines, matrix)
    pointwise = dot(mixing, fields) + shift
    slopes = []
    for batch in BATCHES:
        columns = []
        for group in batch:
            span = rows_of(group, 32)
            pre = spectral[rows_of(group, 128)] + wide_to_columns(pointwise[span])
            phi = 0.5 * (1.0 + lax.erf(pre * 0.7071067811865476))
            field_out[:, span, :] = to_cells(pre * phi).astype(BF)
            slope = phi + pre * jnp.exp(-0.5 * pre * pre) * 0.3989422804014327
            slope = slope * to_columns(cotangent[:, span, :])
            columns.append(slope.astype(BF))
            slope = to_cells(slope).astype(BF)
            slope_out[:, span, :] = slope
            slopes.append(flat_cells(slope))
        put_spectra(matrix, columns, batch[0], out)
    slopes = jnp.concatenate(slopes, axis=0)
    cross = dot(fields, slopes, 1, 1)
    total = dot(jnp.ones((8, CX * ZT), BF), slopes, 1, 1)
    sums[...] = pack_sums(pack_lines(cross, total))


def last_kernel(
    lines,
    depth,
    slope,
    weight,
    coef,
    dual,
    _,
    point_out,
    bias_out,
    field_out,
    weight_to,
    made,
    semaphore,
):
    start_weight_gradient(1 - FIRST, coef, dual, made, weight_to, semaphore)
    tails = jnp.sum(lines[:, ROWS:, :].astype(F32), axis=0)
    sums = (tails[:4] + tails[4:8]) * (NX * NY * ZT) ** -0.5
    for r in range(4):
        for q in range(6):
            index = r * 6 + q
            if index <= C:
                row = sums[r : r + 1]
                row = pltpu.roll(row, 128 - q * C, 1) if q > 0 else row
                if index < C:
                    point_out[index : index + 1, :] = row[:, :C]
                else:
                    bias_out[...] = row[:, :C]
    pointwise = dot(spread_map(weight[...], 0), flat_cells(slope))
    spectral = from_spectra(lines, depth_matrix(depth[...]))
    for group in range(GROUPS):
        span = rows_of(group, 32)
        total = to_cells(spectral[rows_of(group, 128)]) + wide_to_cells(pointwise[span])
        field_out[:, span, :] = total.astype(BF)
    end_weight_gradient(1 - FIRST, made, weight_to, semaphore)


def exchange(values, axis):
    return lax.all_to_all(values, axis, split_axis=0, concat_axis=0, tiled=True)


def body(field_in, point_weight, point_bias, spec_weight, out_cotangent):
    cells = (CX, C * CY, ZT)
    line_message = shaped((N, ROWS, 128), BF)
    mode_message = shaped((N, 24, 128), BF)
    mode_lines = shaped((3, 144, KY), F32)
    wide_weights = pltpu.VMEM((WEIGHTS, KY), F32)
    field = field_in.transpose(0, 2, 1, 3).reshape(cells)
    cotangent = out_cotangent.transpose(0, 2, 1, 3).reshape(cells)
    weights = spec_weight.transpose(1, 2, 4, 3, 0).reshape(WEIGHTS, KY)

    message = call(spectrum_kernel, line_message, name="spectrum")(field, DEPTH_IN)
    message = exchange(message, "gx")
    message = call(x_analysis_kernel, mode_message, name="x_analysis")(message, X_IN)
    message = exchange(message, "gy")
    message, coef, packed = call(
        product_kernel,
        (mode_message, mode_lines, shaped((WEIGHTS // FIVE, 128), F32)),
        [pltpu.VMEM((3, 48, 128), F32)],
        "product",
    )(message, weights, Y_ALL)
    message = exchange(message, "gy")
    message = call(x_synthesis_kernel, line_message, name="x_synthesis")(message, X_MID)
    message = exchange(message, "gx")
    message, sums, slope, output_field = call(
        cells_kernel,
        (line_message, shaped((8, 128), F32), shaped(cells, BF), shaped(cells, BF)),
        name="cells",
    )(message, DEPTH_MID, field, cotangent, point_weight, point_bias.reshape(1, C))
    message = exchange(message, "gx")
    message = call(x_analysis_kernel, mode_message, name="x_analysis_back")(message, X_MID)
    message = exchange(message, "gy")
    message, dual = call(
        back_kernel,
        (shaped((N, 32, 128), BF), mode_lines),
        [pltpu.VMEM((3, 144, 128), F32), pltpu.VMEM((3, 144, KY), F32)],
        "back",
    )(message, packed, sums, Y_ALL)
    message = exchange(message, "gy")
    made = [wide_weights, pltpu.SemaphoreType.DMA(())]
    weight_shape = shaped((WEIGHTS, KY), F32)
    message, weight_grad = call(
        x_synthesis_sums_kernel,
        (shaped((N, 256, 128), BF), weight_shape),
        made,
        "x_synthesis_back",
        [pltpu.VMEM] * 4,
        [pltpu.VMEM, pl.ANY],
    )(message, X_IN, coef, dual)
    message = exchange(message, "gx")
    grad_point, grad_bias, grad_in, weight_grad = call(
        last_kernel,
        (shaped((C, C), F32), shaped((1, C), F32), shaped(cells, BF), weight_shape),
        made,
        "last",
        [pltpu.VMEM] * 6 + [pl.ANY],
        [pltpu.VMEM] * 3 + [pl.ANY],
        {6: 3},
    )(message, DEPTH_IN, slope, point_weight, coef, dual, weight_grad)
    grad_spec = weight_grad.reshape(C, C, PAIRS, 2, KY).transpose(4, 0, 1, 3, 2)

    def natural(values):
        return values.reshape(CX, C, CY, ZT).transpose(0, 2, 1, 3)

    return natural(output_field), natural(grad_in), grad_spec, grad_point, grad_bias.reshape(C)


def solution(mesh):
    return jax.shard_map(
        body,
        mesh=mesh,
        in_specs=(
            P("gx", "gy", None, None),
            P(),
            P(),
            P(None, None, None, None, ("gx", "gy")),
            P("gx", "gy", None, None),
        ),
        out_specs=(
            P("gx", "gy", None, None),
            P("gx", "gy", None, None),
            P(None, None, None, None, ("gx", "gy")),
            P(),
            P(),
        ),
        check_vma=False,
    )
```

```python
import math

import jax
import jax.numpy as jnp
import ml_dtypes
import numpy as np
from jax import lax
from jax.experimental import pallas as pl
from jax.experimental.pallas import tpu as pltpu
from jax.sharding import PartitionSpec as P

C = 20
Z = 32
T_SIZE = 4
KX = 24
KY = 24
KZ = 24
KT = 4
NX = 256
NY = 128
ZT = 128
M = 96
N = 16
CX = NX // N
CY = NY // N
ROWS = 12 * C
GROUPS = C // 4
PAIRS = 9
WEIGHTS = C * C * PAIRS * 2
FIRST = 0

BF = jnp.bfloat16
F32 = jnp.float32


def centered(count):
    return (np.arange(count) + count // 2) % count - count // 2


def rounded(table):
    return np.asarray(table, np.float32).astype(ml_dtypes.bfloat16)


def line_table(modes, length, scale):
    turns = centered(modes)[:, None] * np.arange(length)[None, :] % length
    angle = turns.astype(np.float32) * np.float32(2.0 * math.pi / length)
    scale = np.float32(scale)
    return rounded(np.cos(angle) * scale), rounded(np.sin(angle) * scale)


def depth_table(scale):
    cells = np.arange(ZT)
    turn_z = centered(KZ)[:, None] * (cells // T_SIZE)[None, :] % Z
    turn_t = centered(KT)[:, None] * (cells % T_SIZE)[None, :] % T_SIZE
    angle = turn_z.astype(np.float32)[:, None, :] * np.float32(2.0 * math.pi / Z)
    angle = angle + turn_t.astype(np.float32)[None, :, :] * np.float32(2.0 * math.pi / T_SIZE)
    angle = angle.reshape(M, ZT)
    return rounded(np.stack([np.cos(angle), -np.sin(angle)]) * np.float32(scale))


def depth_rows(scale):
    table = depth_table(scale).reshape(2, N, 2, 3, ZT).transpose(1, 2, 0, 3, 4)
    table = np.broadcast_to(table[:, :, None], (N, 2, 4, 2, 3, ZT))
    return np.ascontiguousarray(table).reshape(2 * N, 24, ZT)


def x_rows(scale):
    table = np.concatenate(line_table(KX, NX, scale), axis=0)
    return np.ascontiguousarray(np.repeat(table, CY, axis=1))


def y_rows(scale):
    return np.concatenate(line_table(KY, NY, scale), axis=0)


def lane_picks():
    rows, lanes = np.arange(6 * 24)[:, None], np.arange(128)[None, :]
    return rounded((lanes == rows % 24 * 6 + rows // 24) & (rows % 24 < C))


DEPTH_IN = depth_rows(ZT**-0.5)
DEPTH_MID = depth_rows(M**-0.5)
X_IN = x_rows(NX**-0.5)
X_MID = x_rows(KX**-0.5)
Y_ALL = np.concatenate([y_rows(NY**-0.5), y_rows(KY**-0.5), lane_picks()], axis=0)
Y_IN = slice(0, 48)
Y_MID = slice(48, 96)
PICKS = slice(96, 96 + 144)


def dot(left, right, left_dim=1, right_dim=0, precision=None):
    return lax.dot_general(
        left,
        right,
        (((left_dim,), (right_dim,)), ((), ())),
        precision=precision,
        preferred_element_type=F32,
    )


def call(kernel, out_shape, scratch=(), name=None, spaces=None, out_spaces=None, aliases=None):
    options = {}
    if spaces is not None:
        options["in_specs"] = [pl.BlockSpec(memory_space=space) for space in spaces]
        options["out_specs"] = [pl.BlockSpec(memory_space=space) for space in out_spaces]
    return pl.pallas_call(
        kernel,
        out_shape=out_shape,
        scratch_shapes=scratch,
        compiler_params=pltpu.CompilerParams(vmem_limit_bytes=24 * 2**20),
        cost_estimate=pl.CostEstimate(flops=10**8, bytes_accessed=4 * 10**6, transcendentals=0),
        input_output_aliases=aliases or {},
        name=name,
        **options,
    )


def shaped(shape, dtype):
    return jax.ShapeDtypeStruct(shape, dtype)


def rows_of(group, count):
    return slice(group * count, group * count + count)


def iota(shape, dim):
    return lax.broadcasted_iota(jnp.int32, shape, dim)


def ones_where(condition):
    return jnp.where(condition, 1.0, 0.0)


def depth_matrix(rows):
    wide = rows.astype(F32)
    channel = iota((1, 24, 1), 1) // 6
    parts = [(wide * ones_where(channel == k)).reshape(N * 48, ZT) for k in range(4)]
    return jnp.concatenate(parts, axis=1).astype(BF)


def x_matrix(rows):
    size = rows.shape[1]
    same = ones_where(iota((1, CY, size), 1) == iota((1, CY, size), 2) % CY)
    wide = rows.reshape(KX, 1, size) * same
    return wide.reshape(KX * CY, size).astype(BF)


def lane_maps():
    row, lane = iota((ROWS, 1), 0), iota((1, 256), 1)
    inner = row % 24
    start = (row // 24) % 2 * 128 + row // 48 * 24
    real = inner % 6 < 3
    plain = ones_where(lane == start + inner)
    other = jnp.where(real, inner + 3, inner - 3)
    turned = ones_where(lane == start + other) * jnp.where(real, -1.0, 1.0)
    return plain.astype(BF), turned.astype(BF)


def spread_matrix():
    return ones_where(iota((C, C * CY), 0) == iota((C, C * CY), 1) // CY)


def to_columns(values):
    wide = values.astype(F32).reshape(CX, 4, CY, ZT)
    return jnp.concatenate([wide[:, k].reshape(CX * CY, ZT) for k in range(4)], axis=1)


def to_cells(columns):
    parts = [columns[:, k * ZT : (k + 1) * ZT].reshape(CX, CY, ZT) for k in range(4)]
    return jnp.stack(parts, axis=1).reshape(CX, 4 * CY, ZT)


def wide_to_columns(wide):
    def channel(k):
        rows = wide[k * CY : k * CY + CY]
        return jnp.concatenate([rows[:, x * ZT : x * ZT + ZT] for x in range(CX)], axis=0)

    return jnp.concatenate([channel(k) for k in range(4)], axis=1)


def wide_to_cells(wide):
    return jnp.stack([wide[:, x * ZT : x * ZT + ZT] for x in range(CX)], axis=0)


def put_spectra(matrix, columns, first, out):
    spectra = dot(matrix, jnp.concatenate(columns, axis=0), 1, 1).astype(BF)
    for k in range(len(columns)):
        spectrum = spectra[:, k * 128 : k * 128 + 128].reshape(N, 48, 128)
        out[:, rows_of(first + k, 48), :] = spectrum


BATCHES = ((0, 1), (2, 3), (4,))


def depth_rows_here(scale):
    row, lane = iota((24, 1), 0), iota((1, ZT), 1)
    mode = row % 3
    quarter = jnp.where(row % 6 < 3, 0.0, 8.0)
    z, t = (lane // T_SIZE).astype(F32), (lane % T_SIZE).astype(F32)
    blocks = []
    for block in range(2 * N):
        jz, jt = divmod(3 * block, KT)
        carry = mode + jt >= KT
        jt = jnp.where(carry, mode + jt - KT, mode + jt)
        jz = jnp.where(carry, jz + 1, jz)
        fz = jnp.where(jz < KZ // 2, jz, jz + Z - KZ).astype(F32)
        turns = fz * z + (jt * (Z // KT)).astype(F32) * t + quarter
        turns = turns - 32.0 * jnp.floor(turns * (1.0 / 32.0))
        angle = (jnp.abs(turns * 0.0625 - 1.0) - 0.5) * math.pi
        square = angle * angle
        wave = 1.0 + square * (-1.0 / 110.0)
        for factor in (72.0, 42.0, 20.0, 6.0):
            wave = 1.0 - square * (1.0 / factor) * wave
        blocks.append(angle * wave * scale)
    return jnp.stack(blocks, axis=0)


def spectrum_kernel(field, out):
    matrix = depth_matrix(depth_rows_here(ZT**-0.5))
    for batch in BATCHES:
        columns = [to_columns(field[:, rows_of(g, 32), :]).astype(BF) for g in batch]
        put_spectra(matrix, columns, batch[0], out)


def from_spectra(lines, matrix):
    rows = [lines[:, rows_of(g, 48), :].reshape(N * 48, 128) for g in range(GROUPS)]
    return dot(jnp.concatenate(rows, axis=1), matrix, 0, 0)


def split_dot(left, right):
    high = left.astype(BF)
    low = (left - high.astype(F32)).astype(BF)
    return dot(high, right) + dot(low, right)


def x_analysis_kernel(lines, table, out):
    plain, turned = lane_maps()
    rows = jnp.concatenate([lines[a] for a in range(N)], axis=1)
    table = table[...].astype(F32)
    matrix = jnp.concatenate([x_matrix(table[:KX]), x_matrix(table[KX:])], axis=0)
    both = dot(matrix, rows, 1, 1)
    half = KX * CY
    coef = split_dot(both[:half], plain) + split_dot(both[half:], turned)
    units = [coef[:, k * 128 : k * 128 + 128].reshape(KX, CY, 128) for k in range(2)]
    out[...] = jnp.stack(units, axis=1).reshape(N, 24, 128).astype(BF)


def x_modes(modes):
    plain, turned = lane_maps()
    units = modes.reshape(KX, 2, CY, 128)
    flat = jnp.concatenate([units[:, k].reshape(KX * CY, 128) for k in range(2)], axis=1)
    flat = flat.astype(BF)
    return dot(plain, flat, 1, 1).astype(BF), dot(turned, flat, 1, 1).astype(BF)


def x_lines(first, second, table):
    table = table.astype(F32)
    lines = dot(first, x_matrix(table[:KX])) + dot(second, x_matrix(table[KX:]))
    return lines.astype(BF)


def x_synthesis_kernel(modes, table, out):
    first, second = x_modes(modes[...].astype(F32))
    lines = x_lines(first, second, table[...])
    for a in range(N):
        out[a] = lines[:, a * 128 : a * 128 + 128]


def when_core(core):
    return pl.when(lax.axis_index("gy") % 2 == core)


def start_weight_gradient(core, coef, dual, made, target, semaphore):
    @when_core(core)
    def _():
        for channel in range(C):
            weight_gradient(coef, dual, channel, made)
        pltpu.make_async_copy(made, target, semaphore).start()


def end_weight_gradient(core, made, target, semaphore):
    @when_core(core)
    def _():
        pltpu.make_async_copy(made, target, semaphore).wait()


def x_synthesis_sums_kernel(modes, table, coef, dual, out, weight_to, made, semaphore):
    start_weight_gradient(FIRST, coef, dual, made, weight_to, semaphore)
    wide = modes[...].astype(F32)
    first, second = x_modes(wide[:, :24])
    lines = x_lines(first, second, table[...])
    sums = jnp.sum(wide[:, 24:], axis=0)
    block = pack_sums(sums[:4] + sums[4:])
    tail = jnp.concatenate([block, jnp.zeros_like(block)], axis=0).astype(BF)
    for a in range(N):
        out[a, :ROWS] = lines[:, a * 128 : a * 128 + 128]
        out[a, ROWS:] = tail
    end_weight_gradient(FIRST, made, weight_to, semaphore)


def pack_sums(values):
    high = values.astype(BF).astype(F32)
    return jnp.concatenate([high, values - high], axis=0)


def turn_lanes(values, sign):
    part = iota(values.shape, 1) % 6
    ahead = pltpu.roll(values, 125, 1)
    behind = pltpu.roll(values, 3, 1)
    return jnp.where(part < 3, sign * ahead, -sign * behind)


def y_analysis(lines, table, picks):
    wide = lines.astype(F32).reshape(N, 3, CY, 128)
    wide = jnp.concatenate([wide[:, u].reshape(NY, 128) for u in range(3)], axis=1)
    both = dot(table, wide.astype(BF))
    result = []
    for u in range(3):
        piece = both[:, u * 128 : u * 128 + 128]
        coef = piece[:KY] + turn_lanes(piece[KY:], 1.0)
        result.append(dot(picks, coef.astype(BF), 1, 1))
    return result


def y_synthesis(units, table, picks):
    columns = []
    for unit in units:
        modes = dot(unit.astype(BF), picks, 0, 0)
        columns.append(jnp.concatenate([modes, turn_lanes(modes, -1.0)], axis=0))
    columns = jnp.concatenate(columns, axis=1).astype(BF)
    lines = dot(table, columns, 0, 0)
    lines = [lines[:, u * 128 : u * 128 + 128].reshape(N, CY, 128) for u in range(3)]
    return jnp.stack(lines, axis=1).reshape(N, 24, 128)


def line_of(modes, unit, kind, channel):
    return modes[unit, pl.ds(kind * 24 + channel, 1), :]


FIVE = 5
STEP = C // FIVE


def beside(pieces):
    empty = jnp.zeros((pieces[0].shape[0], 128 - FIVE * KY), F32)
    return jnp.concatenate(list(pieces) + [empty], axis=1)


def piece_of(values, q):
    return (pltpu.roll(values, 128 - q * KY, 1) if q > 0 else values)[:, :KY]


def pack_weights(weights, packed):
    size = WEIGHTS // C
    for half in range(2):
        wide = weights[half * (WEIGHTS // 2) : (half + 1) * (WEIGHTS // 2), :].astype(F32)
        for group in range(STEP // 2):
            base = group * FIVE * size
            rows = [wide[base + q * size : base + q * size + size] for q in range(FIVE)]
            start = (half * (STEP // 2) + group) * size
            packed[start : start + size, :] = beside(rows)


def mix_forward(packed, modes, lanes):
    size = WEIGHTS // C
    empty = jnp.zeros((4, KY), F32)
    units = []
    for unit in range(3):
        for kind in range(6):
            starts = [kind * 24 + q for q in range(FIVE)]
            rows = [modes[unit, pl.ds(start, STEP, stride=FIVE), :] for start in starts]
            lanes[unit, kind * 8 : kind * 8 + STEP, :] = beside(rows)
        parts = [[], []]
        for mode in range(3):
            real = jnp.zeros((C, 128), F32)
            imag = jnp.zeros((C, 128), F32)
            for group in range(STEP):
                start = group * size + 2 * (unit * 3 + mode)
                weight_re = packed[pl.ds(start, C, stride=2 * PAIRS), :]
                weight_im = packed[pl.ds(start + 1, C, stride=2 * PAIRS), :]
                re = lanes[unit, pl.ds(mode * 8 + group, 1), :]
                im = lanes[unit, pl.ds((3 + mode) * 8 + group, 1), :]
                real = real + (weight_re * re - weight_im * im)
                imag = imag + (weight_re * im + weight_im * re)
            for part, total in enumerate((real, imag)):
                pieces = [piece_of(total, q) for q in range(FIVE)]
                parts[part] += [sum(pieces[1:], pieces[0]), empty]
        units.append(jnp.concatenate(parts[0] + parts[1], axis=0))
    return units


def mix_back(packed, modes, lanes, result):
    size = WEIGHTS // C
    result[...] = jnp.zeros(result.shape, F32)
    units = []
    for unit in range(3):
        lanes[unit] = beside([modes[unit]] * FIVE)
        for mode in range(3):
            real = jnp.zeros((STEP, 128), F32)
            imag = jnp.zeros((STEP, 128), F32)
            for k in range(C):
                start = k * 2 * PAIRS + 2 * (unit * 3 + mode)
                weight_re = packed[pl.ds(start, STEP, stride=size), :]
                weight_im = packed[pl.ds(start + 1, STEP, stride=size), :]
                re = lanes[unit, pl.ds(mode * 24 + k, 1), :]
                im = lanes[unit, pl.ds((3 + mode) * 24 + k, 1), :]
                real = real + (weight_re * re + weight_im * im)
                imag = imag + (weight_re * im - weight_im * re)
            for part, total in enumerate((real, imag)):
                for q in range(FIVE):
                    rows = pl.ds((part * 3 + mode) * 24 + q, STEP, stride=FIVE)
                    result[unit, rows, :] = piece_of(total, q)
        units.append(result[unit])
    return units


def product_kernel(lines, weights, tables, out, coef, packed, lanes):
    pack_weights(weights, packed)
    for u, unit in enumerate(y_analysis(lines[...], tables[Y_IN], tables[PICKS])):
        coef[u] = unit
    product = mix_forward(packed, coef, lanes)
    out[...] = y_synthesis(product, tables[Y_MID], tables[PICKS]).astype(BF)


def back_kernel(lines, packed, sums, tables, out, dual, lanes, result):
    for u, unit in enumerate(y_analysis(lines[...], tables[Y_MID], tables[PICKS])):
        dual[u] = unit
    modes = mix_back(packed, dual, lanes, result)
    modes = y_synthesis(modes, tables[Y_IN], tables[PICKS])
    tail = jnp.broadcast_to(sums[...].reshape(1, 8, 128), (N, 8, 128))
    out[...] = jnp.concatenate([modes, tail], axis=1).astype(BF)


def weight_gradient(coef, dual, channel, out):
    for pair in range(PAIRS):
        unit, mode = divmod(pair, 3)
        dual_re = dual[unit, mode * 24 : mode * 24 + C, :]
        dual_im = dual[unit, (3 + mode) * 24 : (3 + mode) * 24 + C, :]
        re = line_of(coef, unit, mode, channel)
        im = line_of(coef, unit, 3 + mode, channel)
        start = channel * 2 * PAIRS * C + 2 * pair
        out[pl.ds(start, C, stride=2 * PAIRS), :] = re * dual_re + im * dual_im
        out[pl.ds(start + 1, C, stride=2 * PAIRS), :] = re * dual_im - im * dual_re


def same_cell(size):
    return ones_where(iota((size, 1), 0) % CY == iota((1, size), 1) % CY)


def spread_map(weight, weight_dim):
    spread = spread_matrix().astype(BF)
    tall = dot(spread, weight, 0, weight_dim).astype(BF)
    return (dot(tall, spread) * same_cell(C * CY)).astype(BF)


def flat_cells(values):
    return jnp.concatenate([values[x] for x in range(CX)], axis=1)


def pack_lines(cross, bias):
    picks = spread_matrix()
    exact = lax.Precision.HIGHEST
    point = dot(dot(picks, cross * same_cell(C * CY), 1, 0, exact), picks, 1, 1, exact)
    total = dot(bias, picks, 1, 1, exact)[:1]
    rows = jnp.concatenate([point, total], axis=0)
    rows = jnp.concatenate([rows, jnp.zeros((C + 1, 128 - C), F32)], axis=1)
    packed = []
    for r in range(4):
        line = jnp.zeros((1, 128), F32)
        for q in range(6):
            if r * 6 + q <= C:
                row = rows[r * 6 + q : r * 6 + q + 1]
                line = line + (pltpu.roll(row, q * C, 1) if q > 0 else row)
        packed.append(line)
    return jnp.concatenate(packed, axis=0)


def cells_kernel(
    lines, depth, field, cotangent, weight, bias, out, sums, slope_out, field_out
):
    matrix = depth_matrix(depth[...])
    mixing = spread_map(weight[...], 1)
    shift = dot(spread_matrix(), bias[...], 0, 1, lax.Precision.HIGHEST)
    fields = flat_cells(field)
    spectral = from_spectra(lines, matrix)
    pointwise = dot(mixing, fields) + shift
    slopes = []
    for batch in BATCHES:
        columns = []
        for group in batch:
            span = rows_of(group, 32)
            pre = spectral[rows_of(group, 128)] + wide_to_columns(pointwise[span])
            phi = 0.5 * (1.0 + lax.erf(pre * 0.7071067811865476))
            field_out[:, span, :] = to_cells(pre * phi).astype(BF)
            slope = phi + pre * jnp.exp(-0.5 * pre * pre) * 0.3989422804014327
            slope = slope * to_columns(cotangent[:, span, :])
            columns.append(slope.astype(BF))
            slope = to_cells(slope).astype(BF)
            slope_out[:, span, :] = slope
            slopes.append(flat_cells(slope))
        put_spectra(matrix, columns, batch[0], out)
    slopes = jnp.concatenate(slopes, axis=0)
    cross = dot(fields, slopes, 1, 1)
    total = dot(jnp.ones((8, CX * ZT), BF), slopes, 1, 1)
    sums[...] = pack_sums(pack_lines(cross, total))


def last_kernel(
    lines,
    depth,
    slope,
    weight,
    coef,
    dual,
    _,
    point_out,
    bias_out,
    field_out,
    weight_to,
    made,
    semaphore,
):
    start_weight_gradient(1 - FIRST, coef, dual, made, weight_to, semaphore)
    tails = jnp.sum(lines[:, ROWS:, :].astype(F32), axis=0)
    sums = (tails[:4] + tails[4:8]) * (NX * NY * ZT) ** -0.5
    for r in range(4):
        for q in range(6):
            index = r * 6 + q
            if index <= C:
                row = sums[r : r + 1]
                row = pltpu.roll(row, 128 - q * C, 1) if q > 0 else row
                if index < C:
                    point_out[index : index + 1, :] = row[:, :C]
                else:
                    bias_out[...] = row[:, :C]
    pointwise = dot(spread_map(weight[...], 0), flat_cells(slope))
    spectral = from_spectra(lines, depth_matrix(depth[...]))
    for group in range(GROUPS):
        span = rows_of(group, 32)
        total = to_cells(spectral[rows_of(group, 128)]) + wide_to_cells(pointwise[span])
        field_out[:, span, :] = total.astype(BF)
    end_weight_gradient(1 - FIRST, made, weight_to, semaphore)


def exchange(values, axis):
    return lax.all_to_all(values, axis, split_axis=0, concat_axis=0, tiled=True)


def body(field_in, point_weight, point_bias, spec_weight, out_cotangent):
    cells = (CX, C * CY, ZT)
    line_message = shaped((N, ROWS, 128), BF)
    mode_message = shaped((N, 24, 128), BF)
    mode_lines = shaped((3, 144, KY), F32)
    wide_weights = pltpu.VMEM((WEIGHTS, KY), F32)
    field = field_in.transpose(0, 2, 1, 3).reshape(cells)
    cotangent = out_cotangent.transpose(0, 2, 1, 3).reshape(cells)
    weights = spec_weight.transpose(1, 2, 4, 3, 0).reshape(WEIGHTS, KY)

    message = call(spectrum_kernel, line_message, name="spectrum")(field)
    message = exchange(message, "gx")
    message = call(x_analysis_kernel, mode_message, name="x_analysis")(message, X_IN)
    message = exchange(message, "gy")
    message, coef, packed = call(
        product_kernel,
        (mode_message, mode_lines, shaped((WEIGHTS // FIVE, 128), F32)),
        [pltpu.VMEM((3, 48, 128), F32)],
        "product",
    )(message, weights, Y_ALL)
    message = exchange(message, "gy")
    message = call(x_synthesis_kernel, line_message, name="x_synthesis")(message, X_MID)
    message = exchange(message, "gx")
    message, sums, slope, output_field = call(
        cells_kernel,
        (line_message, shaped((8, 128), F32), shaped(cells, BF), shaped(cells, BF)),
        name="cells",
    )(message, DEPTH_MID, field, cotangent, point_weight, point_bias.reshape(1, C))
    message = exchange(message, "gx")
    message = call(x_analysis_kernel, mode_message, name="x_analysis_back")(message, X_MID)
    message = exchange(message, "gy")
    message, dual = call(
        back_kernel,
        (shaped((N, 32, 128), BF), mode_lines),
        [pltpu.VMEM((3, 144, 128), F32), pltpu.VMEM((3, 144, KY), F32)],
        "back",
    )(message, packed, sums, Y_ALL)
    message = exchange(message, "gy")
    made = [wide_weights, pltpu.SemaphoreType.DMA(())]
    weight_shape = shaped((WEIGHTS, KY), F32)
    message, weight_grad = call(
        x_synthesis_sums_kernel,
        (shaped((N, 256, 128), BF), weight_shape),
        made,
        "x_synthesis_back",
        [pltpu.VMEM] * 4,
        [pltpu.VMEM, pl.ANY],
    )(message, X_IN, coef, dual)
    message = exchange(message, "gx")
    grad_point, grad_bias, grad_in, weight_grad = call(
        last_kernel,
        (shaped((C, C), F32), shaped((1, C), F32), shaped(cells, BF), weight_shape),
        made,
        "last",
        [pltpu.VMEM] * 6 + [pl.ANY],
        [pltpu.VMEM] * 3 + [pl.ANY],
        {6: 3},
    )(message, DEPTH_IN, slope, point_weight, coef, dual, weight_grad)
    grad_spec = weight_grad.reshape(C, C, PAIRS, 2, KY).transpose(4, 0, 1, 3, 2)

    def natural(values):
        return values.reshape(CX, C, CY, ZT).transpose(0, 2, 1, 3)

    return natural(output_field), natural(grad_in), grad_spec, grad_point, grad_bias.reshape(C)


def solution(mesh):
    return jax.shard_map(
        body,
        mesh=mesh,
        in_specs=(
            P("gx", "gy", None, None),
            P(),
            P(),
            P(None, None, None, None, ("gx", "gy")),
            P("gx", "gy", None, None),
        ),
        out_specs=(
            P("gx", "gy", None, None),
            P("gx", "gy", None, None),
            P(None, None, None, None, ("gx", "gy")),
            P(),
            P(),
        ),
        check_vma=False,
    )
```

```python
import math

import jax
import jax.numpy as jnp
import ml_dtypes
import numpy as np
from jax import lax
from jax.experimental import pallas as pl
from jax.experimental.pallas import tpu as pltpu
from jax.sharding import PartitionSpec as P

C = 20
Z = 32
T_SIZE = 4
KX = 24
KY = 24
KZ = 24
KT = 4
NX = 256
NY = 128
ZT = 128
M = 96
N = 16
CX = NX // N
CY = NY // N
ROWS = 12 * C
GROUPS = C // 2
PAIRS = 9
WEIGHTS = C * C * PAIRS * 2
FIRST = 0

BF = jnp.bfloat16
F32 = jnp.float32


def centered(count):
    return (np.arange(count) + count // 2) % count - count // 2


def rounded(table):
    return np.asarray(table, np.float32).astype(ml_dtypes.bfloat16)


def line_table(modes, length, scale):
    turns = centered(modes)[:, None] * np.arange(length)[None, :] % length
    angle = turns.astype(np.float32) * np.float32(2.0 * math.pi / length)
    scale = np.float32(scale)
    return rounded(np.cos(angle) * scale), rounded(np.sin(angle) * scale)


def depth_table(scale):
    cells = np.arange(ZT)
    turn_z = centered(KZ)[:, None] * (cells // T_SIZE)[None, :] % Z
    turn_t = centered(KT)[:, None] * (cells % T_SIZE)[None, :] % T_SIZE
    angle = turn_z.astype(np.float32)[:, None, :] * np.float32(2.0 * math.pi / Z)
    angle = angle + turn_t.astype(np.float32)[None, :, :] * np.float32(2.0 * math.pi / T_SIZE)
    angle = angle.reshape(M, ZT)
    return rounded(np.stack([np.cos(angle), -np.sin(angle)]) * np.float32(scale))


def depth_rows(scale):
    table = depth_table(scale).reshape(2, N, 2, 3, ZT).transpose(1, 2, 0, 3, 4)
    table = np.broadcast_to(table[:, :, None], (N, 2, 2, 2, 3, ZT))
    return np.ascontiguousarray(table).reshape(N, 24, ZT)


def x_rows(scale):
    table = np.concatenate(line_table(KX, NX, scale), axis=0)
    return np.ascontiguousarray(np.repeat(table, CY, axis=1))


def y_rows(scale):
    return np.concatenate(line_table(KY, NY, scale), axis=0)


def lane_picks():
    rows, lanes = np.arange(6 * 24)[:, None], np.arange(128)[None, :]
    return rounded((lanes == rows % 24 * 6 + rows // 24) & (rows % 24 < C))


DEPTH_IN = depth_rows(ZT**-0.5)
DEPTH_MID = depth_rows(M**-0.5)
X_IN = x_rows(NX**-0.5)
X_MID = x_rows(KX**-0.5)
Y_ALL = np.concatenate([y_rows(NY**-0.5), y_rows(KY**-0.5), lane_picks()], axis=0)
Y_IN = slice(0, 48)
Y_MID = slice(48, 96)
PICKS = slice(96, 96 + 144)


def dot(left, right, left_dim=1, right_dim=0, precision=None):
    return lax.dot_general(
        left,
        right,
        (((left_dim,), (right_dim,)), ((), ())),
        precision=precision,
        preferred_element_type=F32,
    )


def call(kernel, out_shape, scratch=(), name=None, spaces=None, out_spaces=None, aliases=None):
    options = {}
    if spaces is not None:
        options["in_specs"] = [pl.BlockSpec(memory_space=space) for space in spaces]
        options["out_specs"] = [pl.BlockSpec(memory_space=space) for space in out_spaces]
    return pl.pallas_call(
        kernel,
        out_shape=out_shape,
        scratch_shapes=scratch,
        compiler_params=pltpu.CompilerParams(vmem_limit_bytes=24 * 2**20),
        cost_estimate=pl.CostEstimate(flops=10**8, bytes_accessed=4 * 10**6, transcendentals=0),
        input_output_aliases=aliases or {},
        name=name,
        **options,
    )


def shaped(shape, dtype):
    return jax.ShapeDtypeStruct(shape, dtype)


def rows_of(group, count):
    return slice(group * count, group * count + count)


def iota(shape, dim):
    return lax.broadcasted_iota(jnp.int32, shape, dim)


def ones_where(condition):
    return jnp.where(condition, 1.0, 0.0)


def depth_matrix(rows):
    wide = rows.astype(F32)
    channel = iota((1, 24, 1), 1) // 6 % 2
    parts = [(wide * ones_where(channel == k)).reshape(N * 24, ZT) for k in range(2)]
    return jnp.concatenate(parts, axis=1).astype(BF)


def x_matrix(rows):
    size = rows.shape[1]
    same = ones_where(iota((1, CY, size), 1) == iota((1, CY, size), 2) % CY)
    wide = rows.reshape(KX, 1, size) * same
    return wide.reshape(KX * CY, size).astype(BF)


def lane_maps():
    row, lane = iota((ROWS, 1), 0), iota((1, 256), 1)
    inner = row % 12
    start = (row // 12) % 2 * 128 + row // 24 * 12
    real = inner % 6 < 3
    plain = ones_where(lane == start + inner)
    other = jnp.where(real, inner + 3, inner - 3)
    turned = ones_where(lane == start + other) * jnp.where(real, -1.0, 1.0)
    return plain.astype(BF), turned.astype(BF)


def spread_matrix():
    return ones_where(iota((C, C * CY), 0) == iota((C, C * CY), 1) // CY)


def to_columns(values):
    wide = values.astype(F32).reshape(CX, 2, CY, ZT)
    return jnp.concatenate([wide[:, k].reshape(CX * CY, ZT) for k in range(2)], axis=1)


def to_cells(columns):
    parts = [columns[:, k * ZT : (k + 1) * ZT].reshape(CX, CY, ZT) for k in range(2)]
    return jnp.stack(parts, axis=1).reshape(CX, 2 * CY, ZT)


def wide_to_columns(wide):
    def channel(k):
        rows = wide[k * CY : k * CY + CY]
        return jnp.concatenate([rows[:, x * ZT : x * ZT + ZT] for x in range(CX)], axis=0)

    return jnp.concatenate([channel(k) for k in range(2)], axis=1)


def wide_to_cells(wide):
    return jnp.stack([wide[:, x * ZT : x * ZT + ZT] for x in range(CX)], axis=0)


def put_spectra(matrix, columns, batch, out):
    spectra = dot(matrix, jnp.concatenate(columns, axis=0), 1, 1)
    parts = [spectra[:, k * 128 : k * 128 + 128].reshape(N, 24, 128) for k in range(2)]
    out[:, rows_of(batch, 48), :] = jnp.concatenate(parts, axis=1).astype(BF)


BATCHES = GROUPS // 2


def depth_rows_here(scale):
    row, lane = iota((24, 1), 0), iota((1, ZT), 1)
    mode = row // 12 * 3 + row % 3
    quarter = jnp.where(row % 6 < 3, 0.0, 8.0)
    z, t = (lane // T_SIZE).astype(F32), (lane % T_SIZE).astype(F32)
    blocks = []
    for block in range(N):
        jz, jt = divmod(6 * block, KT)
        jt = mode + jt
        jz = jz + jt // KT
        jt = jt % KT
        fz = jnp.where(jz < KZ // 2, jz, jz + Z - KZ).astype(F32)
        turns = fz * z + (jt * (Z // KT)).astype(F32) * t + quarter
        turns = turns - 32.0 * jnp.floor(turns * (1.0 / 32.0))
        angle = (jnp.abs(turns * 0.0625 - 1.0) - 0.5) * math.pi
        square = angle * angle
        wave = 1.0 + square * (-1.0 / 110.0)
        for factor in (72.0, 42.0, 20.0, 6.0):
            wave = 1.0 - square * (1.0 / factor) * wave
        blocks.append(angle * wave * scale)
    return jnp.stack(blocks, axis=0)


def spectrum_kernel(field, out):
    matrix = depth_matrix(depth_rows_here(ZT**-0.5))
    for batch in range(BATCHES):
        groups = (2 * batch, 2 * batch + 1)
        columns = [to_columns(field[:, rows_of(g, 16), :]).astype(BF) for g in groups]
        put_spectra(matrix, columns, batch, out)


def from_spectra(lines, matrix):
    rows = []
    for batch in range(BATCHES):
        wide = lines[:, rows_of(batch, 48), :].astype(F32).reshape(N, 2, 24, 128)
        rows += [wide[:, k].reshape(N * 24, 128) for k in range(2)]
    return dot(jnp.concatenate(rows, axis=1).astype(BF), matrix, 0, 0)


def split_dot(left, right):
    high = left.astype(BF)
    low = (left - high.astype(F32)).astype(BF)
    return dot(high, right) + dot(low, right)


def x_analysis_kernel(lines, table, out):
    plain, turned = lane_maps()
    rows = jnp.concatenate([lines[a] for a in range(N)], axis=1)
    table = table[...].astype(F32)
    matrix = jnp.concatenate([x_matrix(table[:KX]), x_matrix(table[KX:])], axis=0)
    both = dot(matrix, rows, 1, 1)
    half = KX * CY
    coef = split_dot(both[:half], plain) + split_dot(both[half:], turned)
    units = [coef[:, k * 128 : k * 128 + 128].reshape(KX, CY, 128) for k in range(2)]
    out[...] = jnp.stack(units, axis=1).reshape(N, 24, 128).astype(BF)


def x_modes(modes):
    plain, turned = lane_maps()
    units = modes.reshape(KX, 2, CY, 128)
    flat = jnp.concatenate([units[:, k].reshape(KX * CY, 128) for k in range(2)], axis=1)
    flat = flat.astype(BF)
    return dot(plain, flat, 1, 1).astype(BF), dot(turned, flat, 1, 1).astype(BF)


def x_lines(first, second, table):
    table = table.astype(F32)
    lines = dot(first, x_matrix(table[:KX])) + dot(second, x_matrix(table[KX:]))
    return lines.astype(BF)


def x_synthesis_kernel(modes, table, out):
    first, second = x_modes(modes[...].astype(F32))
    lines = x_lines(first, second, table[...])
    for a in range(N):
        out[a] = lines[:, a * 128 : a * 128 + 128]


def when_core(core):
    return pl.when(lax.axis_index("gy") % 2 == core)


def start_weight_gradient(core, coef, dual, made, target, semaphore):
    @when_core(core)
    def _():
        for channel in range(C):
            weight_gradient(coef, dual, channel, made)
        pltpu.make_async_copy(made, target, semaphore).start()


def end_weight_gradient(core, made, target, semaphore):
    @when_core(core)
    def _():
        pltpu.make_async_copy(made, target, semaphore).wait()


def x_synthesis_sums_kernel(modes, table, coef, dual, out, weight_to, made, semaphore):
    start_weight_gradient(FIRST, coef, dual, made, weight_to, semaphore)
    wide = modes[...].astype(F32)
    first, second = x_modes(wide[:, :24])
    lines = x_lines(first, second, table[...])
    sums = jnp.sum(wide[:, 24:], axis=0)
    block = pack_sums(sums[:4] + sums[4:])
    tail = jnp.concatenate([block, jnp.zeros_like(block)], axis=0).astype(BF)
    for a in range(N):
        out[a, :ROWS] = lines[:, a * 128 : a * 128 + 128]
        out[a, ROWS:] = tail
    end_weight_gradient(FIRST, made, weight_to, semaphore)


def pack_sums(values):
    high = values.astype(BF).astype(F32)
    return jnp.concatenate([high, values - high], axis=0)


def turn_lanes(values, sign):
    part = iota(values.shape, 1) % 6
    ahead = pltpu.roll(values, 125, 1)
    behind = pltpu.roll(values, 3, 1)
    return jnp.where(part < 3, sign * ahead, -sign * behind)


def y_analysis(lines, table, picks):
    wide = lines.astype(F32).reshape(N, 3, CY, 128)
    wide = jnp.concatenate([wide[:, u].reshape(NY, 128) for u in range(3)], axis=1)
    both = dot(table, wide.astype(BF))
    result = []
    for u in range(3):
        piece = both[:, u * 128 : u * 128 + 128]
        coef = piece[:KY] + turn_lanes(piece[KY:], 1.0)
        result.append(dot(picks, coef.astype(BF), 1, 1))
    return result


def y_synthesis(units, table, picks):
    columns = []
    for unit in units:
        modes = dot(unit.astype(BF), picks, 0, 0)
        columns.append(jnp.concatenate([modes, turn_lanes(modes, -1.0)], axis=0))
    columns = jnp.concatenate(columns, axis=1).astype(BF)
    lines = dot(table, columns, 0, 0)
    lines = [lines[:, u * 128 : u * 128 + 128].reshape(N, CY, 128) for u in range(3)]
    return jnp.stack(lines, axis=1).reshape(N, 24, 128)


def line_of(modes, unit, kind, channel):
    return modes[unit, pl.ds(kind * 24 + channel, 1), :]


FIVE = 5
STEP = C // FIVE


def beside(pieces):
    empty = jnp.zeros((pieces[0].shape[0], 128 - FIVE * KY), F32)
    return jnp.concatenate(list(pieces) + [empty], axis=1)


def piece_of(values, q):
    return (pltpu.roll(values, 128 - q * KY, 1) if q > 0 else values)[:, :KY]


def pack_weights(weights, packed):
    size = WEIGHTS // C
    for half in range(2):
        wide = weights[half * (WEIGHTS // 2) : (half + 1) * (WEIGHTS // 2), :].astype(F32)
        for group in range(STEP // 2):
            base = group * FIVE * size
            rows = [wide[base + q * size : base + q * size + size] for q in range(FIVE)]
            start = (half * (STEP // 2) + group) * size
            packed[start : start + size, :] = beside(rows)


def mix_forward(packed, modes, lanes):
    size = WEIGHTS // C
    empty = jnp.zeros((4, KY), F32)
    units = []
    for unit in range(3):
        for kind in range(6):
            starts = [kind * 24 + q for q in range(FIVE)]
            rows = [modes[unit, pl.ds(start, STEP, stride=FIVE), :] for start in starts]
            lanes[unit, kind * 8 : kind * 8 + STEP, :] = beside(rows)
        parts = [[], []]
        for mode in range(3):
            real = jnp.zeros((C, 128), F32)
            imag = jnp.zeros((C, 128), F32)
            for group in range(STEP):
                start = group * size + 2 * (unit * 3 + mode)
                weight_re = packed[pl.ds(start, C, stride=2 * PAIRS), :]
                weight_im = packed[pl.ds(start + 1, C, stride=2 * PAIRS), :]
                re = lanes[unit, pl.ds(mode * 8 + group, 1), :]
                im = lanes[unit, pl.ds((3 + mode) * 8 + group, 1), :]
                real = real + (weight_re * re - weight_im * im)
                imag = imag + (weight_re * im + weight_im * re)
            for part, total in enumerate((real, imag)):
                pieces = [piece_of(total, q) for q in range(FIVE)]
                parts[part] += [sum(pieces[1:], pieces[0]), empty]
        units.append(jnp.concatenate(parts[0] + parts[1], axis=0))
    return units


def mix_back(packed, modes, lanes, result):
    size = WEIGHTS // C
    result[...] = jnp.zeros(result.shape, F32)
    units = []
    for unit in range(3):
        lanes[unit] = beside([modes[unit]] * FIVE)
        for mode in range(3):
            real = jnp.zeros((STEP, 128), F32)
            imag = jnp.zeros((STEP, 128), F32)
            for k in range(C):
                start = k * 2 * PAIRS + 2 * (unit * 3 + mode)
                weight_re = packed[pl.ds(start, STEP, stride=size), :]
                weight_im = packed[pl.ds(start + 1, STEP, stride=size), :]
                re = lanes[unit, pl.ds(mode * 24 + k, 1), :]
                im = lanes[unit, pl.ds((3 + mode) * 24 + k, 1), :]
                real = real + (weight_re * re + weight_im * im)
                imag = imag + (weight_re * im - weight_im * re)
            for part, total in enumerate((real, imag)):
                for q in range(FIVE):
                    rows = pl.ds((part * 3 + mode) * 24 + q, STEP, stride=FIVE)
                    result[unit, rows, :] = piece_of(total, q)
        units.append(result[unit])
    return units


def product_kernel(lines, weights, tables, out, coef, packed, lanes):
    pack_weights(weights, packed)
    for u, unit in enumerate(y_analysis(lines[...], tables[Y_IN], tables[PICKS])):
        coef[u] = unit
    product = mix_forward(packed, coef, lanes)
    out[...] = y_synthesis(product, tables[Y_MID], tables[PICKS]).astype(BF)


def back_kernel(lines, packed, sums, tables, out, dual, lanes, result):
    for u, unit in enumerate(y_analysis(lines[...], tables[Y_MID], tables[PICKS])):
        dual[u] = unit
    modes = mix_back(packed, dual, lanes, result)
    modes = y_synthesis(modes, tables[Y_IN], tables[PICKS])
    tail = jnp.broadcast_to(sums[...].reshape(1, 8, 128), (N, 8, 128))
    out[...] = jnp.concatenate([modes, tail], axis=1).astype(BF)


def weight_gradient(coef, dual, channel, out):
    for pair in range(PAIRS):
        unit, mode = divmod(pair, 3)
        dual_re = dual[unit, mode * 24 : mode * 24 + C, :]
        dual_im = dual[unit, (3 + mode) * 24 : (3 + mode) * 24 + C, :]
        re = line_of(coef, unit, mode, channel)
        im = line_of(coef, unit, 3 + mode, channel)
        start = channel * 2 * PAIRS * C + 2 * pair
        out[pl.ds(start, C, stride=2 * PAIRS), :] = re * dual_re + im * dual_im
        out[pl.ds(start + 1, C, stride=2 * PAIRS), :] = re * dual_im - im * dual_re


def same_cell(size):
    return ones_where(iota((size, 1), 0) % CY == iota((1, size), 1) % CY)


def spread_map(weight, weight_dim):
    spread = spread_matrix().astype(BF)
    tall = dot(spread, weight, 0, weight_dim).astype(BF)
    return (dot(tall, spread) * same_cell(C * CY)).astype(BF)


def flat_cells(values):
    return jnp.concatenate([values[x] for x in range(CX)], axis=1)


def pack_lines(cross, bias):
    picks = spread_matrix()
    exact = lax.Precision.HIGHEST
    point = dot(dot(picks, cross * same_cell(C * CY), 1, 0, exact), picks, 1, 1, exact)
    total = dot(bias, picks, 1, 1, exact)[:1]
    rows = jnp.concatenate([point, total], axis=0)
    rows = jnp.concatenate([rows, jnp.zeros((C + 1, 128 - C), F32)], axis=1)
    packed = []
    for r in range(4):
        line = jnp.zeros((1, 128), F32)
        for q in range(6):
            if r * 6 + q <= C:
                row = rows[r * 6 + q : r * 6 + q + 1]
                line = line + (pltpu.roll(row, q * C, 1) if q > 0 else row)
        packed.append(line)
    return jnp.concatenate(packed, axis=0)


def cells_kernel(
    lines, depth, field, cotangent, weight, bias, out, sums, slope_out, field_out
):
    matrix = depth_matrix(depth[...])
    mixing = spread_map(weight[...], 1)
    shift = dot(spread_matrix(), bias[...], 0, 1, lax.Precision.HIGHEST)
    fields = flat_cells(field)
    spectral = from_spectra(lines, matrix)
    pointwise = dot(mixing, fields) + shift
    slopes = []
    for batch in range(BATCHES):
        columns = []
        for group in (2 * batch, 2 * batch + 1):
            span = rows_of(group, 16)
            pre = spectral[rows_of(group, 128)] + wide_to_columns(pointwise[span])
            phi = 0.5 * (1.0 + lax.erf(pre * 0.7071067811865476))
            field_out[:, span, :] = to_cells(pre * phi).astype(BF)
            slope = phi + pre * jnp.exp(-0.5 * pre * pre) * 0.3989422804014327
            slope = slope * to_columns(cotangent[:, span, :])
            columns.append(slope.astype(BF))
            slope = to_cells(slope).astype(BF)
            slope_out[:, span, :] = slope
            slopes.append(flat_cells(slope))
        put_spectra(matrix, columns, batch, out)
    slopes = jnp.concatenate(slopes, axis=0)
    cross = dot(fields, slopes, 1, 1)
    total = dot(jnp.ones((8, CX * ZT), BF), slopes, 1, 1)
    sums[...] = pack_sums(pack_lines(cross, total))


def last_kernel(
    lines,
    depth,
    slope,
    weight,
    coef,
    dual,
    _,
    point_out,
    bias_out,
    field_out,
    weight_to,
    made,
    semaphore,
):
    start_weight_gradient(1 - FIRST, coef, dual, made, weight_to, semaphore)
    tails = jnp.sum(lines[:, ROWS:, :].astype(F32), axis=0)
    sums = (tails[:4] + tails[4:8]) * (NX * NY * ZT) ** -0.5
    for r in range(4):
        for q in range(6):
            index = r * 6 + q
            if index <= C:
                row = sums[r : r + 1]
                row = pltpu.roll(row, 128 - q * C, 1) if q > 0 else row
                if index < C:
                    point_out[index : index + 1, :] = row[:, :C]
                else:
                    bias_out[...] = row[:, :C]
    pointwise = dot(spread_map(weight[...], 0), flat_cells(slope))
    spectral = from_spectra(lines, depth_matrix(depth[...]))
    for group in range(GROUPS):
        span = rows_of(group, 16)
        total = to_cells(spectral[rows_of(group, 128)]) + wide_to_cells(pointwise[span])
        field_out[:, span, :] = total.astype(BF)
    end_weight_gradient(1 - FIRST, made, weight_to, semaphore)


def exchange(values, axis):
    return lax.all_to_all(values, axis, split_axis=0, concat_axis=0, tiled=True)


def body(field_in, point_weight, point_bias, spec_weight, out_cotangent):
    cells = (CX, C * CY, ZT)
    line_message = shaped((N, ROWS, 128), BF)
    mode_message = shaped((N, 24, 128), BF)
    mode_lines = shaped((3, 144, KY), F32)
    wide_weights = pltpu.VMEM((WEIGHTS, KY), F32)
    field = field_in.transpose(0, 2, 1, 3).reshape(cells)
    cotangent = out_cotangent.transpose(0, 2, 1, 3).reshape(cells)
    weights = spec_weight.transpose(1, 2, 4, 3, 0).reshape(WEIGHTS, KY)

    message = call(spectrum_kernel, line_message, name="spectrum")(field)
    message = exchange(message, "gx")
    message = call(x_analysis_kernel, mode_message, name="x_analysis")(message, X_IN)
    message = exchange(message, "gy")
    message, coef, packed = call(
        product_kernel,
        (mode_message, mode_lines, shaped((WEIGHTS // FIVE, 128), F32)),
        [pltpu.VMEM((3, 48, 128), F32)],
        "product",
    )(message, weights, Y_ALL)
    message = exchange(message, "gy")
    message = call(x_synthesis_kernel, line_message, name="x_synthesis")(message, X_MID)
    message = exchange(message, "gx")
    message, sums, slope, output_field = call(
        cells_kernel,
        (line_message, shaped((8, 128), F32), shaped(cells, BF), shaped(cells, BF)),
        name="cells",
    )(message, DEPTH_MID, field, cotangent, point_weight, point_bias.reshape(1, C))
    message = exchange(message, "gx")
    message = call(x_analysis_kernel, mode_message, name="x_analysis_back")(message, X_MID)
    message = exchange(message, "gy")
    message, dual = call(
        back_kernel,
        (shaped((N, 32, 128), BF), mode_lines),
        [pltpu.VMEM((3, 144, 128), F32), pltpu.VMEM((3, 144, KY), F32)],
        "back",
    )(message, packed, sums, Y_ALL)
    message = exchange(message, "gy")
    made = [wide_weights, pltpu.SemaphoreType.DMA(())]
    weight_shape = shaped((WEIGHTS, KY), F32)
    message, weight_grad = call(
        x_synthesis_sums_kernel,
        (shaped((N, 256, 128), BF), weight_shape),
        made,
        "x_synthesis_back",
        [pltpu.VMEM] * 4,
        [pltpu.VMEM, pl.ANY],
    )(message, X_IN, coef, dual)
    message = exchange(message, "gx")
    grad_point, grad_bias, grad_in, weight_grad = call(
        last_kernel,
        (shaped((C, C), F32), shaped((1, C), F32), shaped(cells, BF), weight_shape),
        made,
        "last",
        [pltpu.VMEM] * 6 + [pl.ANY],
        [pltpu.VMEM] * 3 + [pl.ANY],
        {6: 3},
    )(message, DEPTH_IN, slope, point_weight, coef, dual, weight_grad)
    grad_spec = weight_grad.reshape(C, C, PAIRS, 2, KY).transpose(4, 0, 1, 3, 2)

    def natural(values):
        return values.reshape(CX, C, CY, ZT).transpose(0, 2, 1, 3)

    return natural(output_field), natural(grad_in), grad_spec, grad_point, grad_bias.reshape(C)


def solution(mesh):
    return jax.shard_map(
        body,
        mesh=mesh,
        in_specs=(
            P("gx", "gy", None, None),
            P(),
            P(),
            P(None, None, None, None, ("gx", "gy")),
            P("gx", "gy", None, None),
        ),
        out_specs=(
            P("gx", "gy", None, None),
            P("gx", "gy", None, None),
            P(None, None, None, None, ("gx", "gy")),
            P(),
            P(),
        ),
        check_vma=False,
    )
```

```python
import math

import jax
import jax.numpy as jnp
import ml_dtypes
import numpy as np
from jax import lax
from jax.experimental import pallas as pl
from jax.experimental.pallas import tpu as pltpu
from jax.sharding import PartitionSpec as P

C = 20
Z = 32
T_SIZE = 4
KX = 24
KY = 24
KZ = 24
KT = 4
NX = 256
NY = 128
ZT = 128
M = 96
N = 16
CX = NX // N
CY = NY // N
ROWS = 12 * C
GROUPS = C // 2
PAIRS = 9
WEIGHTS = C * C * PAIRS * 2
FIRST = 0

BF = jnp.bfloat16
F32 = jnp.float32


def centered(count):
    return (np.arange(count) + count // 2) % count - count // 2


def rounded(table):
    return np.asarray(table, np.float32).astype(ml_dtypes.bfloat16)


def line_table(modes, length, scale):
    turns = centered(modes)[:, None] * np.arange(length)[None, :] % length
    angle = turns.astype(np.float32) * np.float32(2.0 * math.pi / length)
    scale = np.float32(scale)
    return rounded(np.cos(angle) * scale), rounded(np.sin(angle) * scale)


def depth_table(scale):
    cells = np.arange(ZT)
    turn_z = centered(KZ)[:, None] * (cells // T_SIZE)[None, :] % Z
    turn_t = centered(KT)[:, None] * (cells % T_SIZE)[None, :] % T_SIZE
    angle = turn_z.astype(np.float32)[:, None, :] * np.float32(2.0 * math.pi / Z)
    angle = angle + turn_t.astype(np.float32)[None, :, :] * np.float32(2.0 * math.pi / T_SIZE)
    angle = angle.reshape(M, ZT)
    return rounded(np.stack([np.cos(angle), -np.sin(angle)]) * np.float32(scale))


def depth_rows(scale):
    table = depth_table(scale).reshape(2, N, 2, 3, ZT).transpose(1, 2, 0, 3, 4)
    table = np.broadcast_to(table[:, :, None], (N, 2, 2, 2, 3, ZT))
    return np.ascontiguousarray(table).reshape(N, 24, ZT)


def x_rows(scale):
    table = np.concatenate(line_table(KX, NX, scale), axis=0)
    return np.ascontiguousarray(np.repeat(table, CY, axis=1))


def y_rows(scale):
    return np.concatenate(line_table(KY, NY, scale), axis=0)


def lane_picks():
    rows, lanes = np.arange(6 * 24)[:, None], np.arange(128)[None, :]
    return rounded((lanes == rows % 24 * 6 + rows // 24) & (rows % 24 < C))


DEPTH_IN = depth_rows(ZT**-0.5)
DEPTH_MID = depth_rows(M**-0.5)
X_IN = x_rows(NX**-0.5)
X_MID = x_rows(KX**-0.5)
Y_ALL = np.concatenate([y_rows(NY**-0.5), y_rows(KY**-0.5), lane_picks()], axis=0)
Y_IN = slice(0, 48)
Y_MID = slice(48, 96)
PICKS = slice(96, 96 + 144)


def dot(left, right, left_dim=1, right_dim=0, precision=None):
    return lax.dot_general(
        left,
        right,
        (((left_dim,), (right_dim,)), ((), ())),
        precision=precision,
        preferred_element_type=F32,
    )


def call(kernel, out_shape, scratch=(), name=None, spaces=None, out_spaces=None, aliases=None):
    options = {}
    if spaces is not None:
        options["in_specs"] = [pl.BlockSpec(memory_space=space) for space in spaces]
        options["out_specs"] = [pl.BlockSpec(memory_space=space) for space in out_spaces]
    return pl.pallas_call(
        kernel,
        out_shape=out_shape,
        scratch_shapes=scratch,
        compiler_params=pltpu.CompilerParams(vmem_limit_bytes=24 * 2**20),
        cost_estimate=pl.CostEstimate(flops=10**8, bytes_accessed=4 * 10**6, transcendentals=0),
        input_output_aliases=aliases or {},
        name=name,
        **options,
    )


def shaped(shape, dtype):
    return jax.ShapeDtypeStruct(shape, dtype)


def rows_of(group, count):
    return slice(group * count, group * count + count)


def iota(shape, dim):
    return lax.broadcasted_iota(jnp.int32, shape, dim)


def ones_where(condition):
    return jnp.where(condition, 1.0, 0.0)


def depth_matrix(rows):
    wide = rows.astype(F32)
    channel = iota((1, 24, 1), 1) // 6 % 2
    parts = [(wide * ones_where(channel == k)).reshape(N * 24, ZT) for k in range(2)]
    return jnp.concatenate(parts, axis=1).astype(BF)


def x_matrix(rows):
    size = rows.shape[1]
    same = ones_where(iota((1, CY, size), 1) == iota((1, CY, size), 2) % CY)
    wide = rows.reshape(KX, 1, size) * same
    return wide.reshape(KX * CY, size).astype(BF)


def lane_maps():
    row, lane = iota((ROWS, 1), 0), iota((1, 256), 1)
    inner = row % 12
    start = (row // 12) % 2 * 128 + row // 24 * 12
    real = inner % 6 < 3
    plain = ones_where(lane == start + inner)
    other = jnp.where(real, inner + 3, inner - 3)
    turned = ones_where(lane == start + other) * jnp.where(real, -1.0, 1.0)
    return plain.astype(BF), turned.astype(BF)


def spread_matrix():
    return ones_where(iota((C, C * CY), 0) == iota((C, C * CY), 1) // CY)


def to_columns(values):
    wide = values.astype(F32).reshape(CX, 2, CY, ZT)
    return jnp.concatenate([wide[:, k].reshape(CX * CY, ZT) for k in range(2)], axis=1)


def to_cells(columns):
    parts = [columns[:, k * ZT : (k + 1) * ZT].reshape(CX, CY, ZT) for k in range(2)]
    return jnp.stack(parts, axis=1).reshape(CX, 2 * CY, ZT)


def wide_to_columns(wide):
    def channel(k):
        rows = wide[k * CY : k * CY + CY]
        return jnp.concatenate([rows[:, x * ZT : x * ZT + ZT] for x in range(CX)], axis=0)

    return jnp.concatenate([channel(k) for k in range(2)], axis=1)


def wide_to_cells(wide):
    return jnp.stack([wide[:, x * ZT : x * ZT + ZT] for x in range(CX)], axis=0)


def put_spectra(matrix, columns, batch, out):
    spectra = dot(matrix, jnp.concatenate(columns, axis=0), 1, 1)
    parts = [spectra[:, k * 128 : k * 128 + 128].reshape(N, 24, 128) for k in range(2)]
    out[:, rows_of(batch, 48), :] = jnp.concatenate(parts, axis=1).astype(BF)


BATCHES = GROUPS // 2


def depth_rows_here(scale):
    row, lane = iota((24, 1), 0), iota((1, ZT), 1)
    mode = row // 12 * 3 + row % 3
    quarter = jnp.where(row % 6 < 3, 0.0, 8.0)
    z, t = (lane // T_SIZE).astype(F32), (lane % T_SIZE).astype(F32)
    blocks = []
    for block in range(N):
        jz, jt = divmod(6 * block, KT)
        jt = mode + jt
        jz = jz + jt // KT
        jt = jt % KT
        fz = jnp.where(jz < KZ // 2, jz, jz + Z - KZ).astype(F32)
        turns = fz * z + (jt * (Z // KT)).astype(F32) * t + quarter
        turns = turns - 32.0 * jnp.floor(turns * (1.0 / 32.0))
        angle = (jnp.abs(turns * 0.0625 - 1.0) - 0.5) * math.pi
        square = angle * angle
        wave = 1.0 + square * (-1.0 / 110.0)
        for factor in (72.0, 42.0, 20.0, 6.0):
            wave = 1.0 - square * (1.0 / factor) * wave
        blocks.append(angle * wave * scale)
    return jnp.stack(blocks, axis=0)


def spectrum_kernel(field, out):
    matrix = depth_matrix(depth_rows_here(ZT**-0.5))
    for batch in range(BATCHES):
        groups = (2 * batch, 2 * batch + 1)
        columns = [to_columns(field[:, rows_of(g, 16), :]).astype(BF) for g in groups]
        put_spectra(matrix, columns, batch, out)


def from_spectra(lines, matrix):
    rows = []
    for batch in range(BATCHES):
        wide = lines[:, rows_of(batch, 48), :].astype(F32).reshape(N, 2, 24, 128)
        rows += [wide[:, k].reshape(N * 24, 128) for k in range(2)]
    return dot(jnp.concatenate(rows, axis=1).astype(BF), matrix, 0, 0)


def split_dot(left, right):
    high = left.astype(BF)
    low = (left - high.astype(F32)).astype(BF)
    return dot(high, right) + dot(low, right)


def x_analysis_kernel(lines, table, out):
    plain, turned = lane_maps()
    rows = jnp.concatenate([lines[a] for a in range(N)], axis=1)
    table = table[...].astype(F32)
    matrix = jnp.concatenate([x_matrix(table[:KX]), x_matrix(table[KX:])], axis=0)
    both = dot(matrix, rows, 1, 1)
    half = KX * CY
    coef = split_dot(both[:half], plain) + split_dot(both[half:], turned)
    units = [coef[:, k * 128 : k * 128 + 128].reshape(KX, CY, 128) for k in range(2)]
    out[...] = jnp.stack(units, axis=1).reshape(N, 24, 128).astype(BF)


def x_modes(modes):
    plain, turned = lane_maps()
    units = modes.reshape(KX, 2, CY, 128)
    flat = jnp.concatenate([units[:, k].reshape(KX * CY, 128) for k in range(2)], axis=1)
    flat = flat.astype(BF)
    return dot(plain, flat, 1, 1).astype(BF), dot(turned, flat, 1, 1).astype(BF)


def x_lines(first, second, table):
    table = table.astype(F32)
    lines = dot(first, x_matrix(table[:KX])) + dot(second, x_matrix(table[KX:]))
    return lines.astype(BF)


def x_synthesis_kernel(modes, table, out):
    first, second = x_modes(modes[...].astype(F32))
    lines = x_lines(first, second, table[...])
    for a in range(N):
        out[a] = lines[:, a * 128 : a * 128 + 128]


def when_core(core):
    return pl.when(lax.axis_index("gy") % 2 == core)


def put_sums(core, field, slope, out):
    @when_core(core)
    def _():
        fields, slopes = flat_cells(field), flat_cells(slope)
        cross = dot(fields, slopes, 1, 1)
        total = dot(jnp.ones((8, CX * ZT), BF), slopes, 1, 1)
        out[...] = pack_sums(pack_lines(cross, total))


def x_analysis_sums_kernel(lines, table, field, slope, out, sums):
    x_analysis_kernel(lines, table, out)
    put_sums(1, field, slope, sums)


def start_weight_gradient(core, coef, dual, made, target, semaphore):
    @when_core(core)
    def _():
        for channel in range(C):
            weight_gradient(coef, dual, channel, made)
        pltpu.make_async_copy(made, target, semaphore).start()


def end_weight_gradient(core, made, target, semaphore):
    @when_core(core)
    def _():
        pltpu.make_async_copy(made, target, semaphore).wait()


def x_synthesis_sums_kernel(modes, table, coef, dual, out, weight_to, made, semaphore):
    start_weight_gradient(FIRST, coef, dual, made, weight_to, semaphore)
    wide = modes[...].astype(F32)
    first, second = x_modes(wide[:, :24])
    lines = x_lines(first, second, table[...])
    sums = jnp.sum(wide[:, 24:], axis=0)
    block = pack_sums(sums[:4] + sums[4:])
    tail = jnp.concatenate([block, jnp.zeros_like(block)], axis=0).astype(BF)
    for a in range(N):
        out[a, :ROWS] = lines[:, a * 128 : a * 128 + 128]
        out[a, ROWS:] = tail
    end_weight_gradient(FIRST, made, weight_to, semaphore)


def pack_sums(values):
    high = values.astype(BF).astype(F32)
    return jnp.concatenate([high, values - high], axis=0)


def turn_lanes(values, sign):
    part = iota(values.shape, 1) % 6
    ahead = pltpu.roll(values, 125, 1)
    behind = pltpu.roll(values, 3, 1)
    return jnp.where(part < 3, sign * ahead, -sign * behind)


def y_analysis(lines, table, picks):
    wide = lines.astype(F32).reshape(N, 3, CY, 128)
    wide = jnp.concatenate([wide[:, u].reshape(NY, 128) for u in range(3)], axis=1)
    both = dot(table, wide.astype(BF))
    result = []
    for u in range(3):
        piece = both[:, u * 128 : u * 128 + 128]
        coef = piece[:KY] + turn_lanes(piece[KY:], 1.0)
        result.append(dot(picks, coef.astype(BF), 1, 1))
    return result


def y_synthesis(units, table, picks):
    columns = []
    for unit in units:
        modes = dot(unit.astype(BF), picks, 0, 0)
        columns.append(jnp.concatenate([modes, turn_lanes(modes, -1.0)], axis=0))
    columns = jnp.concatenate(columns, axis=1).astype(BF)
    lines = dot(table, columns, 0, 0)
    lines = [lines[:, u * 128 : u * 128 + 128].reshape(N, CY, 128) for u in range(3)]
    return jnp.stack(lines, axis=1).reshape(N, 24, 128)


def line_of(modes, unit, kind, channel):
    return modes[unit, pl.ds(kind * 24 + channel, 1), :]


FIVE = 5
STEP = C // FIVE


def beside(pieces):
    empty = jnp.zeros((pieces[0].shape[0], 128 - FIVE * KY), F32)
    return jnp.concatenate(list(pieces) + [empty], axis=1)


def piece_of(values, q):
    return (pltpu.roll(values, 128 - q * KY, 1) if q > 0 else values)[:, :KY]


def pack_weights(weights, packed):
    size = WEIGHTS // C
    for half in range(2):
        wide = weights[half * (WEIGHTS // 2) : (half + 1) * (WEIGHTS // 2), :].astype(F32)
        for group in range(STEP // 2):
            base = group * FIVE * size
            rows = [wide[base + q * size : base + q * size + size] for q in range(FIVE)]
            start = (half * (STEP // 2) + group) * size
            packed[start : start + size, :] = beside(rows)


def mix_forward(packed, modes, lanes):
    size = WEIGHTS // C
    empty = jnp.zeros((4, KY), F32)
    units = []
    for unit in range(3):
        for kind in range(6):
            starts = [kind * 24 + q for q in range(FIVE)]
            rows = [modes[unit, pl.ds(start, STEP, stride=FIVE), :] for start in starts]
            lanes[unit, kind * 8 : kind * 8 + STEP, :] = beside(rows)
        parts = [[], []]
        for mode in range(3):
            real = jnp.zeros((C, 128), F32)
            imag = jnp.zeros((C, 128), F32)
            for group in range(STEP):
                start = group * size + 2 * (unit * 3 + mode)
                weight_re = packed[pl.ds(start, C, stride=2 * PAIRS), :]
                weight_im = packed[pl.ds(start + 1, C, stride=2 * PAIRS), :]
                re = lanes[unit, pl.ds(mode * 8 + group, 1), :]
                im = lanes[unit, pl.ds((3 + mode) * 8 + group, 1), :]
                real = real + (weight_re * re - weight_im * im)
                imag = imag + (weight_re * im + weight_im * re)
            for part, total in enumerate((real, imag)):
                pieces = [piece_of(total, q) for q in range(FIVE)]
                parts[part] += [sum(pieces[1:], pieces[0]), empty]
        units.append(jnp.concatenate(parts[0] + parts[1], axis=0))
    return units


def mix_back(packed, modes, lanes, result):
    size = WEIGHTS // C
    result[...] = jnp.zeros(result.shape, F32)
    units = []
    for unit in range(3):
        lanes[unit] = beside([modes[unit]] * FIVE)
        for mode in range(3):
            real = jnp.zeros((STEP, 128), F32)
            imag = jnp.zeros((STEP, 128), F32)
            for k in range(C):
                start = k * 2 * PAIRS + 2 * (unit * 3 + mode)
                weight_re = packed[pl.ds(start, STEP, stride=size), :]
                weight_im = packed[pl.ds(start + 1, STEP, stride=size), :]
                re = lanes[unit, pl.ds(mode * 24 + k, 1), :]
                im = lanes[unit, pl.ds((3 + mode) * 24 + k, 1), :]
                real = real + (weight_re * re + weight_im * im)
                imag = imag + (weight_re * im - weight_im * re)
            for part, total in enumerate((real, imag)):
                for q in range(FIVE):
                    rows = pl.ds((part * 3 + mode) * 24 + q, STEP, stride=FIVE)
                    result[unit, rows, :] = piece_of(total, q)
        units.append(result[unit])
    return units


def product_kernel(lines, weights, tables, out, coef, packed, lanes):
    pack_weights(weights, packed)
    for u, unit in enumerate(y_analysis(lines[...], tables[Y_IN], tables[PICKS])):
        coef[u] = unit
    product = mix_forward(packed, coef, lanes)
    out[...] = y_synthesis(product, tables[Y_MID], tables[PICKS]).astype(BF)


def back_kernel(lines, packed, sums, late_sums, tables, out, dual, lanes, result):
    for u, unit in enumerate(y_analysis(lines[...], tables[Y_MID], tables[PICKS])):
        dual[u] = unit
    modes = mix_back(packed, dual, lanes, result)
    modes = y_synthesis(modes, tables[Y_IN], tables[PICKS])
    tail = jnp.where(lax.axis_index("gy") % 2 == 0, sums[...], late_sums[...])
    tail = jnp.broadcast_to(tail.reshape(1, 8, 128), (N, 8, 128))
    out[...] = jnp.concatenate([modes, tail], axis=1).astype(BF)


def weight_gradient(coef, dual, channel, out):
    for pair in range(PAIRS):
        unit, mode = divmod(pair, 3)
        dual_re = dual[unit, mode * 24 : mode * 24 + C, :]
        dual_im = dual[unit, (3 + mode) * 24 : (3 + mode) * 24 + C, :]
        re = line_of(coef, unit, mode, channel)
        im = line_of(coef, unit, 3 + mode, channel)
        start = channel * 2 * PAIRS * C + 2 * pair
        out[pl.ds(start, C, stride=2 * PAIRS), :] = re * dual_re + im * dual_im
        out[pl.ds(start + 1, C, stride=2 * PAIRS), :] = re * dual_im - im * dual_re


def same_cell(size):
    return ones_where(iota((size, 1), 0) % CY == iota((1, size), 1) % CY)


def spread_map(weight, weight_dim):
    spread = spread_matrix().astype(BF)
    tall = dot(spread, weight, 0, weight_dim).astype(BF)
    return (dot(tall, spread) * same_cell(C * CY)).astype(BF)


def flat_cells(values):
    return jnp.concatenate([values[x] for x in range(CX)], axis=1)


def pack_lines(cross, bias):
    picks = spread_matrix()
    exact = lax.Precision.HIGHEST
    point = dot(dot(picks, cross * same_cell(C * CY), 1, 0, exact), picks, 1, 1, exact)
    total = dot(bias, picks, 1, 1, exact)[:1]
    rows = jnp.concatenate([point, total], axis=0)
    rows = jnp.concatenate([rows, jnp.zeros((C + 1, 128 - C), F32)], axis=1)
    packed = []
    for r in range(4):
        line = jnp.zeros((1, 128), F32)
        for q in range(6):
            if r * 6 + q <= C:
                row = rows[r * 6 + q : r * 6 + q + 1]
                line = line + (pltpu.roll(row, q * C, 1) if q > 0 else row)
        packed.append(line)
    return jnp.concatenate(packed, axis=0)


def cells_kernel(
    lines, depth, field, cotangent, weight, bias, out, sums, slope_out, field_out
):
    matrix = depth_matrix(depth[...])
    mixing = spread_map(weight[...], 1)
    shift = dot(spread_matrix(), bias[...], 0, 1, lax.Precision.HIGHEST)
    fields = flat_cells(field)
    spectral = from_spectra(lines, matrix)
    pointwise = dot(mixing, fields) + shift
    for batch in range(BATCHES):
        columns = []
        for group in (2 * batch, 2 * batch + 1):
            span = rows_of(group, 16)
            pre = spectral[rows_of(group, 128)] + wide_to_columns(pointwise[span])
            phi = 0.5 * (1.0 + lax.erf(pre * 0.7071067811865476))
            field_out[:, span, :] = to_cells(pre * phi).astype(BF)
            slope = phi + pre * jnp.exp(-0.5 * pre * pre) * 0.3989422804014327
            slope = slope * to_columns(cotangent[:, span, :])
            columns.append(slope.astype(BF))
            slope_out[:, span, :] = to_cells(slope).astype(BF)
        put_spectra(matrix, columns, batch, out)
    put_sums(0, field, slope_out, sums)


def last_kernel(
    lines,
    depth,
    slope,
    weight,
    coef,
    dual,
    _,
    point_out,
    bias_out,
    field_out,
    weight_to,
    made,
    semaphore,
):
    start_weight_gradient(1 - FIRST, coef, dual, made, weight_to, semaphore)
    tails = jnp.sum(lines[:, ROWS:, :].astype(F32), axis=0)
    sums = (tails[:4] + tails[4:8]) * (NX * NY * ZT) ** -0.5
    for r in range(4):
        for q in range(6):
            index = r * 6 + q
            if index <= C:
                row = sums[r : r + 1]
                row = pltpu.roll(row, 128 - q * C, 1) if q > 0 else row
                if index < C:
                    point_out[index : index + 1, :] = row[:, :C]
                else:
                    bias_out[...] = row[:, :C]
    pointwise = dot(spread_map(weight[...], 0), flat_cells(slope))
    spectral = from_spectra(lines, depth_matrix(depth[...]))
    for group in range(GROUPS):
        span = rows_of(group, 16)
        total = to_cells(spectral[rows_of(group, 128)]) + wide_to_cells(pointwise[span])
        field_out[:, span, :] = total.astype(BF)
    end_weight_gradient(1 - FIRST, made, weight_to, semaphore)


def exchange(values, axis):
    return lax.all_to_all(values, axis, split_axis=0, concat_axis=0, tiled=True)


def body(field_in, point_weight, point_bias, spec_weight, out_cotangent):
    cells = (CX, C * CY, ZT)
    line_message = shaped((N, ROWS, 128), BF)
    mode_message = shaped((N, 24, 128), BF)
    mode_lines = shaped((3, 144, KY), F32)
    wide_weights = pltpu.VMEM((WEIGHTS, KY), F32)
    field = field_in.transpose(0, 2, 1, 3).reshape(cells)
    cotangent = out_cotangent.transpose(0, 2, 1, 3).reshape(cells)
    weights = spec_weight.transpose(1, 2, 4, 3, 0).reshape(WEIGHTS, KY)

    message = call(spectrum_kernel, line_message, name="spectrum")(field)
    message = exchange(message, "gx")
    message = call(x_analysis_kernel, mode_message, name="x_analysis")(message, X_IN)
    message = exchange(message, "gy")
    message, coef, packed = call(
        product_kernel,
        (mode_message, mode_lines, shaped((WEIGHTS // FIVE, 128), F32)),
        [pltpu.VMEM((3, 48, 128), F32)],
        "product",
    )(message, weights, Y_ALL)
    message = exchange(message, "gy")
    message = call(x_synthesis_kernel, line_message, name="x_synthesis")(message, X_MID)
    message = exchange(message, "gx")
    message, sums, slope, output_field = call(
        cells_kernel,
        (line_message, shaped((8, 128), F32), shaped(cells, BF), shaped(cells, BF)),
        name="cells",
    )(message, DEPTH_MID, field, cotangent, point_weight, point_bias.reshape(1, C))
    message = exchange(message, "gx")
    message, late_sums = call(
        x_analysis_sums_kernel, (mode_message, shaped((8, 128), F32)), name="x_analysis_back"
    )(message, X_MID, field, slope)
    message = exchange(message, "gy")
    message, dual = call(
        back_kernel,
        (shaped((N, 32, 128), BF), mode_lines),
        [pltpu.VMEM((3, 144, 128), F32), pltpu.VMEM((3, 144, KY), F32)],
        "back",
    )(message, packed, sums, late_sums, Y_ALL)
    message = exchange(message, "gy")
    made = [wide_weights, pltpu.SemaphoreType.DMA(())]
    weight_shape = shaped((WEIGHTS, KY), F32)
    message, weight_grad = call(
        x_synthesis_sums_kernel,
        (shaped((N, 256, 128), BF), weight_shape),
        made,
        "x_synthesis_back",
        [pltpu.VMEM] * 4,
        [pltpu.VMEM, pl.ANY],
    )(message, X_IN, coef, dual)
    message = exchange(message, "gx")
    grad_point, grad_bias, grad_in, weight_grad = call(
        last_kernel,
        (shaped((C, C), F32), shaped((1, C), F32), shaped(cells, BF), weight_shape),
        made,
        "last",
        [pltpu.VMEM] * 6 + [pl.ANY],
        [pltpu.VMEM] * 3 + [pl.ANY],
        {6: 3},
    )(message, DEPTH_IN, slope, point_weight, coef, dual, weight_grad)
    grad_spec = weight_grad.reshape(C, C, PAIRS, 2, KY).transpose(4, 0, 1, 3, 2)

    def natural(values):
        return values.reshape(CX, C, CY, ZT).transpose(0, 2, 1, 3)

    return natural(output_field), natural(grad_in), grad_spec, grad_point, grad_bias.reshape(C)


def solution(mesh):
    return jax.shard_map(
        body,
        mesh=mesh,
        in_specs=(
            P("gx", "gy", None, None),
            P(),
            P(),
            P(None, None, None, None, ("gx", "gy")),
            P("gx", "gy", None, None),
        ),
        out_specs=(
            P("gx", "gy", None, None),
            P("gx", "gy", None, None),
            P(None, None, None, None, ("gx", "gy")),
            P(),
            P(),
        ),
        check_vma=False,
    )
```

```python
import math

import jax
import jax.numpy as jnp
import ml_dtypes
import numpy as np
from jax import lax
from jax.experimental import pallas as pl
from jax.experimental.pallas import tpu as pltpu
from jax.sharding import PartitionSpec as P

C = 20
Z = 32
T_SIZE = 4
KX = 24
KY = 24
KZ = 24
KT = 4
NX = 256
NY = 128
ZT = 128
M = 96
N = 16
CX = NX // N
CY = NY // N
ROWS = 12 * C
GROUPS = C // 2
PAIRS = 9
WEIGHTS = C * C * PAIRS * 2
FIRST = 0

BF = jnp.bfloat16
F32 = jnp.float32


def centered(count):
    return (np.arange(count) + count // 2) % count - count // 2


def rounded(table):
    return np.asarray(table, np.float32).astype(ml_dtypes.bfloat16)


def line_table(modes, length, scale):
    turns = centered(modes)[:, None] * np.arange(length)[None, :] % length
    angle = turns.astype(np.float32) * np.float32(2.0 * math.pi / length)
    scale = np.float32(scale)
    return rounded(np.cos(angle) * scale), rounded(np.sin(angle) * scale)


def depth_table(scale):
    cells = np.arange(ZT)
    turn_z = centered(KZ)[:, None] * (cells // T_SIZE)[None, :] % Z
    turn_t = centered(KT)[:, None] * (cells % T_SIZE)[None, :] % T_SIZE
    angle = turn_z.astype(np.float32)[:, None, :] * np.float32(2.0 * math.pi / Z)
    angle = angle + turn_t.astype(np.float32)[None, :, :] * np.float32(2.0 * math.pi / T_SIZE)
    angle = angle.reshape(M, ZT)
    return rounded(np.stack([np.cos(angle), -np.sin(angle)]) * np.float32(scale))


def depth_rows(scale):
    table = depth_table(scale).reshape(2, N, 2, 3, ZT).transpose(1, 2, 0, 3, 4)
    table = np.broadcast_to(table[:, :, None], (N, 2, 2, 2, 3, ZT))
    return np.ascontiguousarray(table).reshape(N, 24, ZT)


def x_rows(scale):
    table = np.concatenate(line_table(KX, NX, scale), axis=0)
    return np.ascontiguousarray(np.repeat(table, CY, axis=1))


def y_rows(scale):
    return np.concatenate(line_table(KY, NY, scale), axis=0)


def lane_picks():
    rows, lanes = np.arange(6 * 24)[:, None], np.arange(128)[None, :]
    return rounded((lanes == rows % 24 * 6 + rows // 24) & (rows % 24 < C))


DEPTH_IN = depth_rows(ZT**-0.5)
DEPTH_MID = depth_rows(M**-0.5)
X_IN = x_rows(NX**-0.5)
X_MID = x_rows(KX**-0.5)
Y_ALL = np.concatenate([y_rows(NY**-0.5), y_rows(KY**-0.5), lane_picks()], axis=0)
Y_IN = slice(0, 48)
Y_MID = slice(48, 96)
PICKS = slice(96, 96 + 144)


def dot(left, right, left_dim=1, right_dim=0, precision=None):
    return lax.dot_general(
        left,
        right,
        (((left_dim,), (right_dim,)), ((), ())),
        precision=precision,
        preferred_element_type=F32,
    )


def call(kernel, out_shape, scratch=(), name=None, spaces=None, out_spaces=None, aliases=None):
    options = {}
    if spaces is not None:
        options["in_specs"] = [pl.BlockSpec(memory_space=space) for space in spaces]
        options["out_specs"] = [pl.BlockSpec(memory_space=space) for space in out_spaces]
    return pl.pallas_call(
        kernel,
        out_shape=out_shape,
        scratch_shapes=scratch,
        compiler_params=pltpu.CompilerParams(vmem_limit_bytes=24 * 2**20),
        cost_estimate=pl.CostEstimate(flops=10**8, bytes_accessed=4 * 10**6, transcendentals=0),
        input_output_aliases=aliases or {},
        name=name,
        **options,
    )


def shaped(shape, dtype):
    return jax.ShapeDtypeStruct(shape, dtype)


def rows_of(group, count):
    return slice(group * count, group * count + count)


def iota(shape, dim):
    return lax.broadcasted_iota(jnp.int32, shape, dim)


def ones_where(condition):
    return jnp.where(condition, 1.0, 0.0)


def depth_matrix(rows):
    wide = rows.astype(F32)
    channel = iota((1, 24, 1), 1) // 6 % 2
    parts = [(wide * ones_where(channel == k)).reshape(N * 24, ZT) for k in range(2)]
    return jnp.concatenate(parts, axis=1).astype(BF)


def x_matrix(rows):
    size = rows.shape[1]
    same = ones_where(iota((1, CY, size), 1) == iota((1, CY, size), 2) % CY)
    wide = rows.reshape(KX, 1, size) * same
    return wide.reshape(KX * CY, size).astype(BF)


def lane_maps():
    row, lane = iota((ROWS, 1), 0), iota((1, 256), 1)
    inner = row % 12
    start = (row // 12) % 2 * 128 + row // 24 * 12
    real = inner % 6 < 3
    plain = ones_where(lane == start + inner)
    other = jnp.where(real, inner + 3, inner - 3)
    turned = ones_where(lane == start + other) * jnp.where(real, -1.0, 1.0)
    return plain.astype(BF), turned.astype(BF)


def spread_matrix():
    return ones_where(iota((C, C * CY), 0) == iota((C, C * CY), 1) // CY)


def to_columns(values):
    wide = values.astype(F32).reshape(CX, 2, CY, ZT)
    return jnp.concatenate([wide[:, k].reshape(CX * CY, ZT) for k in range(2)], axis=1)


def to_cells(columns):
    parts = [columns[:, k * ZT : (k + 1) * ZT].reshape(CX, CY, ZT) for k in range(2)]
    return jnp.stack(parts, axis=1).reshape(CX, 2 * CY, ZT)


def wide_to_columns(wide):
    def channel(k):
        rows = wide[k * CY : k * CY + CY]
        return jnp.concatenate([rows[:, x * ZT : x * ZT + ZT] for x in range(CX)], axis=0)

    return jnp.concatenate([channel(k) for k in range(2)], axis=1)


def wide_to_cells(wide):
    return jnp.stack([wide[:, x * ZT : x * ZT + ZT] for x in range(CX)], axis=0)


def put_spectra(matrix, columns, batch, out):
    spectra = dot(matrix, jnp.concatenate(columns, axis=0), 1, 1)
    parts = [spectra[:, k * 128 : k * 128 + 128].reshape(N, 24, 128) for k in range(2)]
    out[:, rows_of(batch, 48), :] = jnp.concatenate(parts, axis=1).astype(BF)


BATCHES = GROUPS // 2


def depth_rows_here(scale):
    row, lane = iota((24, 1), 0), iota((1, ZT), 1)
    mode = row // 12 * 3 + row % 3
    quarter = jnp.where(row % 6 < 3, 0.0, 8.0)
    z, t = (lane // T_SIZE).astype(F32), (lane % T_SIZE).astype(F32)
    blocks = []
    for block in range(N):
        jz, jt = divmod(6 * block, KT)
        jt = mode + jt
        jz = jz + jt // KT
        jt = jt % KT
        fz = jnp.where(jz < KZ // 2, jz, jz + Z - KZ).astype(F32)
        turns = fz * z + (jt * (Z // KT)).astype(F32) * t + quarter
        turns = turns - 32.0 * jnp.floor(turns * (1.0 / 32.0))
        angle = (jnp.abs(turns * 0.0625 - 1.0) - 0.5) * math.pi
        square = angle * angle
        wave = 1.0 + square * (-1.0 / 110.0)
        for factor in (72.0, 42.0, 20.0, 6.0):
            wave = 1.0 - square * (1.0 / factor) * wave
        blocks.append(angle * wave * scale)
    return jnp.stack(blocks, axis=0)


def spectrum_kernel(field, out):
    matrix = depth_matrix(depth_rows_here(ZT**-0.5))
    for batch in range(BATCHES):
        groups = (2 * batch, 2 * batch + 1)
        columns = [to_columns(field[:, rows_of(g, 16), :]).astype(BF) for g in groups]
        put_spectra(matrix, columns, batch, out)


def from_spectra(lines, matrix):
    rows = []
    for batch in range(BATCHES):
        wide = lines[:, rows_of(batch, 48), :].astype(F32).reshape(N, 2, 24, 128)
        rows += [wide[:, k].reshape(N * 24, 128) for k in range(2)]
    return dot(jnp.concatenate(rows, axis=1).astype(BF), matrix, 0, 0)


def split_dot(left, right):
    high = left.astype(BF)
    low = (left - high.astype(F32)).astype(BF)
    return dot(high, right) + dot(low, right)


def x_analysis_kernel(lines, table, out):
    plain, turned = lane_maps()
    rows = jnp.concatenate([lines[a] for a in range(N)], axis=1)
    table = table[...].astype(F32)
    matrix = jnp.concatenate([x_matrix(table[:KX]), x_matrix(table[KX:])], axis=0)
    both = dot(matrix, rows, 1, 1)
    half = KX * CY
    coef = split_dot(both[:half], plain) + split_dot(both[half:], turned)
    units = [coef[:, k * 128 : k * 128 + 128].reshape(KX, CY, 128) for k in range(2)]
    out[...] = jnp.stack(units, axis=1).reshape(N, 24, 128).astype(BF)


def x_modes(modes):
    plain, turned = lane_maps()
    units = modes.reshape(KX, 2, CY, 128)
    flat = jnp.concatenate([units[:, k].reshape(KX * CY, 128) for k in range(2)], axis=1)
    flat = flat.astype(BF)
    return dot(plain, flat, 1, 1).astype(BF), dot(turned, flat, 1, 1).astype(BF)


def x_lines(first, second, table):
    table = table.astype(F32)
    lines = dot(first, x_matrix(table[:KX])) + dot(second, x_matrix(table[KX:]))
    return lines.astype(BF)


def x_synthesis_kernel(modes, table, out):
    first, second = x_modes(modes[...].astype(F32))
    lines = x_lines(first, second, table[...])
    for a in range(N):
        out[a] = lines[:, a * 128 : a * 128 + 128]


def when_core(core):
    return pl.when(lax.axis_index("gy") % 2 == core)


def put_sums(core, field, slope, out):
    @when_core(core)
    def _():
        fields, slopes = flat_cells(field), flat_cells(slope)
        cross = dot(fields, slopes, 1, 1)
        total = dot(jnp.ones((8, CX * ZT), BF), slopes, 1, 1)
        out[...] = pack_sums(pack_lines(cross, total))


def put_point_back(core, slope, weight, out):
    @when_core(core)
    def _():
        out[...] = dot(spread_map(weight[...], 0), flat_cells(slope))


def x_analysis_sums_kernel(lines, table, field, slope, weight, out, sums, point):
    x_analysis_kernel(lines, table, out)
    put_sums(1, field, slope, sums)
    put_point_back(1, slope, weight, point)


def start_weight_gradient(core, coef, dual, made, target, semaphore):
    @when_core(core)
    def _():
        for channel in range(C):
            weight_gradient(coef, dual, channel, made)
        pltpu.make_async_copy(made, target, semaphore).start()


def end_weight_gradient(core, made, target, semaphore):
    @when_core(core)
    def _():
        pltpu.make_async_copy(made, target, semaphore).wait()


def x_synthesis_sums_kernel(
    modes, table, coef, dual, slope, weight, out, point, weight_to, made, semaphore
):
    start_weight_gradient(FIRST, coef, dual, made, weight_to, semaphore)
    put_point_back(0, slope, weight, point)
    wide = modes[...].astype(F32)
    first, second = x_modes(wide[:, :24])
    lines = x_lines(first, second, table[...])
    sums = jnp.sum(wide[:, 24:], axis=0)
    block = pack_sums(sums[:4] + sums[4:])
    tail = jnp.concatenate([block, jnp.zeros_like(block)], axis=0).astype(BF)
    for a in range(N):
        out[a, :ROWS] = lines[:, a * 128 : a * 128 + 128]
        out[a, ROWS:] = tail
    end_weight_gradient(FIRST, made, weight_to, semaphore)


def pack_sums(values):
    high = values.astype(BF).astype(F32)
    return jnp.concatenate([high, values - high], axis=0)


def turn_lanes(values, sign):
    part = iota(values.shape, 1) % 6
    ahead = pltpu.roll(values, 125, 1)
    behind = pltpu.roll(values, 3, 1)
    return jnp.where(part < 3, sign * ahead, -sign * behind)


def y_analysis(lines, table, picks):
    wide = lines.astype(F32).reshape(N, 3, CY, 128)
    wide = jnp.concatenate([wide[:, u].reshape(NY, 128) for u in range(3)], axis=1)
    both = dot(table, wide.astype(BF))
    result = []
    for u in range(3):
        piece = both[:, u * 128 : u * 128 + 128]
        coef = piece[:KY] + turn_lanes(piece[KY:], 1.0)
        result.append(dot(picks, coef.astype(BF), 1, 1))
    return result


def y_synthesis(units, table, picks):
    columns = []
    for unit in units:
        modes = dot(unit.astype(BF), picks, 0, 0)
        columns.append(jnp.concatenate([modes, turn_lanes(modes, -1.0)], axis=0))
    columns = jnp.concatenate(columns, axis=1).astype(BF)
    lines = dot(table, columns, 0, 0)
    lines = [lines[:, u * 128 : u * 128 + 128].reshape(N, CY, 128) for u in range(3)]
    return jnp.stack(lines, axis=1).reshape(N, 24, 128)


def line_of(modes, unit, kind, channel):
    return modes[unit, pl.ds(kind * 24 + channel, 1), :]


FIVE = 5
STEP = C // FIVE


def beside(pieces):
    empty = jnp.zeros((pieces[0].shape[0], 128 - FIVE * KY), F32)
    return jnp.concatenate(list(pieces) + [empty], axis=1)


def piece_of(values, q):
    return (pltpu.roll(values, 128 - q * KY, 1) if q > 0 else values)[:, :KY]


def pack_weights(weights, packed):
    size = WEIGHTS // C
    for half in range(2):
        wide = weights[half * (WEIGHTS // 2) : (half + 1) * (WEIGHTS // 2), :].astype(F32)
        for group in range(STEP // 2):
            base = group * FIVE * size
            rows = [wide[base + q * size : base + q * size + size] for q in range(FIVE)]
            start = (half * (STEP // 2) + group) * size
            packed[start : start + size, :] = beside(rows)


def mix_forward(packed, modes, lanes):
    size = WEIGHTS // C
    empty = jnp.zeros((4, KY), F32)
    units = []
    for unit in range(3):
        for kind in range(6):
            starts = [kind * 24 + q for q in range(FIVE)]
            rows = [modes[unit, pl.ds(start, STEP, stride=FIVE), :] for start in starts]
            lanes[unit, kind * 8 : kind * 8 + STEP, :] = beside(rows)
        parts = [[], []]
        for mode in range(3):
            real = jnp.zeros((C, 128), F32)
            imag = jnp.zeros((C, 128), F32)
            for group in range(STEP):
                start = group * size + 2 * (unit * 3 + mode)
                weight_re = packed[pl.ds(start, C, stride=2 * PAIRS), :]
                weight_im = packed[pl.ds(start + 1, C, stride=2 * PAIRS), :]
                re = lanes[unit, pl.ds(mode * 8 + group, 1), :]
                im = lanes[unit, pl.ds((3 + mode) * 8 + group, 1), :]
                real = real + (weight_re * re - weight_im * im)
                imag = imag + (weight_re * im + weight_im * re)
            for part, total in enumerate((real, imag)):
                pieces = [piece_of(total, q) for q in range(FIVE)]
                parts[part] += [sum(pieces[1:], pieces[0]), empty]
        units.append(jnp.concatenate(parts[0] + parts[1], axis=0))
    return units


def mix_back(packed, modes, lanes, result):
    size = WEIGHTS // C
    result[...] = jnp.zeros(result.shape, F32)
    units = []
    for unit in range(3):
        lanes[unit] = beside([modes[unit]] * FIVE)
        for mode in range(3):
            real = jnp.zeros((STEP, 128), F32)
            imag = jnp.zeros((STEP, 128), F32)
            for k in range(C):
                start = k * 2 * PAIRS + 2 * (unit * 3 + mode)
                weight_re = packed[pl.ds(start, STEP, stride=size), :]
                weight_im = packed[pl.ds(start + 1, STEP, stride=size), :]
                re = lanes[unit, pl.ds(mode * 24 + k, 1), :]
                im = lanes[unit, pl.ds((3 + mode) * 24 + k, 1), :]
                real = real + (weight_re * re + weight_im * im)
                imag = imag + (weight_re * im - weight_im * re)
            for part, total in enumerate((real, imag)):
                for q in range(FIVE):
                    rows = pl.ds((part * 3 + mode) * 24 + q, STEP, stride=FIVE)
                    result[unit, rows, :] = piece_of(total, q)
        units.append(result[unit])
    return units


def product_kernel(lines, weights, tables, out, coef, packed, lanes):
    pack_weights(weights, packed)
    for u, unit in enumerate(y_analysis(lines[...], tables[Y_IN], tables[PICKS])):
        coef[u] = unit
    product = mix_forward(packed, coef, lanes)
    out[...] = y_synthesis(product, tables[Y_MID], tables[PICKS]).astype(BF)


def back_kernel(lines, packed, sums, late_sums, tables, out, dual, lanes, result):
    for u, unit in enumerate(y_analysis(lines[...], tables[Y_MID], tables[PICKS])):
        dual[u] = unit
    modes = mix_back(packed, dual, lanes, result)
    modes = y_synthesis(modes, tables[Y_IN], tables[PICKS])
    tail = jnp.where(lax.axis_index("gy") % 2 == 0, sums[...], late_sums[...])
    tail = jnp.broadcast_to(tail.reshape(1, 8, 128), (N, 8, 128))
    out[...] = jnp.concatenate([modes, tail], axis=1).astype(BF)


def weight_gradient(coef, dual, channel, out):
    for pair in range(PAIRS):
        unit, mode = divmod(pair, 3)
        dual_re = dual[unit, mode * 24 : mode * 24 + C, :]
        dual_im = dual[unit, (3 + mode) * 24 : (3 + mode) * 24 + C, :]
        re = line_of(coef, unit, mode, channel)
        im = line_of(coef, unit, 3 + mode, channel)
        start = channel * 2 * PAIRS * C + 2 * pair
        out[pl.ds(start, C, stride=2 * PAIRS), :] = re * dual_re + im * dual_im
        out[pl.ds(start + 1, C, stride=2 * PAIRS), :] = re * dual_im - im * dual_re


def same_cell(size):
    return ones_where(iota((size, 1), 0) % CY == iota((1, size), 1) % CY)


def spread_map(weight, weight_dim):
    spread = spread_matrix().astype(BF)
    tall = dot(spread, weight, 0, weight_dim).astype(BF)
    return (dot(tall, spread) * same_cell(C * CY)).astype(BF)


def flat_cells(values):
    return jnp.concatenate([values[x] for x in range(CX)], axis=1)


def pack_lines(cross, bias):
    picks = spread_matrix()
    exact = lax.Precision.HIGHEST
    point = dot(dot(picks, cross * same_cell(C * CY), 1, 0, exact), picks, 1, 1, exact)
    total = dot(bias, picks, 1, 1, exact)[:1]
    rows = jnp.concatenate([point, total], axis=0)
    rows = jnp.concatenate([rows, jnp.zeros((C + 1, 128 - C), F32)], axis=1)
    packed = []
    for r in range(4):
        line = jnp.zeros((1, 128), F32)
        for q in range(6):
            if r * 6 + q <= C:
                row = rows[r * 6 + q : r * 6 + q + 1]
                line = line + (pltpu.roll(row, q * C, 1) if q > 0 else row)
        packed.append(line)
    return jnp.concatenate(packed, axis=0)


def cells_kernel(
    lines, depth, field, cotangent, weight, bias, out, sums, slope_out, field_out
):
    matrix = depth_matrix(depth[...])
    mixing = spread_map(weight[...], 1)
    shift = dot(spread_matrix(), bias[...], 0, 1, lax.Precision.HIGHEST)
    fields = flat_cells(field)
    spectral = from_spectra(lines, matrix)
    pointwise = dot(mixing, fields) + shift
    for batch in range(BATCHES):
        columns = []
        for group in (2 * batch, 2 * batch + 1):
            span = rows_of(group, 16)
            pre = spectral[rows_of(group, 128)] + wide_to_columns(pointwise[span])
            phi = 0.5 * (1.0 + lax.erf(pre * 0.7071067811865476))
            field_out[:, span, :] = to_cells(pre * phi).astype(BF)
            slope = phi + pre * jnp.exp(-0.5 * pre * pre) * 0.3989422804014327
            slope = slope * to_columns(cotangent[:, span, :])
            columns.append(slope.astype(BF))
            slope_out[:, span, :] = to_cells(slope).astype(BF)
        put_spectra(matrix, columns, batch, out)
    put_sums(0, field, slope_out, sums)


def last_kernel(
    lines,
    depth,
    late_point,
    point,
    coef,
    dual,
    _,
    point_out,
    bias_out,
    field_out,
    weight_to,
    made,
    semaphore,
):
    start_weight_gradient(1 - FIRST, coef, dual, made, weight_to, semaphore)
    tails = jnp.sum(lines[:, ROWS:, :].astype(F32), axis=0)
    sums = (tails[:4] + tails[4:8]) * (NX * NY * ZT) ** -0.5
    for r in range(4):
        for q in range(6):
            index = r * 6 + q
            if index <= C:
                row = sums[r : r + 1]
                row = pltpu.roll(row, 128 - q * C, 1) if q > 0 else row
                if index < C:
                    point_out[index : index + 1, :] = row[:, :C]
                else:
                    bias_out[...] = row[:, :C]
    late = lax.axis_index("gy") % 2 == 0
    spectral = from_spectra(lines, depth_matrix(depth[...]))
    for group in range(GROUPS):
        span = rows_of(group, 16)
        pointwise = jnp.where(late, late_point[span], point[span])
        total = to_cells(spectral[rows_of(group, 128)]) + wide_to_cells(pointwise)
        field_out[:, span, :] = total.astype(BF)
    end_weight_gradient(1 - FIRST, made, weight_to, semaphore)


def exchange(values, axis):
    return lax.all_to_all(values, axis, split_axis=0, concat_axis=0, tiled=True)


def body(field_in, point_weight, point_bias, spec_weight, out_cotangent):
    cells = (CX, C * CY, ZT)
    line_message = shaped((N, ROWS, 128), BF)
    mode_message = shaped((N, 24, 128), BF)
    mode_lines = shaped((3, 144, KY), F32)
    wide_weights = pltpu.VMEM((WEIGHTS, KY), F32)
    field = field_in.transpose(0, 2, 1, 3).reshape(cells)
    cotangent = out_cotangent.transpose(0, 2, 1, 3).reshape(cells)
    weights = spec_weight.transpose(1, 2, 4, 3, 0).reshape(WEIGHTS, KY)

    message = call(spectrum_kernel, line_message, name="spectrum")(field)
    message = exchange(message, "gx")
    message = call(x_analysis_kernel, mode_message, name="x_analysis")(message, X_IN)
    message = exchange(message, "gy")
    message, coef, packed = call(
        product_kernel,
        (mode_message, mode_lines, shaped((WEIGHTS // FIVE, 128), F32)),
        [pltpu.VMEM((3, 48, 128), F32)],
        "product",
    )(message, weights, Y_ALL)
    message = exchange(message, "gy")
    message = call(x_synthesis_kernel, line_message, name="x_synthesis")(message, X_MID)
    message = exchange(message, "gx")
    message, sums, slope, output_field = call(
        cells_kernel,
        (line_message, shaped((8, 128), F32), shaped(cells, BF), shaped(cells, BF)),
        name="cells",
    )(message, DEPTH_MID, field, cotangent, point_weight, point_bias.reshape(1, C))
    message = exchange(message, "gx")
    point_shape = shaped((C * CY, CX * ZT), F32)
    message, late_sums, point = call(
        x_analysis_sums_kernel,
        (mode_message, shaped((8, 128), F32), point_shape),
        name="x_analysis_back",
    )(message, X_MID, field, slope, point_weight)
    message = exchange(message, "gy")
    message, dual = call(
        back_kernel,
        (shaped((N, 32, 128), BF), mode_lines),
        [pltpu.VMEM((3, 144, 128), F32), pltpu.VMEM((3, 144, KY), F32)],
        "back",
    )(message, packed, sums, late_sums, Y_ALL)
    message = exchange(message, "gy")
    made = [wide_weights, pltpu.SemaphoreType.DMA(())]
    weight_shape = shaped((WEIGHTS, KY), F32)
    message, late_point, weight_grad = call(
        x_synthesis_sums_kernel,
        (shaped((N, 256, 128), BF), point_shape, weight_shape),
        made,
        "x_synthesis_back",
        [pltpu.VMEM] * 6,
        [pltpu.VMEM] * 2 + [pl.ANY],
    )(message, X_IN, coef, dual, slope, point_weight)
    message = exchange(message, "gx")
    grad_point, grad_bias, grad_in, weight_grad = call(
        last_kernel,
        (shaped((C, C), F32), shaped((1, C), F32), shaped(cells, BF), weight_shape),
        made,
        "last",
        [pltpu.VMEM] * 6 + [pl.ANY],
        [pltpu.VMEM] * 3 + [pl.ANY],
        {6: 3},
    )(message, DEPTH_IN, late_point, point, coef, dual, weight_grad)
    grad_spec = weight_grad.reshape(C, C, PAIRS, 2, KY).transpose(4, 0, 1, 3, 2)

    def natural(values):
        return values.reshape(CX, C, CY, ZT).transpose(0, 2, 1, 3)

    return natural(output_field), natural(grad_in), grad_spec, grad_point, grad_bias.reshape(C)


def solution(mesh):
    return jax.shard_map(
        body,
        mesh=mesh,
        in_specs=(
            P("gx", "gy", None, None),
            P(),
            P(),
            P(None, None, None, None, ("gx", "gy")),
            P("gx", "gy", None, None),
        ),
        out_specs=(
            P("gx", "gy", None, None),
            P("gx", "gy", None, None),
            P(None, None, None, None, ("gx", "gy")),
            P(),
            P(),
        ),
        check_vma=False,
    )
```
